32 devices in a mesh: dp: 4 (over z), brick: 8 (over y, x, core).
Axes of the slice: x: 2, y: 2, z: 4, core: 2. Of those that a mesh axis runs over, the one named last changes fastest.
Arguments:
- records: bfloat16 [32, 8, 16, 6144], P(('dp', 'brick')), may hold values from -6 to 6
- positions: int32 [32, 8, 16], P(('dp', 'brick')), may hold values from -1 to 127, as said below
- weight: bfloat16 [2592, 192], P('dp'), may hold values from -0.125 to 0.125
- cotangent: bfloat16 [4, 32, 16, 3072], P('dp', 'brick'), may hold values from -0.0234375 to 0.0234375
Outputs:
- activation: bfloat16 [4, 32, 16, 3072], P('dp', 'brick')
- weight_grad: float32 [2592, 192], P('dp')
The draws below stay inside these ranges and needn't reach their ends.
Inputs may be any that keep to these rules, and one draw needn't show every extreme that they name: Entry [d * 8 + s, o, r] is the brick position in owner o's slab of scene d of the r-th record that source s sends to o, or -1 for an empty slot. The live positions at one owner of one scene are distinct; in every scene some owner has all 128 of its slots filled.
All inputs are finite; a program needn't handle non-finite values.
Results may differ from the reference program's by a relative error of at most 0.0029.
Values may be sent and summed in bfloat16 or wider, within the bound.
A program may use at most 64 MiB of HBM per device.

```python
from functools import partial
import jax
import jax.numpy as jnp
from jax import lax

C_IN = 96
C_OUT = 192
BS = 4
BX = 2
BY = 8
BZ = 8
NPOS = 128
CAP = 16
RX = 8
RY = 32
RZ = 32
OX = 4
OY = 16
OZ = 16
NOUT = 1024
KROWS = 2592
REC = 6144
NXO = 32
N_DP = 4
N_BRICK = 8


def draw_positions(key, part):
    slots = N_BRICK * CAP

    def one_owner(owner_key, busiest):
        level_key, slot_key, place_key = jax.random.split(owner_key, 3)
        level = jnp.where(busiest, 3, jax.random.randint(level_key, (), 0, 4))
        occupied = slots * jnp.array([1, 2, 4, 8], jnp.int32)[level] // 8
        slot_order = jax.random.permutation(slot_key, slots)
        place_order = jax.random.permutation(place_key, NPOS)
        return jnp.where(slot_order < occupied, place_order[slot_order], -1).astype(jnp.int32)

    def one_scene(scene_key):
        full_key, owners_key = jax.random.split(scene_key, 2)
        chosen = jax.random.randint(full_key, (), 0, N_BRICK)
        owner_keys = jax.random.split(owners_key, N_BRICK)
        return jax.vmap(one_owner)(owner_keys, jnp.arange(N_BRICK) == chosen)
    scene_keys = jax.random.split(jax.random.fold_in(key, 7), N_DP)
    table = jax.vmap(one_scene)(scene_keys)
    table = table.reshape(N_DP, N_BRICK, N_BRICK, CAP).transpose(0, 2, 1, 3)
    return table.reshape(N_DP * N_BRICK, N_BRICK, CAP)


def level_of(own_key, extent, shards, least, high):
    factor_of = 1.0
    for dim, shards_of in shards:
        draws = jax.random.uniform(jax.random.fold_in(jax.random.fold_in(own_key, 6), dim), (shards_of,), jnp.float32, least / len(shards), high / len(shards))
        factor_of = factor_of * jnp.repeat(jnp.exp(draws), extent[dim] // shards_of).reshape((-1,) + (1,) * (len(extent) - 1 - dim))
    return factor_of


def noise(stream_key, dims, spread, limit, cuts=(), kind=jnp.bfloat16):
    entries = spread * jax.random.normal(stream_key, dims, jnp.float32)
    if cuts:
        entries = entries * level_of(stream_key, dims, cuts, -0.22, 0.18)
    return jnp.clip(entries, -limit, limit).astype(kind)


def setup_inputs(seed: int = 0) -> dict:
    key_of = jax.random.split(jax.random.key(seed), 5)
    return {
        "records": noise(key_of[0], (N_DP * N_BRICK, N_BRICK, CAP, REC), 1.0, 6.0, ((0, 32),)),
        "positions": draw_positions(jax.random.fold_in(key_of[4], 71), 0),
        "weight": noise(key_of[2], (KROWS, C_OUT), KROWS ** -0.5, 0.125, ((0, 4),)),
        "cotangent": noise(key_of[3], (N_DP, NXO, OY, OZ * C_OUT), 0.004, 0.0234375, ((0, 4), (1, 8))),
    }


def place_records(arrived, places, brick_x, brick_y, brick_z, side, channels):
    count = brick_x * brick_y * brick_z
    target = jnp.where(places >= 0, places, count).astype(jnp.int32)
    filled = jnp.zeros((count + 1, arrived.shape[1]), arrived.dtype).at[target].set(arrived)[:count]
    cubes = filled.reshape(brick_x, brick_y, brick_z, side, side, side, channels)
    cubes = cubes.transpose(0, 3, 1, 4, 2, 5, 6)
    return cubes.reshape(brick_x * side, brick_y * side, brick_z * side, channels)


def columns_of(voxels, boundary):
    padded = jnp.concatenate([boundary, voxels], axis=0)
    padded = jnp.pad(padded, ((0, 0), (1, 0), (1, 0), (0, 0)))
    out_x = voxels.shape[0] // 2
    out_y = voxels.shape[1] // 2
    out_z = voxels.shape[2] // 2
    channels = voxels.shape[3]
    tap_list = []
    for offset_x in range(3):
        for offset_y in range(3):
            for offset_z in range(3):
                tap_list.append(lax.slice(padded, (offset_x, offset_y, offset_z, 0),
                                          (offset_x + 2 * out_x - 1, offset_y + 2 * out_y - 1, offset_z + 2 * out_z - 1, channels),
                                          (2, 2, 2, 1)))
    stacked = jnp.concatenate(tap_list, axis=3)
    return stacked.reshape(out_x * out_y * out_z, 27 * channels)


def layer_terms(columns, weight, upstream):
    linear = jnp.dot(columns, weight, preferred_element_type=jnp.float32)
    activation = jax.nn.silu(linear).astype(jnp.bfloat16)
    sigma = jax.nn.sigmoid(linear)
    slope = sigma * (1.0 + linear * (1.0 - sigma))
    slope_grad = (upstream.astype(jnp.float32) * slope).astype(jnp.bfloat16)
    partial_grad = jnp.dot(columns.T, slope_grad, preferred_element_type=jnp.float32)
    return activation, partial_grad


def reference(records, positions, weight, cotangent):
    width = records.shape[-1]
    slots = N_BRICK * CAP
    scene_records = records.reshape(N_DP, N_BRICK, N_BRICK, CAP, width).transpose(0, 2, 1, 3, 4).reshape(N_DP, N_BRICK, slots, width)
    scene_places = positions.reshape(N_DP, N_BRICK, N_BRICK, CAP).transpose(0, 2, 1, 3).reshape(N_DP, N_BRICK, slots)
    scene_upstream = cotangent.reshape(N_DP, N_BRICK, NOUT, C_OUT)
    placer = partial(place_records, brick_x=BX, brick_y=BY, brick_z=BZ, side=BS, channels=C_IN)

    def one_scene(inputs):
        owner_records, owner_places, owner_upstream = inputs
        grids = jax.vmap(placer)(owner_records, owner_places)
        rims = jnp.concatenate([jnp.zeros((1, 1, RY, RZ, C_IN), grids.dtype), grids[:-1, RX - 1:]], axis=0)

        def one_owner(block):
            voxels, boundary, upstream = block
            return layer_terms(columns_of(voxels, boundary), weight, upstream)

        outputs, grads = lax.map(one_owner, (grids, rims, owner_upstream))
        return outputs, jnp.sum(grads, axis=0)

    outputs, grads = lax.map(one_scene, (scene_records, scene_places, scene_upstream))
    activation = outputs.reshape(N_DP, N_BRICK * OX, OY, OZ * C_OUT)
    return activation, jnp.sum(grads, axis=0)
```

```python
import functools

import jax
import jax.numpy as jnp
from jax import lax
from jax.experimental import pallas as pl
from jax.experimental.pallas import tpu as pltpu
from jax.sharding import PartitionSpec as P

C_IN = 96
C_OUT = 192
BS = 4
BX = 2
BY = 8
BZ = 8
TAPS = 27
PLANE = BS * BS * C_IN
ROW = BS * C_IN
KB = 512
NB = 256
MESH = pl.DeviceIdType.MESH
VMEM_LIMIT = 48 * 1024 * 1024


def up(n, k):
    return -(-n // k) * k


def copy_to(src, dst, send, recv, axis, peer):
    return pltpu.make_async_remote_copy(
        src_ref=src, dst_ref=dst, send_sem=send, recv_sem=recv,
        device_id={axis: peer}, device_id_type=MESH,
    )


def exchange_kernel(nb, nd, half, rec, pos, wt, rec_out, pos_out, wt_out,
                    rs, rr, ps, pr, ws, wr, xs, xr, loc):
    me = lax.axis_index("brick")
    dp = lax.axis_index("dp")
    core = lax.rem(me, 2)
    sib = me + 1 - 2 * core
    barrier = pltpu.get_barrier_semaphore()
    for k in range(1, nb):
        pl.semaphore_signal(barrier, inc=1, device_id={"brick": lax.rem(me + k, nb)}, device_id_type=MESH)
    for k in range(1, nd):
        pl.semaphore_signal(barrier, inc=1, device_id={"dp": lax.rem(dp + k, nd)}, device_id_type=MESH)
    own = [
        pltpu.make_async_copy(rec.at[me], rec_out.at[me], loc.at[0]),
        pltpu.make_async_copy(pos.at[me], pos_out.at[me], loc.at[1]),
        pltpu.make_async_copy(wt, wt_out.at[dp], loc.at[2]),
    ]
    for c in own:
        c.start()
    pl.semaphore_wait(barrier, nb + nd - 2)
    mine = pl.ds(pl.multiple_of(core * half, 16), half)
    sent = []
    for k in range(1, nd):
        o = lax.rem(dp + k, nd)
        c = copy_to(wt.at[mine], wt_out.at[dp, mine], ws.at[k], wr.at[k], "dp", o)
        c.start()
        sent.append(c)
    for k in range(1, nb):
        o = lax.rem(me + k, nb)
        c = copy_to(pos.at[o], pos_out.at[me], ps.at[k], pr.at[k], "brick", o)
        c.start()
        sent.append(c)
        c = copy_to(rec.at[o], rec_out.at[me], rs.at[k], rr.at[k], "brick", o)
        c.start()
        sent.append(c)
    theirs = pl.ds(pl.multiple_of((1 - core) * half, 16), half)
    for k in range(1, nd):
        s = lax.rem(dp + nd - k, nd)
        copy_to(wt.at[mine], wt_out.at[s, mine], ws.at[k], wr.at[k], "dp", s).wait_recv()
        c = copy_to(wt_out.at[s, mine], wt_out.at[s, mine], xs.at[k], xr.at[k], "brick", sib)
        c.start()
        sent.append(c)
    for k in range(1, nd):
        s = lax.rem(dp + nd - k, nd)
        copy_to(wt.at[theirs], wt_out.at[s, theirs], xs.at[k], xr.at[k], "brick", sib).wait_recv()
    for k in range(1, nb):
        s = lax.rem(me + nb - k, nb)
        copy_to(pos.at[s], pos_out.at[s], ps.at[k], pr.at[k], "brick", s).wait_recv()
        copy_to(rec.at[s], rec_out.at[s], rs.at[k], rr.at[k], "brick", s).wait_recv()
    for c in sent:
        c.wait_send()
    for c in own:
        c.wait()


def exchange(rec, pos, wt, nb, nd):
    half = wt.shape[0] // 2
    dma = pltpu.SemaphoreType.DMA
    return pl.pallas_call(
        functools.partial(exchange_kernel, nb, nd, half),
        out_shape=(
            jax.ShapeDtypeStruct(rec.shape, rec.dtype),
            jax.ShapeDtypeStruct(pos.shape, pos.dtype),
            jax.ShapeDtypeStruct((nd,) + wt.shape, wt.dtype),
        ),
        in_specs=[pl.BlockSpec(memory_space=pl.ANY)] * 3,
        out_specs=(pl.BlockSpec(memory_space=pl.ANY),) * 3,
        scratch_shapes=[dma((nb,)), dma((nb,)), dma((nb,)), dma((nb,)),
                        dma((nd,)), dma((nd,)), dma((nd,)), dma((nd,)), dma((3,))],
        compiler_params=pltpu.CompilerParams(collective_id=0, has_side_effects=True),
        name="exchange",
    )(rec, pos, wt)


def place_kernel(arrived, places, filled, rim):
    n = filled.shape[0]
    slots = arrived.shape[0]
    want = lax.broadcasted_iota(jnp.int32, (n, slots), 0)
    pick = jnp.where(places[...] == want, 1.0, 0.0).astype(jnp.bfloat16)
    for x in range(BS):
        lanes = slice(x * PLANE, (x + 1) * PLANE)
        part = jnp.dot(pick, arrived[:, lanes], preferred_element_type=jnp.float32).astype(jnp.bfloat16)
        filled[:, lanes] = part
        if x == BS - 1:
            rim[...] = part[n - n // BX:]


def place(arrived, places):
    n = BX * BY * BZ
    return pl.pallas_call(
        place_kernel,
        out_shape=(
            jax.ShapeDtypeStruct((n, arrived.shape[1]), arrived.dtype),
            jax.ShapeDtypeStruct((n // BX, PLANE), arrived.dtype),
        ),
        compiler_params=pltpu.CompilerParams(vmem_limit_bytes=VMEM_LIMIT),
        name="place",
    )(arrived, places)


def shift_matrix(n, dy, dz):
    r = lax.broadcasted_iota(jnp.int32, (n, n), 0)
    c = lax.broadcasted_iota(jnp.int32, (n, n), 1)
    hit = c == r - dy * BZ - dz
    if dy:
        hit = hit & (lax.rem(r // BZ, BY) > 0)
    if dz:
        hit = hit & (lax.rem(r, BZ) > 0)
    return jnp.where(hit, 1.0, 0.0).astype(jnp.bfloat16)


def row_parts(first, count, shard):
    done = 0
    while done < count:
        d, r = divmod(first + done, shard)
        take = min(count - done, shard - r)
        yield d, r, take, done
        done += take


def layer_kernel(nd, shard, cut, piece, filled, rim, wt, cot, act, terms, cols, band, slopes):
    n = filled.shape[0]
    rows = 4 * n
    f32, bf16 = jnp.float32, jnp.bfloat16
    band[...] = jnp.zeros_like(band)
    slopes[...] = jnp.zeros_like(slopes)
    terms[...] = jnp.zeros_like(terms)
    spots = {0: ((KB - C_IN, 0), (C_IN, NB)), 1: ((0, 0), (2 * C_IN, NB)), 2: ((C_IN, 0), (3 * C_IN, NB))}
    for t in range(TAPS):
        ab, e = divmod(t, 3)
        for d, r, take, off in row_parts(t * C_IN, C_IN, shard):
            w = wt[d, r:r + take, :]
            for row, col in spots[e]:
                at = ab * KB + row + off
                band[at:at + take, col:col + C_OUT] = w
    sy = shift_matrix(n, 1, 0)
    sz = shift_matrix(n, 0, 1)
    syz = shift_matrix(n, 1, 1)

    def move(s, v):
        return jnp.dot(s, v, preferred_element_type=f32).astype(bf16)

    for x in range(-1, BS):
        if x < 0:
            last = slice((BS - 1) * PLANE, BS * PLANE)
            plane = jnp.concatenate([rim[...], filled[:n - n // BX, last]], axis=0)
        else:
            plane = filled[:, x * PLANE:(x + 1) * PLANE]
        places_x = [(ox, x + 1 - 2 * ox) for ox in range(2) if 0 <= x + 1 - 2 * ox <= 2]
        for y in range(-1, BS):
            at = (y if y >= 0 else BS - 1) * ROW
            whole = plane[:, at:at + ROW]
            tail = plane[:, at + ROW - 128:at + ROW]
            if y < 0:
                whole, tail = move(sy, whole), move(syz, tail)
            else:
                tail = move(sz, tail)
            places_y = [(oy, y + 1 - 2 * oy) for oy in range(2) if 0 <= y + 1 - 2 * oy <= 2]
            for ox, a in places_x:
                for oy, b in places_y:
                    q = slice((ox * 2 + oy) * n, (ox * 2 + oy + 1) * n)
                    k = (a * 3 + b) * KB
                    cols[q, k:k + ROW] = whole
                    cols[q, k + ROW:k + KB] = tail
    for oz in range(2):
        v = jnp.dot(cols[...], band[:, oz * NB:(oz + 1) * NB], preferred_element_type=f32)[:, :C_OUT]
        s = 1.0 / (1.0 + jnp.exp(-v))
        act[oz] = (v * s).astype(bf16)
        slope = s * (1.0 + v * (1.0 - s))
        slopes[:, oz * NB:oz * NB + C_OUT] = (cot[oz].astype(f32) * slope).astype(bf16)
    for ab in range(9):
        g = lax.dot_general(cols[:, ab * KB:(ab + 1) * KB], slopes[...], (((0,), (0,)), ((), ())),
                            preferred_element_type=f32)
        for e in range(3):
            (r0, c0), (r1, c1) = spots[e]
            tap = g[r0:r0 + C_IN, c0:c0 + C_OUT] + g[r1:r1 + C_IN, c1:c1 + C_OUT]
            for d, r, take, off in row_parts((ab * 3 + e) * C_IN, C_IN, shard):
                left = max(0, min(take, cut - r))
                for start, length, base, lane in ((off, left, r, 0), (off + left, take - left, r + left - cut, C_OUT)):
                    if length:
                        for j, rr, tk, o2 in row_parts(base, length, piece):
                            terms[j, d, rr:rr + tk, lane:lane + C_OUT] = tap[start + o2:start + o2 + tk]


def layer(filled, rim, wt, cot, nb, nd, shard, cut, piece):
    rows = cot.shape[1]
    return pl.pallas_call(
        functools.partial(layer_kernel, nd, shard, cut, piece),
        out_shape=(
            jax.ShapeDtypeStruct(cot.shape, jnp.bfloat16),
            jax.ShapeDtypeStruct((nb, nd, piece, 2 * C_OUT), jnp.float32),
        ),
        scratch_shapes=[
            pltpu.VMEM((rows, 9 * KB), jnp.bfloat16),
            pltpu.VMEM((9 * KB, 2 * NB), jnp.bfloat16),
            pltpu.VMEM((rows, 2 * NB), jnp.bfloat16),
        ],
        compiler_params=pltpu.CompilerParams(vmem_limit_bytes=VMEM_LIMIT),
        name="layer",
    )(filled, rim, wt, cot)


def sum_kernel(nb, nd, shard, cut, piece, terms, out, give, got, pass_on, plane_in, down, down_in, final,
               s1, r1, s2, r2, s3, r3, s4, r4):
    f32, bf16 = jnp.float32, jnp.bfloat16
    nc = nb // 2
    me = lax.axis_index("brick")
    dp = lax.axis_index("dp")
    core = lax.rem(me, 2)
    chip = me // 2
    sib = me + 1 - 2 * core
    barrier = pltpu.get_barrier_semaphore()
    for k in range(1, nb):
        pl.semaphore_signal(barrier, inc=1, device_id={"brick": lax.rem(me + k, nb)}, device_id_type=MESH)
    for k in range(1, nd):
        pl.semaphore_signal(barrier, inc=1, device_id={"dp": lax.rem(dp + k, nd)}, device_id_type=MESH)
    pl.semaphore_wait(barrier, nb + nd - 2)
    sent = []
    for k in range(1, nc + 1):
        q = lax.rem(chip + k, nc)
        give[q] = terms[(1 - core) * nc + q].astype(bf16)
        c = copy_to(give.at[q], got.at[q], s1.at[k], r1.at[k], "brick", sib)
        c.start()
        sent.append(c)
    for k in range(1, nc):
        q = lax.rem(chip + k, nc)
        copy_to(give.at[q], got.at[q], s1.at[k], r1.at[k], "brick", sib).wait_recv()
        pass_on[k] = (terms[core * nc + q] + got[q].astype(f32)).astype(bf16)
        c = copy_to(pass_on.at[k], plane_in.at[k], s2.at[k], r2.at[k], "brick", q * 2 + core)
        c.start()
        sent.append(c)
    copy_to(give.at[chip], got.at[chip], s1.at[nc], r1.at[nc], "brick", sib).wait_recv()
    for k in range(1, nc):
        q = lax.rem(chip + nc - k, nc)
        copy_to(pass_on.at[k], plane_in.at[k], s2.at[k], r2.at[k], "brick", q * 2 + core).wait_recv()

    def plane_sum(d):
        total = terms[core * nc + chip, d] + got[chip, d].astype(f32)
        for k in range(1, nc):
            total = total + plane_in[k, d].astype(f32)
        return total

    for k in range(1, nd):
        o = lax.rem(dp + k, nd)
        down[k] = plane_sum(o).astype(bf16)
        c = copy_to(down.at[k], down_in.at[k], s3.at[k], r3.at[k], "dp", o)
        c.start()
        sent.append(c)
    total = plane_sum(dp)
    for k in range(1, nd):
        s = lax.rem(dp + nd - k, nd)
        copy_to(down.at[k], down_in.at[k], s3.at[k], r3.at[k], "dp", s).wait_recv()
        total = total + down_in[k].astype(f32)
    final[core * nc + chip] = total.astype(bf16)
    for k in range(1, nb):
        o = lax.rem(me + k, nb)
        slot = final.at[core * nc + chip]
        c = copy_to(slot, slot, s4.at[k], r4.at[k], "brick", o)
        c.start()
        sent.append(c)
    for k in range(1, nb):
        s = lax.rem(me + nb - k, nb)
        slot = final.at[lax.rem(s, 2) * nc + s // 2]
        copy_to(slot, slot, s4.at[k], r4.at[k], "brick", s).wait_recv()
    for j in range(nb):
        for rows, first, lane in ((cut, 0, 0), (shard - cut, cut, C_OUT)):
            take = min(piece, rows - j * piece)
            if take > 0:
                out[first + j * piece:first + j * piece + take, :] = (
                    final[j, :, lane:lane + C_OUT].astype(f32)[:take])
    for c in sent:
        c.wait_send()


def sum_terms(terms, nb, nd, shard, cut, piece):
    bf16 = jnp.bfloat16
    dma = pltpu.SemaphoreType.DMA
    nc = nb // 2
    wide = 2 * C_OUT
    return pl.pallas_call(
        functools.partial(sum_kernel, nb, nd, shard, cut, piece),
        out_shape=jax.ShapeDtypeStruct((shard, C_OUT), jnp.float32),
        scratch_shapes=[
            pltpu.VMEM((nc, nd, piece, wide), bf16),
            pltpu.VMEM((nc, nd, piece, wide), bf16),
            pltpu.VMEM((nc, nd, piece, wide), bf16),
            pltpu.VMEM((nc, nd, piece, wide), bf16),
            pltpu.VMEM((nd, piece, wide), bf16),
            pltpu.VMEM((nd, piece, wide), bf16),
            pltpu.VMEM((nb, piece, wide), bf16),
            dma((nc + 1,)), dma((nc + 1,)), dma((nc,)), dma((nc,)),
            dma((nd,)), dma((nd,)), dma((nb,)), dma((nb,)),
        ],
        compiler_params=pltpu.CompilerParams(
            collective_id=1, has_side_effects=True, vmem_limit_bytes=VMEM_LIMIT),
        name="sum_terms",
    )(terms)


def body(nb, nd, records, positions, weight, cotangent):
    cap = records.shape[2]
    shard = weight.shape[0]
    cut = up(-(-shard // 2), 8)
    piece = up(-(-cut // nb), 16)
    half = up(-(-shard // 2), 16)
    pos = jnp.pad(positions.reshape(nb, 1, cap), ((0, 0), (0, 7), (0, 128 - cap)))
    wt = jnp.pad(weight, ((0, 2 * half - shard), (0, 0)))
    arrived, places, full = exchange(records.reshape(records.shape[1:]), pos, wt, nb, nd)
    slots = nb * cap
    filled, edge = place(arrived.reshape(slots, -1), places[:, 0, :cap].reshape(1, slots))
    rim = lax.ppermute(edge, "brick", [(i, i + 1) for i in range(nb - 1)])
    shape7 = (BX, 2, BY, 2, BZ, 2, C_OUT)
    cot = cotangent.reshape(shape7).transpose(5, 1, 3, 0, 2, 4, 6).reshape(2, -1, C_OUT)
    act, terms = layer(filled, rim, full, cot, nb, nd, shard, cut, piece)
    act = act.reshape(2, 2, 2, BX, BY, BZ, C_OUT).transpose(3, 1, 4, 2, 5, 0, 6)
    return act.reshape(cotangent.shape), sum_terms(terms, nb, nd, shard, cut, piece)


def solution(mesh):
    placed = (
        P(("dp", "brick"), None, None, None),
        P(("dp", "brick"), None, None),
        P("dp", None),
        P("dp", "brick", None, None),
    )
    return jax.shard_map(
        functools.partial(body, mesh.shape["brick"], mesh.shape["dp"]),
        mesh=mesh,
        in_specs=placed,
        out_specs=(P("dp", "brick", None, None), P("dp", None)),
        check_vma=False,
    )
```

```python
import functools

import jax
import jax.numpy as jnp
from jax import lax
from jax.experimental import pallas as pl
from jax.experimental.pallas import tpu as pltpu
from jax.sharding import PartitionSpec as P

C_IN = 96
C_OUT = 192
BS = 4
BX = 2
BY = 8
BZ = 8
TAPS = 27
PLANE = BS * BS * C_IN
ROW = BS * C_IN
KB = 512
NB = 256
MESH = pl.DeviceIdType.MESH
VMEM_LIMIT = 48 * 1024 * 1024


def up(n, k):
    return -(-n // k) * k


def copy_to(src, dst, send, recv, axis, peer):
    return pltpu.make_async_remote_copy(
        src_ref=src, dst_ref=dst, send_sem=send, recv_sem=recv,
        device_id={axis: peer}, device_id_type=MESH,
    )


def exchange_kernel(nb, nd, half, rec, pos, wt, rec_out, pos_out, wt_out,
                    rs, rr, ps, pr, ws, wr, xs, xr, loc):
    me = lax.axis_index("brick")
    dp = lax.axis_index("dp")
    core = lax.rem(me, 2)
    sib = me + 1 - 2 * core
    barrier = pltpu.get_barrier_semaphore()
    for k in range(1, nb):
        pl.semaphore_signal(barrier, inc=1, device_id={"brick": lax.rem(me + k, nb)}, device_id_type=MESH)
    for k in range(1, nd):
        pl.semaphore_signal(barrier, inc=1, device_id={"dp": lax.rem(dp + k, nd)}, device_id_type=MESH)
    own = [
        pltpu.make_async_copy(rec.at[me], rec_out.at[me], loc.at[0]),
        pltpu.make_async_copy(pos.at[me], pos_out.at[me], loc.at[1]),
        pltpu.make_async_copy(wt, wt_out.at[dp], loc.at[2]),
    ]
    for c in own:
        c.start()
    pl.semaphore_wait(barrier, nb + nd - 2)
    mine = pl.ds(pl.multiple_of(core * half, 16), half)
    sent = []
    for k in range(1, nd):
        o = lax.rem(dp + k, nd)
        c = copy_to(wt.at[mine], wt_out.at[dp, mine], ws.at[k], wr.at[k], "dp", o)
        c.start()
        sent.append(c)
    for k in range(1, nb):
        o = lax.rem(me + k, nb)
        c = copy_to(pos.at[o], pos_out.at[me], ps.at[k], pr.at[k], "brick", o)
        c.start()
        sent.append(c)
        c = copy_to(rec.at[o], rec_out.at[me], rs.at[k], rr.at[k], "brick", o)
        c.start()
        sent.append(c)
    theirs = pl.ds(pl.multiple_of((1 - core) * half, 16), half)
    for k in range(1, nd):
        s = lax.rem(dp + nd - k, nd)
        copy_to(wt.at[mine], wt_out.at[s, mine], ws.at[k], wr.at[k], "dp", s).wait_recv()
        c = copy_to(wt_out.at[s, mine], wt_out.at[s, mine], xs.at[k], xr.at[k], "brick", sib)
        c.start()
        sent.append(c)
    for k in range(1, nd):
        s = lax.rem(dp + nd - k, nd)
        copy_to(wt.at[theirs], wt_out.at[s, theirs], xs.at[k], xr.at[k], "brick", sib).wait_recv()
    for k in range(1, nb):
        s = lax.rem(me + nb - k, nb)
        copy_to(pos.at[s], pos_out.at[s], ps.at[k], pr.at[k], "brick", s).wait_recv()
        copy_to(rec.at[s], rec_out.at[s], rs.at[k], rr.at[k], "brick", s).wait_recv()
    for c in sent:
        c.wait_send()
    for c in own:
        c.wait()


def exchange(rec, pos, wt, nb, nd):
    half = wt.shape[0] // 2
    dma = pltpu.SemaphoreType.DMA
    return pl.pallas_call(
        functools.partial(exchange_kernel, nb, nd, half),
        out_shape=(
            jax.ShapeDtypeStruct(rec.shape, rec.dtype),
            jax.ShapeDtypeStruct(pos.shape, pos.dtype),
            jax.ShapeDtypeStruct((nd,) + wt.shape, wt.dtype),
        ),
        in_specs=[pl.BlockSpec(memory_space=pl.ANY)] * 3,
        out_specs=(pl.BlockSpec(memory_space=pl.ANY),) * 3,
        scratch_shapes=[dma((nb,)), dma((nb,)), dma((nb,)), dma((nb,)),
                        dma((nd,)), dma((nd,)), dma((nd,)), dma((nd,)), dma((3,))],
        compiler_params=pltpu.CompilerParams(collective_id=0, has_side_effects=True),
        name="exchange",
    )(rec, pos, wt)


def place_kernel(arrived, places, filled, rim):
    n = filled.shape[0]
    slots = arrived.shape[0]
    want = lax.broadcasted_iota(jnp.int32, (n, slots), 0)
    pick = jnp.where(places[...] == want, 1.0, 0.0).astype(jnp.bfloat16)
    for x in range(BS):
        lanes = slice(x * PLANE, (x + 1) * PLANE)
        part = jnp.dot(pick, arrived[:, lanes], preferred_element_type=jnp.float32).astype(jnp.bfloat16)
        filled[:, lanes] = part
        if x == BS - 1:
            rim[...] = part[n - n // BX:]


def place(arrived, places):
    n = BX * BY * BZ
    return pl.pallas_call(
        place_kernel,
        out_shape=(
            jax.ShapeDtypeStruct((n, arrived.shape[1]), arrived.dtype),
            jax.ShapeDtypeStruct((n // BX, PLANE), arrived.dtype),
        ),
        compiler_params=pltpu.CompilerParams(vmem_limit_bytes=VMEM_LIMIT),
        name="place",
    )(arrived, places)


def shift_matrix(n, dy, dz):
    r = lax.broadcasted_iota(jnp.int32, (n, n), 0)
    c = lax.broadcasted_iota(jnp.int32, (n, n), 1)
    hit = c == r - dy * BZ - dz
    if dy:
        hit = hit & (lax.rem(r // BZ, BY) > 0)
    if dz:
        hit = hit & (lax.rem(r, BZ) > 0)
    return jnp.where(hit, 1.0, 0.0).astype(jnp.bfloat16)


def row_parts(first, count, shard):
    done = 0
    while done < count:
        d, r = divmod(first + done, shard)
        take = min(count - done, shard - r)
        yield d, r, take, done
        done += take


def layer_kernel(nd, shard, cut, piece, filled, rim, wt, cot, act, terms, cols, band, slopes):
    n = filled.shape[0]
    rows = 4 * n
    f32, bf16 = jnp.float32, jnp.bfloat16
    band[...] = jnp.zeros_like(band)
    slopes[...] = jnp.zeros_like(slopes)
    terms[...] = jnp.zeros_like(terms)
    spots = {0: ((KB - C_IN, 0), (C_IN, NB)), 1: ((0, 0), (2 * C_IN, NB)), 2: ((C_IN, 0), (3 * C_IN, NB))}
    for t in range(TAPS):
        ab, e = divmod(t, 3)
        for d, r, take, off in row_parts(t * C_IN, C_IN, shard):
            w = wt[d, r:r + take, :]
            for row, col in spots[e]:
                at = ab * KB + row + off
                band[at:at + take, col:col + C_OUT] = w
    sy = shift_matrix(n, 1, 0)
    sz = shift_matrix(n, 0, 1)
    syz = shift_matrix(n, 1, 1)

    def move(s, v):
        return jnp.dot(s, v, preferred_element_type=f32).astype(bf16)

    for x in range(-1, BS):
        if x < 0:
            last = slice((BS - 1) * PLANE, BS * PLANE)
            plane = jnp.concatenate([rim[...], filled[:n - n // BX, last]], axis=0)
        else:
            plane = filled[:, x * PLANE:(x + 1) * PLANE]
        places_x = [(ox, x + 1 - 2 * ox) for ox in range(2) if 0 <= x + 1 - 2 * ox <= 2]
        for y in range(-1, BS):
            at = (y if y >= 0 else BS - 1) * ROW
            whole = plane[:, at:at + ROW]
            tail = plane[:, at + ROW - 128:at + ROW]
            if y < 0:
                whole, tail = move(sy, whole), move(syz, tail)
            else:
                tail = move(sz, tail)
            places_y = [(oy, y + 1 - 2 * oy) for oy in range(2) if 0 <= y + 1 - 2 * oy <= 2]
            for ox, a in places_x:
                for oy, b in places_y:
                    q = slice((ox * 2 + oy) * n, (ox * 2 + oy + 1) * n)
                    k = (a * 3 + b) * KB
                    cols[q, k:k + ROW] = whole
                    cols[q, k + ROW:k + KB] = tail
    for oz in range(2):
        v = jnp.dot(cols[...], band[:, oz * NB:(oz + 1) * NB], preferred_element_type=f32)[:, :C_OUT]
        s = 1.0 / (1.0 + jnp.exp(-v))
        act[oz] = (v * s).astype(bf16)
        slope = s * (1.0 + v * (1.0 - s))
        slopes[:, oz * NB:oz * NB + C_OUT] = (cot[oz].astype(f32) * slope).astype(bf16)
    for ab in range(9):
        g = lax.dot_general(cols[:, ab * KB:(ab + 1) * KB], slopes[...], (((0,), (0,)), ((), ())),
                            preferred_element_type=f32)
        for e in range(3):
            (r0, c0), (r1, c1) = spots[e]
            tap = g[r0:r0 + C_IN, c0:c0 + C_OUT] + g[r1:r1 + C_IN, c1:c1 + C_OUT]
            for d, r, take, off in row_parts((ab * 3 + e) * C_IN, C_IN, shard):
                left = max(0, min(take, cut - r))
                for start, length, base, lane in ((off, left, r, 0), (off + left, take - left, r + left - cut, C_OUT)):
                    if length:
                        for j, rr, tk, o2 in row_parts(base, length, piece):
                            terms[j, d, rr:rr + tk, lane:lane + C_OUT] = tap[start + o2:start + o2 + tk]


def layer(filled, rim, wt, cot, nb, nd, shard, cut, piece):
    rows = cot.shape[1]
    return pl.pallas_call(
        functools.partial(layer_kernel, nd, shard, cut, piece),
        out_shape=(
            jax.ShapeDtypeStruct(cot.shape, jnp.bfloat16),
            jax.ShapeDtypeStruct((nb, nd, piece, 2 * C_OUT), jnp.float32),
        ),
        scratch_shapes=[
            pltpu.VMEM((rows, 9 * KB), jnp.bfloat16),
            pltpu.VMEM((9 * KB, 2 * NB), jnp.bfloat16),
            pltpu.VMEM((rows, 2 * NB), jnp.bfloat16),
        ],
        compiler_params=pltpu.CompilerParams(vmem_limit_bytes=VMEM_LIMIT),
        name="layer",
    )(filled, rim, wt, cot)


def sum_kernel(nb, nd, shard, cut, piece, terms, out, got, pass_on, plane_in, down, down_in, final,
               s1, r1, s2, r2, s3, r3, s4, r4):
    f32, bf16 = jnp.float32, jnp.bfloat16
    nc = nb // 2
    me = lax.axis_index("brick")
    dp = lax.axis_index("dp")
    core = lax.rem(me, 2)
    chip = me // 2
    sib = me + 1 - 2 * core
    barrier = pltpu.get_barrier_semaphore()
    for k in range(1, nb):
        pl.semaphore_signal(barrier, inc=1, device_id={"brick": lax.rem(me + k, nb)}, device_id_type=MESH)
    for k in range(1, nd):
        pl.semaphore_signal(barrier, inc=1, device_id={"dp": lax.rem(dp + k, nd)}, device_id_type=MESH)
    pl.semaphore_wait(barrier, nb + nd - 2)
    sent = []
    for k in range(1, nc + 1):
        q = lax.rem(chip + k, nc)
        c = copy_to(terms.at[(1 - core) * nc + q], got.at[q], s1.at[k], r1.at[k], "brick", sib)
        c.start()
        sent.append(c)
    for k in range(1, nc):
        q = lax.rem(chip + k, nc)
        copy_to(terms.at[q], got.at[q], s1.at[k], r1.at[k], "brick", sib).wait_recv()
        pass_on[k] = (terms[core * nc + q] + got[q]).astype(bf16)
        c = copy_to(pass_on.at[k], plane_in.at[k], s2.at[k], r2.at[k], "brick", q * 2 + core)
        c.start()
        sent.append(c)
    copy_to(terms.at[chip], got.at[chip], s1.at[nc], r1.at[nc], "brick", sib).wait_recv()
    for k in range(1, nc):
        q = lax.rem(chip + nc - k, nc)
        copy_to(pass_on.at[k], plane_in.at[k], s2.at[k], r2.at[k], "brick", q * 2 + core).wait_recv()

    def plane_sum(d):
        total = terms[core * nc + chip, d] + got[chip, d]
        for k in range(1, nc):
            total = total + plane_in[k, d].astype(f32)
        return total

    for k in range(1, nd):
        o = lax.rem(dp + k, nd)
        down[k] = plane_sum(o).astype(bf16)
        c = copy_to(down.at[k], down_in.at[k], s3.at[k], r3.at[k], "dp", o)
        c.start()
        sent.append(c)
    total = plane_sum(dp)
    for k in range(1, nd):
        s = lax.rem(dp + nd - k, nd)
        copy_to(down.at[k], down_in.at[k], s3.at[k], r3.at[k], "dp", s).wait_recv()
        total = total + down_in[k].astype(f32)
    final[core * nc + chip] = total
    for k in range(1, nb):
        o = lax.rem(me + k, nb)
        slot = final.at[core * nc + chip]
        c = copy_to(slot, slot, s4.at[k], r4.at[k], "brick", o)
        c.start()
        sent.append(c)
    for k in range(1, nb):
        s = lax.rem(me + nb - k, nb)
        slot = final.at[lax.rem(s, 2) * nc + s // 2]
        copy_to(slot, slot, s4.at[k], r4.at[k], "brick", s).wait_recv()
    for j in range(nb):
        for rows, first, lane in ((cut, 0, 0), (shard - cut, cut, C_OUT)):
            take = min(piece, rows - j * piece)
            if take > 0:
                out[first + j * piece:first + j * piece + take, :] = (
                    final[j, :take, lane:lane + C_OUT])
    for c in sent:
        c.wait_send()


def sum_terms(terms, nb, nd, shard, cut, piece):
    bf16 = jnp.bfloat16
    dma = pltpu.SemaphoreType.DMA
    nc = nb // 2
    wide = 2 * C_OUT
    return pl.pallas_call(
        functools.partial(sum_kernel, nb, nd, shard, cut, piece),
        out_shape=jax.ShapeDtypeStruct((shard, C_OUT), jnp.float32),
        scratch_shapes=[
            pltpu.VMEM((nc, nd, piece, wide), jnp.float32),
            pltpu.VMEM((nc, nd, piece, wide), bf16),
            pltpu.VMEM((nc, nd, piece, wide), bf16),
            pltpu.VMEM((nd, piece, wide), bf16),
            pltpu.VMEM((nd, piece, wide), bf16),
            pltpu.VMEM((nb, piece, wide), jnp.float32),
            dma((nc + 1,)), dma((nc + 1,)), dma((nc,)), dma((nc,)),
            dma((nd,)), dma((nd,)), dma((nb,)), dma((nb,)),
        ],
        compiler_params=pltpu.CompilerParams(
            collective_id=1, has_side_effects=True, vmem_limit_bytes=VMEM_LIMIT),
        name="sum_terms",
    )(terms)


def staged(nb, nd, records, positions, weight, cotangent):
    cap = records.shape[2]
    shard = weight.shape[0]
    cut = up(-(-shard // 2), 8)
    piece = up(-(-cut // nb), 16)
    half = up(-(-shard // 2), 16)
    pos = jnp.pad(positions.reshape(nb, 1, cap), ((0, 0), (0, 7), (0, 128 - cap)))
    wt = jnp.pad(weight, ((0, 2 * half - shard), (0, 0)))
    arrived, places, full = exchange(records.reshape(records.shape[1:]), pos, wt, nb, nd)
    slots = nb * cap
    filled, edge = place(arrived.reshape(slots, -1), places[:, 0, :cap].reshape(1, slots))
    rim = lax.ppermute(edge, "brick", [(i, i + 1) for i in range(nb - 1)])
    shape7 = (BX, 2, BY, 2, BZ, 2, C_OUT)
    cot = cotangent.reshape(shape7).transpose(5, 1, 3, 0, 2, 4, 6).reshape(2, -1, C_OUT)
    act, terms = layer(filled, rim, full, cot, nb, nd, shard, cut, piece)
    act = act.reshape(2, 2, 2, BX, BY, BZ, C_OUT).transpose(3, 1, 4, 2, 5, 0, 6)
    return act.reshape(cotangent.shape), sum_terms(terms, nb, nd, shard, cut, piece)


def fused_kernel(nb, nd, cap, shard, cut, piece, rec, pos, wt, cot, act_out, grad_out,
                 stage, spread, arrived, wts, filled, rim, cols, band, slopes, cots, acts,
                 terms, got, pass_on, plane_in, down, down_in, own, final, grad,
                 rs, rr, ps, pr, ws, wr, xs, xr, loc, bs, br, s1, r1, s2, r2, s3, r3, s4, r4, s5, r5):
    f32, bf16 = jnp.float32, jnp.bfloat16
    n = BX * BY * BZ
    nc = nb // 2
    me = lax.axis_index("brick")
    dp = lax.axis_index("dp")
    core = lax.rem(me, 2)
    chip = me // 2
    sib = me + 1 - 2 * core
    barrier = pltpu.get_barrier_semaphore()
    for k in range(1, nb):
        pl.semaphore_signal(barrier, inc=1, device_id={"brick": lax.rem(me + k, nb)}, device_id_type=MESH)
    for k in range(1, nd):
        pl.semaphore_signal(barrier, inc=1, device_id={"dp": lax.rem(dp + k, nd)}, device_id_type=MESH)
    local = [
        pltpu.make_async_copy(rec.at[me], arrived.at[me], loc.at[0]),
        pltpu.make_async_copy(wt, wts.at[dp], loc.at[1]),
    ]
    for c in local:
        c.start()
    lane = lax.broadcasted_iota(jnp.int32, (cap, nb * cap), 1)
    slot = lax.broadcasted_iota(jnp.int32, (cap, nb * cap), 0)
    to_lanes = jnp.where(lane == slot + me * cap, 1.0, 0.0).astype(bf16)
    lined = jnp.dot(pos[...].astype(f32).astype(bf16), to_lanes, preferred_element_type=f32)
    for o in range(nb):
        stage[o] = jnp.broadcast_to(lined[o:o + 1], stage.shape[1:])
    pl.semaphore_wait(barrier, nb + nd - 2)
    half = wt.shape[0] // 2
    mine = pl.ds(pl.multiple_of(core * half, 16), half)
    theirs = pl.ds(pl.multiple_of((1 - core) * half, 16), half)
    sent = []

    def go(c):
        c.start()
        sent.append(c)

    for k in range(1, nd):
        o = lax.rem(dp + k, nd)
        go(copy_to(wt.at[mine], wts.at[dp, mine], ws.at[k], wr.at[k], "dp", o))
    for k in range(1, nb):
        o = lax.rem(me + k, nb)
        go(copy_to(stage.at[o], spread.at[me], ps.at[k], pr.at[k], "brick", o))
        go(copy_to(rec.at[o], arrived.at[me], rs.at[k], rr.at[k], "brick", o))
    band[...] = jnp.zeros_like(band)
    slopes[...] = jnp.zeros_like(slopes)
    terms[...] = jnp.zeros_like(terms)
    rows = 4 * n
    strip = 4 * BX * BY
    pair = 2 * C_OUT

    def home(r):
        bz, i, j = r // strip, lax.rem(r // (2 * BY), 2 * BX), lax.rem(r, 2 * BY)
        q = lax.rem(i, 2) * 2 + lax.rem(j, 2)
        return q * n + (i // 2) * (BY * BZ) + (j // 2) * BZ + bz

    r_id = lax.broadcasted_iota(jnp.int32, (rows, rows), 0)
    c_id = lax.broadcasted_iota(jnp.int32, (rows, rows), 1)
    turn = jnp.where(r_id == home(c_id), 1.0, 0.0).astype(bf16)
    lined_cot = jnp.concatenate(
        [cot[:, :, z * pair:(z + 1) * pair].reshape(strip, pair) for z in range(BZ)], axis=0)
    turned = jnp.dot(turn, lined_cot, preferred_element_type=f32)
    cots[0] = turned[:, :C_OUT]
    cots[1] = turned[:, C_OUT:]
    for k in range(1, nd):
        s = lax.rem(dp + nd - k, nd)
        copy_to(wt.at[mine], wts.at[s, mine], ws.at[k], wr.at[k], "dp", s).wait_recv()
        go(copy_to(wts.at[s, mine], wts.at[s, mine], xs.at[k], xr.at[k], "brick", sib))
    for k in range(1, nd):
        s = lax.rem(dp + nd - k, nd)
        copy_to(wt.at[theirs], wts.at[s, theirs], xs.at[k], xr.at[k], "brick", sib).wait_recv()
    local[1].wait()
    spots = {0: ((KB - C_IN, 0), (C_IN, NB)), 1: ((0, 0), (2 * C_IN, NB)), 2: ((C_IN, 0), (3 * C_IN, NB))}
    for d in range(nd):
        w = wts[d].astype(f32).T.astype(bf16)
        for t in range(TAPS):
            ab, e = divmod(t, 3)
            for d2, r, take, off in row_parts(t * C_IN, C_IN, shard):
                if d2 == d:
                    for row, col in spots[e]:
                        at = ab * KB + row + off
                        band[at:at + take, col:col + C_OUT] = w[r:r + take]
    sy = shift_matrix(n, 1, 0)
    sz = shift_matrix(n, 0, 1)
    syz = shift_matrix(n, 1, 1)
    for k in range(1, nb):
        s = lax.rem(me + nb - k, nb)
        copy_to(stage.at[s], spread.at[s], ps.at[k], pr.at[k], "brick", s).wait_recv()
    spread[me] = stage[me]
    for k in range(1, nb):
        s = lax.rem(me + nb - k, nb)
        copy_to(rec.at[s], arrived.at[s], rs.at[k], rr.at[k], "brick", s).wait_recv()
    local[0].wait()
    held = spread[0]
    for s in range(1, nb):
        held = held + spread[s]
    want = lax.broadcasted_iota(jnp.int32, (n, nb * cap), 0).astype(f32)
    pick = jnp.where(held[0:1] == want, 1.0, 0.0).astype(bf16)

    def place_plane(x):
        lanes = slice(x * PLANE, (x + 1) * PLANE)
        records = arrived[:, :, lanes].reshape(nb * cap, PLANE)
        filled[:, lanes] = jnp.dot(pick, records, preferred_element_type=f32).astype(bf16)

    last = slice((BS - 1) * PLANE, BS * PLANE)
    place_plane(BS - 1)
    edge = copy_to(filled.at[n - n // BX:n, last], rim, bs, br, "brick", lax.rem(me + 1, nb))
    pl.when(me < nb - 1)(edge.start)
    for x in range(BS - 1):
        place_plane(x)

    def move(s, v):
        return jnp.dot(s, v, preferred_element_type=f32).astype(bf16)

    def fill_columns(x, plane):
        for y in range(-1, BS):
            at = (y if y >= 0 else BS - 1) * ROW
            whole = plane[:, at:at + ROW]
            tail = plane[:, at + ROW - 128:at + ROW]
            if y < 0:
                whole, tail = move(sy, whole), move(syz, tail)
            else:
                tail = move(sz, tail)
            for ox in range(2):
                a = x + 1 - 2 * ox
                for oy in range(2):
                    b = y + 1 - 2 * oy
                    if 0 <= a <= 2 and 0 <= b <= 2:
                        q = slice((ox * 2 + oy) * n, (ox * 2 + oy + 1) * n)
                        k = (a * 3 + b) * KB
                        cols[q, k:k + ROW] = whole
                        cols[q, k + ROW:k + KB] = tail

    def forward(ox):
        q = slice(ox * 2 * n, (ox + 1) * 2 * n)
        for oz in range(2):
            v = jnp.dot(cols[q, :], band[:, oz * NB:(oz + 1) * NB], preferred_element_type=f32)[:, :C_OUT]
            s = 1.0 / (1.0 + jnp.exp(-v))
            acts[q, oz * C_OUT:(oz + 1) * C_OUT] = v * s
            slope = s * (1.0 + v * (1.0 - s))
            slopes[q, oz * NB:oz * NB + C_OUT] = (cots[oz, q, :] * slope).astype(bf16)

    for x in range(BS):
        fill_columns(x, filled[:, x * PLANE:(x + 1) * PLANE])
    forward(1)

    @pl.when(me > 0)
    def _():
        edge.wait_recv()

    @pl.when(me == 0)
    def _():
        rim[...] = jnp.zeros_like(rim)

    fill_columns(-1, jnp.concatenate([rim[...], filled[:n - n // BX, last]], axis=0))
    forward(0)

    def tap_rows(ab):
        g = lax.dot_general(cols[:, ab * KB:(ab + 1) * KB], slopes[...], (((0,), (0,)), ((), ())),
                            preferred_element_type=f32)
        for e in range(3):
            (r0, c0), (r1, c1) = spots[e]
            tap = g[r0:r0 + C_IN, c0:c0 + C_OUT] + g[r1:r1 + C_IN, c1:c1 + C_OUT]
            for d, r, take, off in row_parts((ab * 3 + e) * C_IN, C_IN, shard):
                left = max(0, min(take, cut - r))
                for start, length, base, at in ((off, left, r, 0), (off + left, take - left, r + left - cut, C_OUT)):
                    if length:
                        for j, row, tk, o2 in row_parts(base, length, piece):
                            terms[d, j, row:row + tk, at:at + C_OUT] = tap[start + o2:start + o2 + tk]

    def to_sibling(d):
        return copy_to(terms.at[d, pl.ds((1 - core) * nc, nc)], got.at[d], s1.at[d], r1.at[d], "brick", sib)

    def to_chips(d):
        to_sibling(d).wait_recv()
        for k in range(1, nc):
            q = lax.rem(chip + k, nc)
            pass_on[d, k] = (terms[d, core * nc + q] + got[d, q]).astype(bf16)
            go(copy_to(pass_on.at[d, k], plane_in.at[d, k], s2.at[d, k], r2.at[d, k], "brick", q * 2 + core))

    def to_rank(d):
        total = terms[d, core * nc + chip] + got[d, chip]
        for k in range(1, nc):
            q = lax.rem(chip + nc - k, nc)
            copy_to(pass_on.at[d, k], plane_in.at[d, k], s2.at[d, k], r2.at[d, k], "brick", q * 2 + core).wait_recv()
            total = total + plane_in[d, k].astype(f32)

        @pl.when(dp == d)
        def _():
            own[...] = total

        @pl.when(dp != d)
        def _():
            down[d] = total.astype(bf16)
            copy_to(down.at[d], down_in.at[dp], s3.at[d], r3.at[dp], "dp", d).start()

    ready = 0
    for ab in range(9):
        tap_rows(ab)
        while ready < nd and (ready + 1) * shard <= (ab + 1) * 3 * C_IN:
            go(to_sibling(ready))
            if ready:
                to_chips(ready - 1)
            ready += 1
    to_chips(nd - 1)
    shown = lax.dot_general(turn, acts[...].astype(bf16), (((0,), (0,)), ((), ())), preferred_element_type=f32)
    for z in range(BZ):
        act_out[:, :, z * pair:(z + 1) * pair] = (
            shown[z * strip:(z + 1) * strip].astype(bf16).reshape(2 * BX, 2 * BY, pair))
    for d in range(nd):
        to_rank(d)
    total = own[...]
    for k in range(1, nd):
        s = lax.rem(dp + nd - k, nd)
        copy_to(down.at[s], down_in.at[s], s3.at[s], r3.at[s], "dp", s).wait_recv()
        total = total + down_in[s].astype(f32)
    here = core * nc + chip
    final[here] = total
    for k in range(1, nc):
        q = lax.rem(chip + k, nc)
        go(copy_to(final.at[here], final.at[here], s4.at[k], r4.at[k], "brick", q * 2 + core))
    go(copy_to(final.at[here], final.at[here], s5.at[0], r5.at[0], "brick", sib))
    for k in range(1, nc):
        q = lax.rem(chip + nc - k, nc)
        there = final.at[core * nc + q]
        copy_to(there, there, s4.at[k], r4.at[k], "brick", q * 2 + core).wait_recv()
        go(copy_to(there, there, s5.at[k], r5.at[k], "brick", sib))
    for k in range(nc):
        q = lax.rem(chip + nc - k, nc)
        there = final.at[(1 - core) * nc + q]
        copy_to(there, there, s5.at[k], r5.at[k], "brick", sib).wait_recv()
    for j in range(nb):
        for count, first, at in ((cut, 0, 0), (shard - cut, cut, C_OUT)):
            take = min(piece, count - j * piece)
            if take > 0:
                grad[first + j * piece:first + j * piece + take, :] = final[j, :take, at:at + C_OUT]
    grad_out[...] = grad[...].T
    for c in sent:
        c.wait_send()
    pl.when(me < nb - 1)(edge.wait_send)
    for d in range(nd):
        @pl.when(dp != d)
        def _():
            copy_to(down.at[d], down_in.at[dp], s3.at[d], r3.at[dp], "dp", d).wait_send()


def fused(nb, nd, records, positions, weight, cotangent):
    cap = records.shape[2]
    shard = weight.shape[0]
    cut = up(-(-shard // 2), 8)
    piece = up(-(-cut // nb), 16)
    f32, bf16 = jnp.float32, jnp.bfloat16
    n = BX * BY * BZ
    nc = nb // 2
    wide = 2 * C_OUT
    dma = pltpu.SemaphoreType.DMA
    vmem = pltpu.VMEM
    act, grad = pl.pallas_call(
        functools.partial(fused_kernel, nb, nd, cap, shard, cut, piece),
        out_shape=(
            jax.ShapeDtypeStruct(cotangent.shape[1:], bf16),
            jax.ShapeDtypeStruct((C_OUT, shard), f32),
        ),
        in_specs=[
            pl.BlockSpec(memory_space=pl.ANY),
            pl.BlockSpec(memory_space=pltpu.VMEM),
            pl.BlockSpec(memory_space=pltpu.VMEM),
            pl.BlockSpec(memory_space=pltpu.VMEM),
        ],
        scratch_shapes=[
            vmem((nb, 8, nb * cap), f32),
            vmem((nb, 8, nb * cap), f32),
            vmem(records.shape[1:], bf16),
            vmem((nd, C_OUT, shard), bf16),
            vmem((n, BS * PLANE), bf16),
            vmem((n // BX, PLANE), bf16),
            vmem((4 * n, 9 * KB), bf16),
            vmem((9 * KB, 2 * NB), bf16),
            vmem((4 * n, 2 * NB), bf16),
            vmem((2, 4 * n, C_OUT), f32),
            vmem((4 * n, wide), f32),
            vmem((nd, nb, piece, wide), f32),
            vmem((nd, nc, piece, wide), f32),
            vmem((nd, nc, piece, wide), bf16),
            vmem((nd, nc, piece, wide), bf16),
            vmem((nd, piece, wide), bf16),
            vmem((nd, piece, wide), bf16),
            vmem((piece, wide), f32),
            vmem((nb, piece, wide), f32),
            vmem((shard, C_OUT), f32),
            dma((nb,)), dma((nb,)), dma((nb,)), dma((nb,)),
            dma((nd,)), dma((nd,)), dma((nd,)), dma((nd,)), dma((2,)), dma, dma,
            dma((nd,)), dma((nd,)), dma((nd, nc)), dma((nd, nc)),
            dma((nd,)), dma((nd,)), dma((nc,)), dma((nc,)), dma((nc,)), dma((nc,)),
        ],
        compiler_params=pltpu.CompilerParams(
            collective_id=2, has_side_effects=True, vmem_limit_bytes=VMEM_LIMIT),
        name="fused",
    )(records.reshape(records.shape[1:]), positions.reshape(nb, cap), weight.T,
      cotangent.reshape(cotangent.shape[1:]))
    return act.reshape(cotangent.shape), grad.T


def body(nb, nd, records, positions, weight, cotangent):
    path = staged if records.shape[2] % 16 else fused
    return path(nb, nd, records, positions, weight, cotangent)


def solution(mesh):
    placed = (
        P(("dp", "brick"), None, None, None),
        P(("dp", "brick"), None, None),
        P("dp", None),
        P("dp", "brick", None, None),
    )
    return jax.shard_map(
        functools.partial(body, mesh.shape["brick"], mesh.shape["dp"]),
        mesh=mesh,
        in_specs=placed,
        out_specs=(P("dp", "brick", None, None), P("dp", None)),
        check_vma=False,
    )
```

```python
import functools

import jax
import jax.numpy as jnp
from jax import lax
from jax.experimental import pallas as pl
from jax.experimental.pallas import tpu as pltpu
from jax.sharding import PartitionSpec as P

C_IN = 96
C_OUT = 192
BS = 4
BX = 2
BY = 8
BZ = 8
TAPS = 27
PLANE = BS * BS * C_IN
ROW = BS * C_IN
KB = 512
NB = 256
MESH = pl.DeviceIdType.MESH
VMEM_LIMIT = 48 * 1024 * 1024
FUSED_LIMIT = 62 * 1024 * 1024


def up(n, k):
    return -(-n // k) * k


def copy_to(src, dst, send, recv, axis, peer):
    return pltpu.make_async_remote_copy(
        src_ref=src, dst_ref=dst, send_sem=send, recv_sem=recv,
        device_id={axis: peer}, device_id_type=MESH,
    )


def exchange_kernel(nb, nd, half, rec, pos, wt, rec_out, pos_out, wt_out,
                    rs, rr, ps, pr, ws, wr, xs, xr, loc):
    me = lax.axis_index("brick")
    dp = lax.axis_index("dp")
    core = lax.rem(me, 2)
    sib = me + 1 - 2 * core
    barrier = pltpu.get_barrier_semaphore()
    for k in range(1, nb):
        pl.semaphore_signal(barrier, inc=1, device_id={"brick": lax.rem(me + k, nb)}, device_id_type=MESH)
    for k in range(1, nd):
        pl.semaphore_signal(barrier, inc=1, device_id={"dp": lax.rem(dp + k, nd)}, device_id_type=MESH)
    own = [
        pltpu.make_async_copy(rec.at[me], rec_out.at[me], loc.at[0]),
        pltpu.make_async_copy(pos.at[me], pos_out.at[me], loc.at[1]),
        pltpu.make_async_copy(wt, wt_out.at[dp], loc.at[2]),
    ]
    for c in own:
        c.start()
    pl.semaphore_wait(barrier, nb + nd - 2)
    mine = pl.ds(pl.multiple_of(core * half, 16), half)
    sent = []
    for k in range(1, nd):
        o = lax.rem(dp + k, nd)
        c = copy_to(wt.at[mine], wt_out.at[dp, mine], ws.at[k], wr.at[k], "dp", o)
        c.start()
        sent.append(c)
    for k in range(1, nb):
        o = lax.rem(me + k, nb)
        c = copy_to(pos.at[o], pos_out.at[me], ps.at[k], pr.at[k], "brick", o)
        c.start()
        sent.append(c)
        c = copy_to(rec.at[o], rec_out.at[me], rs.at[k], rr.at[k], "brick", o)
        c.start()
        sent.append(c)
    theirs = pl.ds(pl.multiple_of((1 - core) * half, 16), half)
    for k in range(1, nd):
        s = lax.rem(dp + nd - k, nd)
        copy_to(wt.at[mine], wt_out.at[s, mine], ws.at[k], wr.at[k], "dp", s).wait_recv()
        c = copy_to(wt_out.at[s, mine], wt_out.at[s, mine], xs.at[k], xr.at[k], "brick", sib)
        c.start()
        sent.append(c)
    for k in range(1, nd):
        s = lax.rem(dp + nd - k, nd)
        copy_to(wt.at[theirs], wt_out.at[s, theirs], xs.at[k], xr.at[k], "brick", sib).wait_recv()
    for k in range(1, nb):
        s = lax.rem(me + nb - k, nb)
        copy_to(pos.at[s], pos_out.at[s], ps.at[k], pr.at[k], "brick", s).wait_recv()
        copy_to(rec.at[s], rec_out.at[s], rs.at[k], rr.at[k], "brick", s).wait_recv()
    for c in sent:
        c.wait_send()
    for c in own:
        c.wait()


def exchange(rec, pos, wt, nb, nd):
    half = wt.shape[0] // 2
    dma = pltpu.SemaphoreType.DMA
    return pl.pallas_call(
        functools.partial(exchange_kernel, nb, nd, half),
        out_shape=(
            jax.ShapeDtypeStruct(rec.shape, rec.dtype),
            jax.ShapeDtypeStruct(pos.shape, pos.dtype),
            jax.ShapeDtypeStruct((nd,) + wt.shape, wt.dtype),
        ),
        in_specs=[pl.BlockSpec(memory_space=pl.ANY)] * 3,
        out_specs=(pl.BlockSpec(memory_space=pl.ANY),) * 3,
        scratch_shapes=[dma((nb,)), dma((nb,)), dma((nb,)), dma((nb,)),
                        dma((nd,)), dma((nd,)), dma((nd,)), dma((nd,)), dma((3,))],
        compiler_params=pltpu.CompilerParams(collective_id=0, has_side_effects=True),
        name="exchange",
    )(rec, pos, wt)


def place_kernel(arrived, places, filled, rim):
    n = filled.shape[0]
    slots = arrived.shape[0]
    want = lax.broadcasted_iota(jnp.int32, (n, slots), 0)
    pick = jnp.where(places[...] == want, 1.0, 0.0).astype(jnp.bfloat16)
    for x in range(BS):
        lanes = slice(x * PLANE, (x + 1) * PLANE)
        part = jnp.dot(pick, arrived[:, lanes], preferred_element_type=jnp.float32).astype(jnp.bfloat16)
        filled[:, lanes] = part
        if x == BS - 1:
            rim[...] = part[n - n // BX:]


def place(arrived, places):
    n = BX * BY * BZ
    return pl.pallas_call(
        place_kernel,
        out_shape=(
            jax.ShapeDtypeStruct((n, arrived.shape[1]), arrived.dtype),
            jax.ShapeDtypeStruct((n // BX, PLANE), arrived.dtype),
        ),
        compiler_params=pltpu.CompilerParams(vmem_limit_bytes=VMEM_LIMIT),
        name="place",
    )(arrived, places)


def shift_matrix(n, dy, dz):
    r = lax.broadcasted_iota(jnp.int32, (n, n), 0)
    c = lax.broadcasted_iota(jnp.int32, (n, n), 1)
    hit = c == r - dy * BZ - dz
    if dy:
        hit = hit & (lax.rem(r // BZ, BY) > 0)
    if dz:
        hit = hit & (lax.rem(r, BZ) > 0)
    return jnp.where(hit, 1.0, 0.0).astype(jnp.bfloat16)


def row_parts(first, count, shard):
    done = 0
    while done < count:
        d, r = divmod(first + done, shard)
        take = min(count - done, shard - r)
        yield d, r, take, done
        done += take


def layer_kernel(nd, shard, cut, piece, filled, rim, wt, cot, act, terms, cols, band, slopes):
    n = filled.shape[0]
    rows = 4 * n
    f32, bf16 = jnp.float32, jnp.bfloat16
    band[...] = jnp.zeros_like(band)
    slopes[...] = jnp.zeros_like(slopes)
    terms[...] = jnp.zeros_like(terms)
    spots = {0: ((KB - C_IN, 0), (C_IN, NB)), 1: ((0, 0), (2 * C_IN, NB)), 2: ((C_IN, 0), (3 * C_IN, NB))}
    for t in range(TAPS):
        ab, e = divmod(t, 3)
        for d, r, take, off in row_parts(t * C_IN, C_IN, shard):
            w = wt[d, r:r + take, :]
            for row, col in spots[e]:
                at = ab * KB + row + off
                band[at:at + take, col:col + C_OUT] = w
    sy = shift_matrix(n, 1, 0)
    sz = shift_matrix(n, 0, 1)
    syz = shift_matrix(n, 1, 1)

    def move(s, v):
        return jnp.dot(s, v, preferred_element_type=f32).astype(bf16)

    for x in range(-1, BS):
        if x < 0:
            last = slice((BS - 1) * PLANE, BS * PLANE)
            plane = jnp.concatenate([rim[...], filled[:n - n // BX, last]], axis=0)
        else:
            plane = filled[:, x * PLANE:(x + 1) * PLANE]
        places_x = [(ox, x + 1 - 2 * ox) for ox in range(2) if 0 <= x + 1 - 2 * ox <= 2]
        for y in range(-1, BS):
            at = (y if y >= 0 else BS - 1) * ROW
            whole = plane[:, at:at + ROW]
            tail = plane[:, at + ROW - 128:at + ROW]
            if y < 0:
                whole, tail = move(sy, whole), move(syz, tail)
            else:
                tail = move(sz, tail)
            places_y = [(oy, y + 1 - 2 * oy) for oy in range(2) if 0 <= y + 1 - 2 * oy <= 2]
            for ox, a in places_x:
                for oy, b in places_y:
                    q = slice((ox * 2 + oy) * n, (ox * 2 + oy + 1) * n)
                    k = (a * 3 + b) * KB
                    cols[q, k:k + ROW] = whole
                    cols[q, k + ROW:k + KB] = tail
    for oz in range(2):
        v = jnp.dot(cols[...], band[:, oz * NB:(oz + 1) * NB], preferred_element_type=f32)[:, :C_OUT]
        s = 1.0 / (1.0 + jnp.exp(-v))
        act[oz] = (v * s).astype(bf16)
        slope = s * (1.0 + v * (1.0 - s))
        slopes[:, oz * NB:oz * NB + C_OUT] = (cot[oz].astype(f32) * slope).astype(bf16)
    for ab in range(9):
        g = lax.dot_general(cols[:, ab * KB:(ab + 1) * KB], slopes[...], (((0,), (0,)), ((), ())),
                            preferred_element_type=f32)
        for e in range(3):
            (r0, c0), (r1, c1) = spots[e]
            tap = g[r0:r0 + C_IN, c0:c0 + C_OUT] + g[r1:r1 + C_IN, c1:c1 + C_OUT]
            for d, r, take, off in row_parts((ab * 3 + e) * C_IN, C_IN, shard):
                left = max(0, min(take, cut - r))
                for start, length, base, lane in ((off, left, r, 0), (off + left, take - left, r + left - cut, C_OUT)):
                    if length:
                        for j, rr, tk, o2 in row_parts(base, length, piece):
                            terms[j, d, rr:rr + tk, lane:lane + C_OUT] = tap[start + o2:start + o2 + tk]


def layer(filled, rim, wt, cot, nb, nd, shard, cut, piece):
    rows = cot.shape[1]
    return pl.pallas_call(
        functools.partial(layer_kernel, nd, shard, cut, piece),
        out_shape=(
            jax.ShapeDtypeStruct(cot.shape, jnp.bfloat16),
            jax.ShapeDtypeStruct((nb, nd, piece, 2 * C_OUT), jnp.float32),
        ),
        scratch_shapes=[
            pltpu.VMEM((rows, 9 * KB), jnp.bfloat16),
            pltpu.VMEM((9 * KB, 2 * NB), jnp.bfloat16),
            pltpu.VMEM((rows, 2 * NB), jnp.bfloat16),
        ],
        compiler_params=pltpu.CompilerParams(vmem_limit_bytes=VMEM_LIMIT),
        name="layer",
    )(filled, rim, wt, cot)


def sum_kernel(nb, nd, shard, cut, piece, terms, out, got, pass_on, plane_in, down, down_in, final,
               s1, r1, s2, r2, s3, r3, s4, r4):
    f32, bf16 = jnp.float32, jnp.bfloat16
    nc = nb // 2
    me = lax.axis_index("brick")
    dp = lax.axis_index("dp")
    core = lax.rem(me, 2)
    chip = me // 2
    sib = me + 1 - 2 * core
    barrier = pltpu.get_barrier_semaphore()
    for k in range(1, nb):
        pl.semaphore_signal(barrier, inc=1, device_id={"brick": lax.rem(me + k, nb)}, device_id_type=MESH)
    for k in range(1, nd):
        pl.semaphore_signal(barrier, inc=1, device_id={"dp": lax.rem(dp + k, nd)}, device_id_type=MESH)
    pl.semaphore_wait(barrier, nb + nd - 2)
    sent = []
    for k in range(1, nc + 1):
        q = lax.rem(chip + k, nc)
        c = copy_to(terms.at[(1 - core) * nc + q], got.at[q], s1.at[k], r1.at[k], "brick", sib)
        c.start()
        sent.append(c)
    for k in range(1, nc):
        q = lax.rem(chip + k, nc)
        copy_to(terms.at[q], got.at[q], s1.at[k], r1.at[k], "brick", sib).wait_recv()
        pass_on[k] = (terms[core * nc + q] + got[q]).astype(bf16)
        c = copy_to(pass_on.at[k], plane_in.at[k], s2.at[k], r2.at[k], "brick", q * 2 + core)
        c.start()
        sent.append(c)
    copy_to(terms.at[chip], got.at[chip], s1.at[nc], r1.at[nc], "brick", sib).wait_recv()
    for k in range(1, nc):
        q = lax.rem(chip + nc - k, nc)
        copy_to(pass_on.at[k], plane_in.at[k], s2.at[k], r2.at[k], "brick", q * 2 + core).wait_recv()

    def plane_sum(d):
        total = terms[core * nc + chip, d] + got[chip, d]
        for k in range(1, nc):
            total = total + plane_in[k, d].astype(f32)
        return total

    for k in range(1, nd):
        o = lax.rem(dp + k, nd)
        down[k] = plane_sum(o).astype(bf16)
        c = copy_to(down.at[k], down_in.at[k], s3.at[k], r3.at[k], "dp", o)
        c.start()
        sent.append(c)
    total = plane_sum(dp)
    for k in range(1, nd):
        s = lax.rem(dp + nd - k, nd)
        copy_to(down.at[k], down_in.at[k], s3.at[k], r3.at[k], "dp", s).wait_recv()
        total = total + down_in[k].astype(f32)
    final[core * nc + chip] = total
    for k in range(1, nb):
        o = lax.rem(me + k, nb)
        slot = final.at[core * nc + chip]
        c = copy_to(slot, slot, s4.at[k], r4.at[k], "brick", o)
        c.start()
        sent.append(c)
    for k in range(1, nb):
        s = lax.rem(me + nb - k, nb)
        slot = final.at[lax.rem(s, 2) * nc + s // 2]
        copy_to(slot, slot, s4.at[k], r4.at[k], "brick", s).wait_recv()
    for j in range(nb):
        for rows, first, lane in ((cut, 0, 0), (shard - cut, cut, C_OUT)):
            take = min(piece, rows - j * piece)
            if take > 0:
                out[first + j * piece:first + j * piece + take, :] = (
                    final[j, :take, lane:lane + C_OUT])
    for c in sent:
        c.wait_send()


def sum_terms(terms, nb, nd, shard, cut, piece):
    bf16 = jnp.bfloat16
    dma = pltpu.SemaphoreType.DMA
    nc = nb // 2
    wide = 2 * C_OUT
    return pl.pallas_call(
        functools.partial(sum_kernel, nb, nd, shard, cut, piece),
        out_shape=jax.ShapeDtypeStruct((shard, C_OUT), jnp.float32),
        scratch_shapes=[
            pltpu.VMEM((nc, nd, piece, wide), jnp.float32),
            pltpu.VMEM((nc, nd, piece, wide), bf16),
            pltpu.VMEM((nc, nd, piece, wide), bf16),
            pltpu.VMEM((nd, piece, wide), bf16),
            pltpu.VMEM((nd, piece, wide), bf16),
            pltpu.VMEM((nb, piece, wide), jnp.float32),
            dma((nc + 1,)), dma((nc + 1,)), dma((nc,)), dma((nc,)),
            dma((nd,)), dma((nd,)), dma((nb,)), dma((nb,)),
        ],
        compiler_params=pltpu.CompilerParams(
            collective_id=1, has_side_effects=True, vmem_limit_bytes=VMEM_LIMIT),
        name="sum_terms",
    )(terms)


def staged(nb, nd, records, positions, weight, cotangent):
    cap = records.shape[2]
    shard = weight.shape[0]
    cut = up(-(-shard // 2), 8)
    piece = up(-(-cut // nb), 16)
    half = up(-(-shard // 2), 16)
    pos = jnp.pad(positions.reshape(nb, 1, cap), ((0, 0), (0, 7), (0, 128 - cap)))
    wt = jnp.pad(weight, ((0, 2 * half - shard), (0, 0)))
    arrived, places, full = exchange(records.reshape(records.shape[1:]), pos, wt, nb, nd)
    slots = nb * cap
    filled, edge = place(arrived.reshape(slots, -1), places[:, 0, :cap].reshape(1, slots))
    rim = lax.ppermute(edge, "brick", [(i, i + 1) for i in range(nb - 1)])
    shape7 = (BX, 2, BY, 2, BZ, 2, C_OUT)
    cot = cotangent.reshape(shape7).transpose(5, 1, 3, 0, 2, 4, 6).reshape(2, -1, C_OUT)
    act, terms = layer(filled, rim, full, cot, nb, nd, shard, cut, piece)
    act = act.reshape(2, 2, 2, BX, BY, BZ, C_OUT).transpose(3, 1, 4, 2, 5, 0, 6)
    return act.reshape(cotangent.shape), sum_terms(terms, nb, nd, shard, cut, piece)


def fused_kernel(nb, nd, cap, shard, cut, piece, rec, pos_in, wt_in, cot_in, act_hbm, grad_out,
                 act_out, pos, wt, cot, linear, stage, spread, arrived, wts, filled, rim, cols, band, slopes, cots, acts,
                 terms, got, pass_on, plane_in, down, down_in, own, final, grad,
                 rs, rr, ps, pr, ws, wr, xs, xr, loc, bs, br, s1, r1, s2, r2, s3, r3, s4, r4, s5, r5):
    f32, bf16 = jnp.float32, jnp.bfloat16
    n = BX * BY * BZ
    nc = nb // 2
    me = lax.axis_index("brick")
    dp = lax.axis_index("dp")
    core = lax.rem(me, 2)
    chip = me // 2
    sib = me + 1 - 2 * core
    barrier = pltpu.get_barrier_semaphore()
    for k in range(1, nb):
        pl.semaphore_signal(barrier, inc=1, device_id={"brick": lax.rem(me + k, nb)}, device_id_type=MESH)
    for k in range(1, nd):
        pl.semaphore_signal(barrier, inc=1, device_id={"dp": lax.rem(dp + k, nd)}, device_id_type=MESH)
    local = [
        pltpu.make_async_copy(rec.at[me], arrived.at[me], loc.at[0]),
        pltpu.make_async_copy(wt_in, wts.at[dp], loc.at[1]),
        pltpu.make_async_copy(cot_in, cot, loc.at[2]),
        pltpu.make_async_copy(wt_in, wt, loc.at[3]),
        pltpu.make_async_copy(pos_in, pos, loc.at[4]),
    ]
    for c in reversed(local):
        c.start()
    local[4].wait()
    lane = lax.broadcasted_iota(jnp.int32, (cap, nb * cap), 1)
    slot = lax.broadcasted_iota(jnp.int32, (cap, nb * cap), 0)
    to_lanes = jnp.where(lane == slot + me * cap, 1.0, 0.0).astype(bf16)
    lined = jnp.dot(pos[...].astype(f32).astype(bf16), to_lanes, preferred_element_type=f32)
    for o in range(nb):
        stage[o] = jnp.broadcast_to(lined[o:o + 1], stage.shape[1:])
    pl.semaphore_wait(barrier, nb + nd - 2)
    local[3].wait()
    half = wt.shape[0] // 2
    mine = pl.ds(pl.multiple_of(core * half, 16), half)
    theirs = pl.ds(pl.multiple_of((1 - core) * half, 16), half)
    sent = []

    def go(c):
        c.start()
        sent.append(c)

    for k in range(1, nd):
        o = lax.rem(dp + k, nd)
        go(copy_to(wt.at[mine], wts.at[dp, mine], ws.at[k], wr.at[k], "dp", o))
    for k in range(1, nb):
        o = lax.rem(me + k, nb)
        go(copy_to(stage.at[o], spread.at[me], ps.at[k], pr.at[k], "brick", o))
    order = (3, 1, 0, 2)

    def plane_of(x):
        return pl.ds(x * PLANE, PLANE)

    for x in order:
        for k in range(1, nb):
            o = lax.rem(me + k, nb)
            go(copy_to(rec.at[o, :, plane_of(x)], arrived.at[me, :, plane_of(x)],
                       rs.at[x, k], rr.at[x, k], "brick", o))
    band[...] = jnp.zeros_like(band)
    slopes[...] = jnp.zeros_like(slopes)
    terms[...] = jnp.zeros_like(terms)
    rows = 4 * n
    strip = 4 * BX * BY
    pair = 2 * C_OUT

    def home(r):
        bz, i, j = r // strip, lax.rem(r // (2 * BY), 2 * BX), lax.rem(r, 2 * BY)
        q = lax.rem(i, 2) * 2 + lax.rem(j, 2)
        return q * n + (i // 2) * (BY * BZ) + (j // 2) * BZ + bz

    r_id = lax.broadcasted_iota(jnp.int32, (rows, rows), 0)
    c_id = lax.broadcasted_iota(jnp.int32, (rows, rows), 1)
    turn = jnp.where(r_id == home(c_id), 1.0, 0.0).astype(bf16)
    local[2].wait()
    lined_cot = jnp.concatenate(
        [cot[:, :, z * pair:(z + 1) * pair].reshape(strip, pair) for z in range(BZ)], axis=0)
    turned = jnp.dot(turn, lined_cot, preferred_element_type=f32)
    cots[0] = turned[:, :C_OUT]
    cots[1] = turned[:, C_OUT:]
    sy = shift_matrix(n, 1, 0)
    sz = shift_matrix(n, 0, 1)
    syz = shift_matrix(n, 1, 1)
    for k in range(1, nb):
        s = lax.rem(me + nb - k, nb)
        copy_to(stage.at[s], spread.at[s], ps.at[k], pr.at[k], "brick", s).wait_recv()
    spread[me] = stage[me]
    local[0].wait()
    held = spread[0]
    for s in range(1, nb):
        held = held + spread[s]
    want = lax.broadcasted_iota(jnp.int32, (n, nb * cap), 0).astype(f32)
    pick = jnp.where(held[0:1] == want, 1.0, 0.0).astype(bf16)

    def place_plane(x):
        lanes = slice(x * PLANE, (x + 1) * PLANE)
        for k in range(1, nb):
            s = lax.rem(me + nb - k, nb)
            copy_to(rec.at[s, :, plane_of(x)], arrived.at[s, :, plane_of(x)],
                    rs.at[x, k], rr.at[x, k], "brick", s).wait_recv()
        records = arrived[:, :, lanes].reshape(nb * cap, PLANE)
        filled[:, lanes] = jnp.dot(pick, records, preferred_element_type=f32).astype(bf16)

    last = slice((BS - 1) * PLANE, BS * PLANE)
    edge = copy_to(filled.at[n - n // BX:n, last], rim, bs, br, "brick", lax.rem(me + 1, nb))

    def move(s, v):
        return jnp.dot(s, v, preferred_element_type=f32).astype(bf16)

    def fill_columns(x, plane):
        for y in range(-1, BS):
            at = (y if y >= 0 else BS - 1) * ROW
            whole = plane[:, at:at + ROW]
            tail = plane[:, at + ROW - 128:at + ROW]
            if y < 0:
                whole, tail = move(sy, whole), move(syz, tail)
            else:
                tail = move(sz, tail)
            for ox in range(2):
                a = x + 1 - 2 * ox
                for oy in range(2):
                    b = y + 1 - 2 * oy
                    if 0 <= a <= 2 and 0 <= b <= 2:
                        q = slice((ox * 2 + oy) * n, (ox * 2 + oy + 1) * n)
                        k = (a * 3 + b) * KB
                        cols[q, k:k + ROW] = whole
                        cols[q, k + ROW:k + KB] = tail

    def forward(ox, a, first=False):
        q = slice(ox * 2 * n, (ox + 1) * 2 * n)
        k = slice(a * 3 * KB, (a + 1) * 3 * KB)
        part = jnp.dot(cols[q, k], band[k, :], preferred_element_type=f32)
        linear[q, :] = part if first else linear[q, :] + part

    def activate(ox):
        q = slice(ox * 2 * n, (ox + 1) * 2 * n)
        for oz in range(2):
            v = linear[q, oz * NB:oz * NB + C_OUT]
            s = 1.0 / (1.0 + jnp.exp(-v))
            acts[q, oz * C_OUT:(oz + 1) * C_OUT] = v * s
            slope = s * (1.0 + v * (1.0 - s))
            slopes[q, oz * NB:oz * NB + C_OUT] = (cots[oz, q, :] * slope).astype(bf16)

    def take_plane(x):
        place_plane(x)
        if x == BS - 1:
            pl.when(me < nb - 1)(edge.start)
        fill_columns(x, filled[:, x * PLANE:(x + 1) * PLANE])

    take_plane(3)
    take_plane(1)
    for k in range(1, nd):
        s = lax.rem(dp + nd - k, nd)
        copy_to(wt.at[mine], wts.at[s, mine], ws.at[k], wr.at[k], "dp", s).wait_recv()
        go(copy_to(wts.at[s, mine], wts.at[s, mine], xs.at[k], xr.at[k], "brick", sib))
    for k in range(1, nd):
        s = lax.rem(dp + nd - k, nd)
        copy_to(wt.at[theirs], wts.at[s, theirs], xs.at[k], xr.at[k], "brick", sib).wait_recv()
    local[1].wait()
    spots = {0: ((KB - C_IN, 0), (C_IN, NB)), 1: ((0, 0), (2 * C_IN, NB)), 2: ((C_IN, 0), (3 * C_IN, NB))}
    for d in range(nd):
        w = wts[d].astype(f32).T.astype(bf16)
        for t in range(TAPS):
            ab, e = divmod(t, 3)
            for d2, r, take, off in row_parts(t * C_IN, C_IN, shard):
                if d2 == d:
                    for row, col in spots[e]:
                        at = ab * KB + row + off
                        band[at:at + take, col:col + C_OUT] = w[r:r + take]
    forward(1, 2, True)
    forward(0, 2, True)
    forward(1, 0)
    take_plane(0)
    forward(0, 1)

    @pl.when(me > 0)
    def _():
        edge.wait_recv()

    @pl.when(me == 0)
    def _():
        rim[...] = jnp.zeros_like(rim)

    fill_columns(-1, jnp.concatenate([rim[...], filled[:n - n // BX, last]], axis=0))
    forward(0, 0)
    activate(0)
    take_plane(2)
    forward(1, 1)
    activate(1)

    def tap_rows(ab):
        g = lax.dot_general(cols[:, ab * KB:(ab + 1) * KB], slopes[...], (((0,), (0,)), ((), ())),
                            preferred_element_type=f32)
        for e in range(3):
            (r0, c0), (r1, c1) = spots[e]
            tap = g[r0:r0 + C_IN, c0:c0 + C_OUT] + g[r1:r1 + C_IN, c1:c1 + C_OUT]
            for d, r, take, off in row_parts((ab * 3 + e) * C_IN, C_IN, shard):
                left = max(0, min(take, cut - r))
                for start, length, base, at in ((off, left, r, 0), (off + left, take - left, r + left - cut, C_OUT)):
                    if length:
                        for j, row, tk, o2 in row_parts(base, length, piece):
                            terms[d, j, row:row + tk, at:at + C_OUT] = tap[start + o2:start + o2 + tk]

    def to_sibling(d):
        return copy_to(terms.at[d, pl.ds((1 - core) * nc, nc)], got.at[d], s1.at[d], r1.at[d], "brick", sib)

    def to_chips(d):
        to_sibling(d).wait_recv()
        for k in range(1, nc):
            q = lax.rem(chip + k, nc)
            pass_on[d, k] = (terms[d, core * nc + q] + got[d, q]).astype(bf16)
            go(copy_to(pass_on.at[d, k], plane_in.at[d, k], s2.at[d, k], r2.at[d, k], "brick", q * 2 + core))

    def to_rank(d):
        total = terms[d, core * nc + chip] + got[d, chip]
        for k in range(1, nc):
            q = lax.rem(chip + nc - k, nc)
            copy_to(pass_on.at[d, k], plane_in.at[d, k], s2.at[d, k], r2.at[d, k], "brick", q * 2 + core).wait_recv()
            total = total + plane_in[d, k].astype(f32)

        @pl.when(dp == d)
        def _():
            own[...] = total

        @pl.when(dp != d)
        def _():
            down[d] = total.astype(bf16)
            copy_to(down.at[d], down_in.at[dp], s3.at[d], r3.at[dp], "dp", d).start()

    ready = 0
    for ab in range(9):
        tap_rows(ab)
        while ready < nd and (ready + 1) * shard <= (ab + 1) * 3 * C_IN:
            go(to_sibling(ready))
            if ready:
                to_chips(ready - 1)
            ready += 1
    to_chips(nd - 1)
    shown = lax.dot_general(turn, acts[...].astype(bf16), (((0,), (0,)), ((), ())), preferred_element_type=f32)
    for z in range(BZ):
        act_out[:, :, z * pair:(z + 1) * pair] = (
            shown[z * strip:(z + 1) * strip].astype(bf16).reshape(2 * BX, 2 * BY, pair))
    stored = pltpu.make_async_copy(act_out, act_hbm, loc.at[5])
    stored.start()
    for d in range(nd):
        to_rank(d)
    total = own[...]
    for k in range(1, nd):
        s = lax.rem(dp + nd - k, nd)
        copy_to(down.at[s], down_in.at[s], s3.at[s], r3.at[s], "dp", s).wait_recv()
        total = total + down_in[s].astype(f32)
    here = core * nc + chip
    final[here] = total
    for k in range(1, nc):
        q = lax.rem(chip + k, nc)
        go(copy_to(final.at[here], final.at[here], s4.at[k], r4.at[k], "brick", q * 2 + core))
    go(copy_to(final.at[here], final.at[here], s5.at[0], r5.at[0], "brick", sib))
    for k in range(1, nc):
        q = lax.rem(chip + nc - k, nc)
        there = final.at[core * nc + q]
        copy_to(there, there, s4.at[k], r4.at[k], "brick", q * 2 + core).wait_recv()
        go(copy_to(there, there, s5.at[k], r5.at[k], "brick", sib))
    for k in range(nc):
        q = lax.rem(chip + nc - k, nc)
        there = final.at[(1 - core) * nc + q]
        copy_to(there, there, s5.at[k], r5.at[k], "brick", sib).wait_recv()
    for j in range(nb):
        for count, first, at in ((cut, 0, 0), (shard - cut, cut, C_OUT)):
            take = min(piece, count - j * piece)
            if take > 0:
                grad[first + j * piece:first + j * piece + take, :] = final[j, :take, at:at + C_OUT]
    grad_out[...] = grad[...].T
    stored.wait()
    for c in sent:
        c.wait_send()
    pl.when(me < nb - 1)(edge.wait_send)
    for d in range(nd):
        @pl.when(dp != d)
        def _():
            copy_to(down.at[d], down_in.at[dp], s3.at[d], r3.at[dp], "dp", d).wait_send()


def fused(nb, nd, records, positions, weight, cotangent):
    cap = records.shape[2]
    shard = weight.shape[0]
    cut = up(-(-shard // 2), 8)
    piece = up(-(-cut // nb), 16)
    f32, bf16 = jnp.float32, jnp.bfloat16
    n = BX * BY * BZ
    nc = nb // 2
    wide = 2 * C_OUT
    dma = pltpu.SemaphoreType.DMA
    vmem = pltpu.VMEM
    act, grad = pl.pallas_call(
        functools.partial(fused_kernel, nb, nd, cap, shard, cut, piece),
        out_shape=(
            jax.ShapeDtypeStruct(cotangent.shape[1:], bf16),
            jax.ShapeDtypeStruct((C_OUT, shard), f32),
        ),
        in_specs=[pl.BlockSpec(memory_space=pl.ANY)] * 4,
        out_specs=(pl.BlockSpec(memory_space=pl.ANY), pl.BlockSpec(memory_space=pltpu.VMEM)),
        scratch_shapes=[
            vmem(cotangent.shape[1:], bf16),
            vmem((nb, cap), jnp.int32),
            vmem((C_OUT, shard), bf16),
            vmem(cotangent.shape[1:], bf16),
            vmem((4 * n, 2 * NB), f32),
            vmem((nb, 8, nb * cap), f32),
            vmem((nb, 8, nb * cap), f32),
            vmem(records.shape[1:], bf16),
            vmem((nd, C_OUT, shard), bf16),
            vmem((n, BS * PLANE), bf16),
            vmem((n // BX, PLANE), bf16),
            vmem((4 * n, 9 * KB), bf16),
            vmem((9 * KB, 2 * NB), bf16),
            vmem((4 * n, 2 * NB), bf16),
            vmem((2, 4 * n, C_OUT), f32),
            vmem((4 * n, wide), f32),
            vmem((nd, nb, piece, wide), f32),
            vmem((nd, nc, piece, wide), f32),
            vmem((nd, nc, piece, wide), bf16),
            vmem((nd, nc, piece, wide), bf16),
            vmem((nd, piece, wide), bf16),
            vmem((nd, piece, wide), bf16),
            vmem((piece, wide), f32),
            vmem((nb, piece, wide), f32),
            vmem((shard, C_OUT), f32),
            dma((BS, nb)), dma((BS, nb)), dma((nb,)), dma((nb,)),
            dma((nd,)), dma((nd,)), dma((nd,)), dma((nd,)), dma((6,)), dma, dma,
            dma((nd,)), dma((nd,)), dma((nd, nc)), dma((nd, nc)),
            dma((nd,)), dma((nd,)), dma((nc,)), dma((nc,)), dma((nc,)), dma((nc,)),
        ],
        compiler_params=pltpu.CompilerParams(
            collective_id=2, has_side_effects=True, vmem_limit_bytes=FUSED_LIMIT),
        name="fused",
    )(records.reshape(records.shape[1:]), positions.reshape(nb, cap), weight.T,
      cotangent.reshape(cotangent.shape[1:]))
    return act.reshape(cotangent.shape), grad.T


def body(nb, nd, records, positions, weight, cotangent):
    path = staged if records.shape[2] % 16 else fused
    return path(nb, nd, records, positions, weight, cotangent)


def solution(mesh):
    placed = (
        P(("dp", "brick"), None, None, None),
        P(("dp", "brick"), None, None),
        P("dp", None),
        P("dp", "brick", None, None),
    )
    return jax.shard_map(
        functools.partial(body, mesh.shape["brick"], mesh.shape["dp"]),
        mesh=mesh,
        in_specs=placed,
        out_specs=(P("dp", "brick", None, None), P("dp", None)),
        check_vma=False,
    )
```

```python
import functools

import jax
import jax.numpy as jnp
from jax import lax
from jax.experimental import pallas as pl
from jax.experimental.pallas import tpu as pltpu
from jax.sharding import PartitionSpec as P

C_IN = 96
C_OUT = 192
BS = 4
BX = 2
BY = 8
BZ = 8
TAPS = 27
PLANE = BS * BS * C_IN
ROW = BS * C_IN
KB = 512
SIDE = 64
NB = 256
MESH = pl.DeviceIdType.MESH
VMEM_LIMIT = 48 * 1024 * 1024
FUSED_LIMIT = 62 * 1024 * 1024


def up(n, k):
    return -(-n // k) * k


def copy_to(src, dst, send, recv, axis, peer):
    return pltpu.make_async_remote_copy(
        src_ref=src, dst_ref=dst, send_sem=send, recv_sem=recv,
        device_id={axis: peer}, device_id_type=MESH,
    )


def exchange_kernel(nb, nd, half, rec, pos, wt, rec_out, pos_out, wt_out,
                    rs, rr, ps, pr, ws, wr, xs, xr, loc):
    me = lax.axis_index("brick")
    dp = lax.axis_index("dp")
    core = lax.rem(me, 2)
    sib = me + 1 - 2 * core
    barrier = pltpu.get_barrier_semaphore()
    for k in range(1, nb):
        pl.semaphore_signal(barrier, inc=1, device_id={"brick": lax.rem(me + k, nb)}, device_id_type=MESH)
    for k in range(1, nd):
        pl.semaphore_signal(barrier, inc=1, device_id={"dp": lax.rem(dp + k, nd)}, device_id_type=MESH)
    own = [
        pltpu.make_async_copy(rec.at[me], rec_out.at[me], loc.at[0]),
        pltpu.make_async_copy(pos.at[me], pos_out.at[me], loc.at[1]),
        pltpu.make_async_copy(wt, wt_out.at[dp], loc.at[2]),
    ]
    for c in own:
        c.start()
    pl.semaphore_wait(barrier, nb + nd - 2)
    mine = pl.ds(pl.multiple_of(core * half, 16), half)
    sent = []
    for k in range(1, nd):
        o = lax.rem(dp + k, nd)
        c = copy_to(wt.at[mine], wt_out.at[dp, mine], ws.at[k], wr.at[k], "dp", o)
        c.start()
        sent.append(c)
    for k in range(1, nb):
        o = lax.rem(me + k, nb)
        c = copy_to(pos.at[o], pos_out.at[me], ps.at[k], pr.at[k], "brick", o)
        c.start()
        sent.append(c)
        c = copy_to(rec.at[o], rec_out.at[me], rs.at[k], rr.at[k], "brick", o)
        c.start()
        sent.append(c)
    theirs = pl.ds(pl.multiple_of((1 - core) * half, 16), half)
    for k in range(1, nd):
        s = lax.rem(dp + nd - k, nd)
        copy_to(wt.at[mine], wt_out.at[s, mine], ws.at[k], wr.at[k], "dp", s).wait_recv()
        c = copy_to(wt_out.at[s, mine], wt_out.at[s, mine], xs.at[k], xr.at[k], "brick", sib)
        c.start()
        sent.append(c)
    for k in range(1, nd):
        s = lax.rem(dp + nd - k, nd)
        copy_to(wt.at[theirs], wt_out.at[s, theirs], xs.at[k], xr.at[k], "brick", sib).wait_recv()
    for k in range(1, nb):
        s = lax.rem(me + nb - k, nb)
        copy_to(pos.at[s], pos_out.at[s], ps.at[k], pr.at[k], "brick", s).wait_recv()
        copy_to(rec.at[s], rec_out.at[s], rs.at[k], rr.at[k], "brick", s).wait_recv()
    for c in sent:
        c.wait_send()
    for c in own:
        c.wait()


def exchange(rec, pos, wt, nb, nd):
    half = wt.shape[0] // 2
    dma = pltpu.SemaphoreType.DMA
    return pl.pallas_call(
        functools.partial(exchange_kernel, nb, nd, half),
        out_shape=(
            jax.ShapeDtypeStruct(rec.shape, rec.dtype),
            jax.ShapeDtypeStruct(pos.shape, pos.dtype),
            jax.ShapeDtypeStruct((nd,) + wt.shape, wt.dtype),
        ),
        in_specs=[pl.BlockSpec(memory_space=pl.ANY)] * 3,
        out_specs=(pl.BlockSpec(memory_space=pl.ANY),) * 3,
        scratch_shapes=[dma((nb,)), dma((nb,)), dma((nb,)), dma((nb,)),
                        dma((nd,)), dma((nd,)), dma((nd,)), dma((nd,)), dma((3,))],
        compiler_params=pltpu.CompilerParams(collective_id=0, has_side_effects=True),
        name="exchange",
    )(rec, pos, wt)


def place_kernel(arrived, places, filled, rim):
    n = filled.shape[0]
    slots = arrived.shape[0]
    want = lax.broadcasted_iota(jnp.int32, (n, slots), 0)
    pick = jnp.where(places[...] == want, 1.0, 0.0).astype(jnp.bfloat16)
    for x in range(BS):
        lanes = slice(x * PLANE, (x + 1) * PLANE)
        part = jnp.dot(pick, arrived[:, lanes], preferred_element_type=jnp.float32).astype(jnp.bfloat16)
        filled[:, lanes] = part
        if x == BS - 1:
            rim[...] = part[n - n // BX:]


def place(arrived, places):
    n = BX * BY * BZ
    return pl.pallas_call(
        place_kernel,
        out_shape=(
            jax.ShapeDtypeStruct((n, arrived.shape[1]), arrived.dtype),
            jax.ShapeDtypeStruct((n // BX, PLANE), arrived.dtype),
        ),
        compiler_params=pltpu.CompilerParams(vmem_limit_bytes=VMEM_LIMIT),
        name="place",
    )(arrived, places)


def shift_matrix(n, dy, dz):
    r = lax.broadcasted_iota(jnp.int32, (n, n), 0)
    c = lax.broadcasted_iota(jnp.int32, (n, n), 1)
    hit = c == r - dy * BZ - dz
    if dy:
        hit = hit & (lax.rem(r // BZ, BY) > 0)
    if dz:
        hit = hit & (lax.rem(r, BZ) > 0)
    return jnp.where(hit, 1.0, 0.0).astype(jnp.bfloat16)


def row_parts(first, count, shard):
    done = 0
    while done < count:
        d, r = divmod(first + done, shard)
        take = min(count - done, shard - r)
        yield d, r, take, done
        done += take


def layer_kernel(nd, shard, cut, piece, filled, rim, wt, cot, act, terms, cols, band, slopes):
    n = filled.shape[0]
    rows = 4 * n
    f32, bf16 = jnp.float32, jnp.bfloat16
    band[...] = jnp.zeros_like(band)
    slopes[...] = jnp.zeros_like(slopes)
    terms[...] = jnp.zeros_like(terms)
    spots = {0: ((KB - C_IN, 0), (C_IN, NB)), 1: ((0, 0), (2 * C_IN, NB)), 2: ((C_IN, 0), (3 * C_IN, NB))}
    for t in range(TAPS):
        ab, e = divmod(t, 3)
        for d, r, take, off in row_parts(t * C_IN, C_IN, shard):
            w = wt[d, r:r + take, :]
            for row, col in spots[e]:
                at = ab * KB + row + off
                band[at:at + take, col:col + C_OUT] = w
    sy = shift_matrix(n, 1, 0)
    sz = shift_matrix(n, 0, 1)
    syz = shift_matrix(n, 1, 1)

    def move(s, v):
        return jnp.dot(s, v, preferred_element_type=f32).astype(bf16)

    for x in range(-1, BS):
        if x < 0:
            last = slice((BS - 1) * PLANE, BS * PLANE)
            plane = jnp.concatenate([rim[...], filled[:n - n // BX, last]], axis=0)
        else:
            plane = filled[:, x * PLANE:(x + 1) * PLANE]
        places_x = [(ox, x + 1 - 2 * ox) for ox in range(2) if 0 <= x + 1 - 2 * ox <= 2]
        for y in range(-1, BS):
            at = (y if y >= 0 else BS - 1) * ROW
            whole = plane[:, at:at + ROW]
            tail = plane[:, at + ROW - 128:at + ROW]
            if y < 0:
                whole, tail = move(sy, whole), move(syz, tail)
            else:
                tail = move(sz, tail)
            places_y = [(oy, y + 1 - 2 * oy) for oy in range(2) if 0 <= y + 1 - 2 * oy <= 2]
            for ox, a in places_x:
                for oy, b in places_y:
                    q = slice((ox * 2 + oy) * n, (ox * 2 + oy + 1) * n)
                    k = (a * 3 + b) * KB
                    cols[q, k:k + ROW] = whole
                    cols[q, k + ROW:k + KB] = tail
    for oz in range(2):
        v = jnp.dot(cols[...], band[:, oz * NB:(oz + 1) * NB], preferred_element_type=f32)[:, :C_OUT]
        s = 1.0 / (1.0 + jnp.exp(-v))
        act[oz] = (v * s).astype(bf16)
        slope = s * (1.0 + v * (1.0 - s))
        slopes[:, oz * NB:oz * NB + C_OUT] = (cot[oz].astype(f32) * slope).astype(bf16)
    for ab in range(9):
        g = lax.dot_general(cols[:, ab * KB:(ab + 1) * KB], slopes[...], (((0,), (0,)), ((), ())),
                            preferred_element_type=f32)
        for e in range(3):
            (r0, c0), (r1, c1) = spots[e]
            tap = g[r0:r0 + C_IN, c0:c0 + C_OUT] + g[r1:r1 + C_IN, c1:c1 + C_OUT]
            for d, r, take, off in row_parts((ab * 3 + e) * C_IN, C_IN, shard):
                left = max(0, min(take, cut - r))
                for start, length, base, lane in ((off, left, r, 0), (off + left, take - left, r + left - cut, C_OUT)):
                    if length:
                        for j, rr, tk, o2 in row_parts(base, length, piece):
                            terms[j, d, rr:rr + tk, lane:lane + C_OUT] = tap[start + o2:start + o2 + tk]


def layer(filled, rim, wt, cot, nb, nd, shard, cut, piece):
    rows = cot.shape[1]
    return pl.pallas_call(
        functools.partial(layer_kernel, nd, shard, cut, piece),
        out_shape=(
            jax.ShapeDtypeStruct(cot.shape, jnp.bfloat16),
            jax.ShapeDtypeStruct((nb, nd, piece, 2 * C_OUT), jnp.float32),
        ),
        scratch_shapes=[
            pltpu.VMEM((rows, 9 * KB), jnp.bfloat16),
            pltpu.VMEM((9 * KB, 2 * NB), jnp.bfloat16),
            pltpu.VMEM((rows, 2 * NB), jnp.bfloat16),
        ],
        compiler_params=pltpu.CompilerParams(vmem_limit_bytes=VMEM_LIMIT),
        name="layer",
    )(filled, rim, wt, cot)


def sum_kernel(nb, nd, shard, cut, piece, terms, out, got, pass_on, plane_in, down, down_in, final,
               s1, r1, s2, r2, s3, r3, s4, r4):
    f32, bf16 = jnp.float32, jnp.bfloat16
    nc = nb // 2
    me = lax.axis_index("brick")
    dp = lax.axis_index("dp")
    core = lax.rem(me, 2)
    chip = me // 2
    sib = me + 1 - 2 * core
    barrier = pltpu.get_barrier_semaphore()
    for k in range(1, nb):
        pl.semaphore_signal(barrier, inc=1, device_id={"brick": lax.rem(me + k, nb)}, device_id_type=MESH)
    for k in range(1, nd):
        pl.semaphore_signal(barrier, inc=1, device_id={"dp": lax.rem(dp + k, nd)}, device_id_type=MESH)
    pl.semaphore_wait(barrier, nb + nd - 2)
    sent = []
    for k in range(1, nc + 1):
        q = lax.rem(chip + k, nc)
        c = copy_to(terms.at[(1 - core) * nc + q], got.at[q], s1.at[k], r1.at[k], "brick", sib)
        c.start()
        sent.append(c)
    for k in range(1, nc):
        q = lax.rem(chip + k, nc)
        copy_to(terms.at[q], got.at[q], s1.at[k], r1.at[k], "brick", sib).wait_recv()
        pass_on[k] = (terms[core * nc + q] + got[q]).astype(bf16)
        c = copy_to(pass_on.at[k], plane_in.at[k], s2.at[k], r2.at[k], "brick", q * 2 + core)
        c.start()
        sent.append(c)
    copy_to(terms.at[chip], got.at[chip], s1.at[nc], r1.at[nc], "brick", sib).wait_recv()
    for k in range(1, nc):
        q = lax.rem(chip + nc - k, nc)
        copy_to(pass_on.at[k], plane_in.at[k], s2.at[k], r2.at[k], "brick", q * 2 + core).wait_recv()

    def plane_sum(d):
        total = terms[core * nc + chip, d] + got[chip, d]
        for k in range(1, nc):
            total = total + plane_in[k, d].astype(f32)
        return total

    for k in range(1, nd):
        o = lax.rem(dp + k, nd)
        down[k] = plane_sum(o).astype(bf16)
        c = copy_to(down.at[k], down_in.at[k], s3.at[k], r3.at[k], "dp", o)
        c.start()
        sent.append(c)
    total = plane_sum(dp)
    for k in range(1, nd):
        s = lax.rem(dp + nd - k, nd)
        copy_to(down.at[k], down_in.at[k], s3.at[k], r3.at[k], "dp", s).wait_recv()
        total = total + down_in[k].astype(f32)
    final[core * nc + chip] = total
    for k in range(1, nb):
        o = lax.rem(me + k, nb)
        slot = final.at[core * nc + chip]
        c = copy_to(slot, slot, s4.at[k], r4.at[k], "brick", o)
        c.start()
        sent.append(c)
    for k in range(1, nb):
        s = lax.rem(me + nb - k, nb)
        slot = final.at[lax.rem(s, 2) * nc + s // 2]
        copy_to(slot, slot, s4.at[k], r4.at[k], "brick", s).wait_recv()
    for j in range(nb):
        for rows, first, lane in ((cut, 0, 0), (shard - cut, cut, C_OUT)):
            take = min(piece, rows - j * piece)
            if take > 0:
                out[first + j * piece:first + j * piece + take, :] = (
                    final[j, :take, lane:lane + C_OUT])
    for c in sent:
        c.wait_send()


def sum_terms(terms, nb, nd, shard, cut, piece):
    bf16 = jnp.bfloat16
    dma = pltpu.SemaphoreType.DMA
    nc = nb // 2
    wide = 2 * C_OUT
    return pl.pallas_call(
        functools.partial(sum_kernel, nb, nd, shard, cut, piece),
        out_shape=jax.ShapeDtypeStruct((shard, C_OUT), jnp.float32),
        scratch_shapes=[
            pltpu.VMEM((nc, nd, piece, wide), jnp.float32),
            pltpu.VMEM((nc, nd, piece, wide), bf16),
            pltpu.VMEM((nc, nd, piece, wide), bf16),
            pltpu.VMEM((nd, piece, wide), bf16),
            pltpu.VMEM((nd, piece, wide), bf16),
            pltpu.VMEM((nb, piece, wide), jnp.float32),
            dma((nc + 1,)), dma((nc + 1,)), dma((nc,)), dma((nc,)),
            dma((nd,)), dma((nd,)), dma((nb,)), dma((nb,)),
        ],
        compiler_params=pltpu.CompilerParams(
            collective_id=1, has_side_effects=True, vmem_limit_bytes=VMEM_LIMIT),
        name="sum_terms",
    )(terms)


def staged(nb, nd, records, positions, weight, cotangent):
    cap = records.shape[2]
    shard = weight.shape[0]
    cut = up(-(-shard // 2), 8)
    piece = up(-(-cut // nb), 16)
    half = up(-(-shard // 2), 16)
    pos = jnp.pad(positions.reshape(nb, 1, cap), ((0, 0), (0, 7), (0, 128 - cap)))
    wt = jnp.pad(weight, ((0, 2 * half - shard), (0, 0)))
    arrived, places, full = exchange(records.reshape(records.shape[1:]), pos, wt, nb, nd)
    slots = nb * cap
    filled, edge = place(arrived.reshape(slots, -1), places[:, 0, :cap].reshape(1, slots))
    rim = lax.ppermute(edge, "brick", [(i, i + 1) for i in range(nb - 1)])
    shape7 = (BX, 2, BY, 2, BZ, 2, C_OUT)
    cot = cotangent.reshape(shape7).transpose(5, 1, 3, 0, 2, 4, 6).reshape(2, -1, C_OUT)
    act, terms = layer(filled, rim, full, cot, nb, nd, shard, cut, piece)
    act = act.reshape(2, 2, 2, BX, BY, BZ, C_OUT).transpose(3, 1, 4, 2, 5, 0, 6)
    return act.reshape(cotangent.shape), sum_terms(terms, nb, nd, shard, cut, piece)


def fused_kernel(nb, nd, cap, shard, main, piece, rec, pos_in, wt_in, cot_in, act_hbm, grad_out,
                 act_out, pos, wt, cot, linear, stage, spread, arrived, wts, turned_wts, filled, rim, cols, band, slopes, cots, acts,
                 terms, got, pass_on, plane_in, down, down_in, own, final,
                 rs, rr, ps, pr, ws, wr, xs, xr, loc, bs, br, s1, r1, s2, r2, s3, r3, s4, r4, s5, r5):
    f32, bf16 = jnp.float32, jnp.bfloat16
    n = BX * BY * BZ
    nc = nb // 2
    me = lax.axis_index("brick")
    dp = lax.axis_index("dp")
    core = lax.rem(me, 2)
    chip = me // 2
    sib = me + 1 - 2 * core
    barrier = pltpu.get_barrier_semaphore()
    for k in range(1, nb):
        pl.semaphore_signal(barrier, inc=1, device_id={"brick": lax.rem(me + k, nb)}, device_id_type=MESH)
    for k in range(1, nd):
        pl.semaphore_signal(barrier, inc=1, device_id={"dp": lax.rem(dp + k, nd)}, device_id_type=MESH)
    local = [
        pltpu.make_async_copy(rec.at[me], arrived.at[me], loc.at[0]),
        pltpu.make_async_copy(wt_in, wts.at[dp], loc.at[1]),
        pltpu.make_async_copy(cot_in, cot, loc.at[2]),
        pltpu.make_async_copy(wt_in, wt, loc.at[3]),
        pltpu.make_async_copy(pos_in, pos, loc.at[4]),
    ]
    for c in reversed(local):
        c.start()
    local[4].wait()
    lane = lax.broadcasted_iota(jnp.int32, (cap, nb * cap), 1)
    slot = lax.broadcasted_iota(jnp.int32, (cap, nb * cap), 0)
    to_lanes = jnp.where(lane == slot + me * cap, 1.0, 0.0).astype(bf16)
    lined = jnp.dot(pos[...].astype(f32).astype(bf16), to_lanes, preferred_element_type=f32)
    for o in range(nb):
        stage[o] = jnp.broadcast_to(lined[o:o + 1], stage.shape[1:])
    pl.semaphore_wait(barrier, nb + nd - 2)
    local[3].wait()
    half = wt.shape[0] // 2
    mine = pl.ds(pl.multiple_of(core * half, 16), half)
    theirs = pl.ds(pl.multiple_of((1 - core) * half, 16), half)
    sent = []

    def go(c):
        c.start()
        sent.append(c)

    for k in range(1, nd):
        o = lax.rem(dp + k, nd)
        go(copy_to(wt.at[mine], wts.at[dp, mine], ws.at[k], wr.at[k], "dp", o))
    for k in range(1, nb):
        o = lax.rem(me + k, nb)
        go(copy_to(stage.at[o], spread.at[me], ps.at[k], pr.at[k], "brick", o))
    order = (3, 1, 0, 2)

    def plane_of(x):
        return pl.ds(x * PLANE, PLANE)

    for x in order:
        for k in range(1, nb):
            o = lax.rem(me + k, nb)
            go(copy_to(rec.at[o, :, plane_of(x)], arrived.at[me, :, plane_of(x)],
                       rs.at[x, k], rr.at[x, k], "brick", o))
    band[...] = jnp.zeros_like(band)
    slopes[...] = jnp.zeros_like(slopes)
    terms[...] = jnp.zeros_like(terms)
    rows = 4 * n
    strip = 4 * BX * BY
    pair = 2 * C_OUT

    def home(r):
        bz, i, j = r // strip, lax.rem(r // (2 * BY), 2 * BX), lax.rem(r, 2 * BY)
        q = lax.rem(i, 2) * 2 + lax.rem(j, 2)
        return q * n + (i // 2) * (BY * BZ) + (j // 2) * BZ + bz

    r_id = lax.broadcasted_iota(jnp.int32, (rows, rows), 0)
    c_id = lax.broadcasted_iota(jnp.int32, (rows, rows), 1)
    turn = jnp.where(r_id == home(c_id), 1.0, 0.0).astype(bf16)
    local[2].wait()
    lined_cot = jnp.concatenate(
        [cot[:, :, z * pair:(z + 1) * pair].reshape(strip, pair) for z in range(BZ)], axis=0)
    turned = jnp.dot(turn, lined_cot, preferred_element_type=f32)
    cots[0] = turned[:, :C_OUT]
    cots[1] = turned[:, C_OUT:]
    sy = shift_matrix(n, 1, 0)
    sz = shift_matrix(n, 0, 1)
    syz = shift_matrix(n, 1, 1)
    for k in range(1, nb):
        s = lax.rem(me + nb - k, nb)
        copy_to(stage.at[s], spread.at[s], ps.at[k], pr.at[k], "brick", s).wait_recv()
    spread[me] = stage[me]
    local[0].wait()
    held = spread[0]
    for s in range(1, nb):
        held = held + spread[s]
    want = lax.broadcasted_iota(jnp.int32, (n, nb * cap), 0).astype(f32)
    pick = jnp.where(held[0:1] == want, 1.0, 0.0).astype(bf16)

    def place_plane(x):
        lanes = slice(x * PLANE, (x + 1) * PLANE)
        for k in range(1, nb):
            s = lax.rem(me + nb - k, nb)
            copy_to(rec.at[s, :, plane_of(x)], arrived.at[s, :, plane_of(x)],
                    rs.at[x, k], rr.at[x, k], "brick", s).wait_recv()
        records = arrived[:, :, lanes].reshape(nb * cap, PLANE)
        filled[:, lanes] = jnp.dot(pick, records, preferred_element_type=f32).astype(bf16)

    last = slice((BS - 1) * PLANE, BS * PLANE)
    edge = copy_to(filled.at[n - n // BX:n, last], rim, bs, br, "brick", lax.rem(me + 1, nb))

    def move(s, v):
        return jnp.dot(s, v, preferred_element_type=f32).astype(bf16)

    def fill_columns(x, plane):
        for y in range(-1, BS):
            at = (y if y >= 0 else BS - 1) * ROW
            whole = plane[:, at:at + ROW]
            tail = plane[:, at + ROW - 128:at + ROW]
            if y < 0:
                whole, tail = move(sy, whole), move(syz, tail)
            else:
                tail = move(sz, tail)
            for ox in range(2):
                a = x + 1 - 2 * ox
                for oy in range(2):
                    b = y + 1 - 2 * oy
                    if 0 <= a <= 2 and 0 <= b <= 2:
                        q = slice((ox * 2 + oy) * n, (ox * 2 + oy + 1) * n)
                        k = (a * 3 + b) * KB
                        cols[q, k:k + ROW] = whole
                        cols[q, k + ROW:k + KB] = tail

    def forward(ox, a, first=False):
        q = slice(ox * 2 * n, (ox + 1) * 2 * n)
        k = slice(a * 3 * KB, (a + 1) * 3 * KB)
        part = jnp.dot(cols[q, k], band[k, :], preferred_element_type=f32)
        linear[q, :] = part if first else linear[q, :] + part

    def activate(ox):
        q = slice(ox * 2 * n, (ox + 1) * 2 * n)
        for oz in range(2):
            v = linear[q, oz * NB:oz * NB + C_OUT]
            s = 1.0 / (1.0 + jnp.exp(-v))
            acts[q, oz * C_OUT:(oz + 1) * C_OUT] = v * s
            slope = s * (1.0 + v * (1.0 - s))
            slopes[q, oz * NB:oz * NB + C_OUT] = (cots[oz, q, :] * slope).astype(bf16)

    def take_plane(x):
        place_plane(x)
        if x == BS - 1:
            pl.when(me < nb - 1)(edge.start)
        fill_columns(x, filled[:, x * PLANE:(x + 1) * PLANE])

    def turn_weights(d):
        turned_wts[d] = wts[d].astype(f32).T.astype(bf16)

    take_plane(3)
    take_plane(1)
    for k in range(1, nd):
        s = lax.rem(dp + nd - k, nd)
        copy_to(wt.at[mine], wts.at[s, mine], ws.at[k], wr.at[k], "dp", s).wait_recv()
        go(copy_to(wts.at[s, mine], wts.at[s, mine], xs.at[k], xr.at[k], "brick", sib))
    local[1].wait()
    turn_weights(dp)
    for k in range(1, nd):
        s = lax.rem(dp + nd - k, nd)
        copy_to(wt.at[theirs], wts.at[s, theirs], xs.at[k], xr.at[k], "brick", sib).wait_recv()
        turn_weights(s)
    spots = {0: ((KB - C_IN, 0), (C_IN, NB)), 1: ((0, 0), (2 * C_IN, NB)), 2: ((C_IN, 0), (3 * C_IN, NB))}
    for d in range(nd):
        w = turned_wts[d]
        for t in range(TAPS):
            ab, e = divmod(t, 3)
            for d2, r, take, off in row_parts(t * C_IN, C_IN, shard):
                if d2 == d:
                    for row, col in spots[e]:
                        at = ab * KB + row + off
                        band[at:at + take, col:col + C_OUT] = w[r:r + take]
    forward(1, 2, True)
    forward(0, 2, True)
    forward(1, 0)
    take_plane(0)
    forward(0, 1)

    @pl.when(me > 0)
    def _():
        edge.wait_recv()

    @pl.when(me == 0)
    def _():
        rim[...] = jnp.zeros_like(rim)

    fill_columns(-1, jnp.concatenate([rim[...], filled[:n - n // BX, last]], axis=0))
    forward(0, 0)
    activate(0)
    take_plane(2)
    forward(1, 1)
    activate(1)

    def put(d, r, rows, first):
        count = rows.shape[0]
        head = max(0, min(count, main - r))
        spans = [(0, head, r, 0, 0, C_OUT)] if head else []
        if head < count:
            for m in range(C_OUT // SIDE):
                spans.append((head, count, r + head - main + m * (shard - main), C_OUT, m * SIDE, SIDE))
        for lo, hi, base, at, col, width in spans:
            for j, row, tk, off in row_parts(base, hi - lo, piece):
                part = rows[lo + off:lo + off + tk, col:col + width]
                if not first:
                    part = part + terms[d, j, row:row + tk, at:at + width]
                terms[d, j, row:row + tk, at:at + width] = part

    def tap_rows(ab, first=True):
        g = lax.dot_general(cols[:, ab * KB:(ab + 1) * KB], slopes[...], (((0,), (0,)), ((), ())),
                            preferred_element_type=f32)
        for e in range(3):
            (r0, c0), (r1, c1) = spots[e]
            tap = g[r0:r0 + C_IN, c0:c0 + C_OUT] + g[r1:r1 + C_IN, c1:c1 + C_OUT]
            for d, r, take, off in row_parts((ab * 3 + e) * C_IN, C_IN, shard):
                put(d, r, tap[off:off + take], first)

    def to_sibling(d):
        return copy_to(terms.at[d, pl.ds((1 - core) * nc, nc)], got.at[d], s1.at[d], r1.at[d], "brick", sib)

    def to_chips(d):
        to_sibling(d).wait_recv()
        for k in range(1, nc):
            q = lax.rem(chip + k, nc)
            pass_on[d, k] = (terms[d, core * nc + q] + got[d, q]).astype(bf16)
            go(copy_to(pass_on.at[d, k], plane_in.at[d, k], s2.at[d, k], r2.at[d, k], "brick", q * 2 + core))

    def to_rank(d):
        total = terms[d, core * nc + chip] + got[d, chip]
        for k in range(1, nc):
            q = lax.rem(chip + nc - k, nc)
            copy_to(pass_on.at[d, k], plane_in.at[d, k], s2.at[d, k], r2.at[d, k], "brick", q * 2 + core).wait_recv()
            total = total + plane_in[d, k].astype(f32)

        @pl.when(dp == d)
        def _():
            own[...] = total

        @pl.when(dp != d)
        def _():
            down[d] = total.astype(bf16)
            copy_to(down.at[d], down_in.at[dp], s3.at[d], r3.at[dp], "dp", d).start()

    ready = 0
    for ab in range(9):
        tap_rows(ab)
        while ready < nd and (ready + 1) * shard <= (ab + 1) * 3 * C_IN:
            go(to_sibling(ready))
            if ready:
                to_chips(ready - 1)
            ready += 1
    to_chips(nd - 1)
    shown = lax.dot_general(turn, acts[...].astype(bf16), (((0,), (0,)), ((), ())), preferred_element_type=f32)
    for z in range(BZ):
        act_out[:, :, z * pair:(z + 1) * pair] = (
            shown[z * strip:(z + 1) * strip].reshape(2 * BX, 2 * BY, pair))
    stored = pltpu.make_async_copy(act_out, act_hbm, loc.at[5])
    stored.start()
    for d in range(nd):
        to_rank(d)
    total = own[...]
    for k in range(1, nd):
        s = lax.rem(dp + nd - k, nd)
        copy_to(down.at[s], down_in.at[s], s3.at[s], r3.at[s], "dp", s).wait_recv()
        total = total + down_in[s].astype(f32)
    here = core * nc + chip
    final[here] = total
    for k in range(1, nc):
        q = lax.rem(chip + k, nc)
        go(copy_to(final.at[here], final.at[here], s4.at[k], r4.at[k], "brick", q * 2 + core))
    go(copy_to(final.at[here], final.at[here], s5.at[0], r5.at[0], "brick", sib))
    for k in range(1, nc):
        q = lax.rem(chip + nc - k, nc)
        there = final.at[core * nc + q]
        copy_to(there, there, s4.at[k], r4.at[k], "brick", q * 2 + core).wait_recv()
        go(copy_to(there, there, s5.at[k], r5.at[k], "brick", sib))
    for k in range(nc):
        q = lax.rem(chip + nc - k, nc)
        there = final.at[(1 - core) * nc + q]
        copy_to(there, there, s5.at[k], r5.at[k], "brick", sib).wait_recv()
    for j in range(nb):
        grad_out[j * piece:(j + 1) * piece, :] = final[j, :, :C_OUT]
    for m in range(C_OUT // SIDE):
        for j, row, tk, off in row_parts(m * (shard - main), shard - main, piece):
            grad_out[main + off:main + off + tk, m * SIDE:(m + 1) * SIDE] = final[j, row:row + tk, C_OUT:]
    stored.wait()
    for c in sent:
        c.wait_send()
    pl.when(me < nb - 1)(edge.wait_send)
    for d in range(nd):
        @pl.when(dp != d)
        def _():
            copy_to(down.at[d], down_in.at[dp], s3.at[d], r3.at[dp], "dp", d).wait_send()


def fused(nb, nd, records, positions, weight, cotangent):
    cap = records.shape[2]
    shard = weight.shape[0]
    main = up(-(-shard * C_OUT // (C_OUT + SIDE)), nb * 16)
    piece = main // nb
    f32, bf16 = jnp.float32, jnp.bfloat16
    n = BX * BY * BZ
    nc = nb // 2
    wide = C_OUT + SIDE
    dma = pltpu.SemaphoreType.DMA
    vmem = pltpu.VMEM
    act, grad = pl.pallas_call(
        functools.partial(fused_kernel, nb, nd, cap, shard, main, piece),
        out_shape=(
            jax.ShapeDtypeStruct(cotangent.shape[1:], f32),
            jax.ShapeDtypeStruct((shard, C_OUT), f32),
        ),
        in_specs=[pl.BlockSpec(memory_space=pl.ANY)] * 4,
        out_specs=(pl.BlockSpec(memory_space=pl.ANY), pl.BlockSpec(memory_space=pltpu.VMEM)),
        scratch_shapes=[
            vmem(cotangent.shape[1:], f32),
            vmem((nb, cap), jnp.int32),
            vmem((C_OUT, shard), bf16),
            vmem(cotangent.shape[1:], bf16),
            vmem((4 * n, 2 * NB), f32),
            vmem((nb, 8, nb * cap), f32),
            vmem((nb, 8, nb * cap), f32),
            vmem(records.shape[1:], bf16),
            vmem((nd, C_OUT, shard), bf16),
            vmem((nd, shard, C_OUT), bf16),
            vmem((n, BS * PLANE), bf16),
            vmem((n // BX, PLANE), bf16),
            vmem((4 * n, 9 * KB), bf16),
            vmem((9 * KB, 2 * NB), bf16),
            vmem((4 * n, 2 * NB), bf16),
            vmem((2, 4 * n, C_OUT), f32),
            vmem((4 * n, 2 * C_OUT), f32),
            vmem((nd, nb, piece, wide), f32),
            vmem((nd, nc, piece, wide), f32),
            vmem((nd, nc, piece, wide), bf16),
            vmem((nd, nc, piece, wide), bf16),
            vmem((nd, piece, wide), bf16),
            vmem((nd, piece, wide), bf16),
            vmem((piece, wide), f32),
            vmem((nb, piece, wide), f32),
            dma((BS, nb)), dma((BS, nb)), dma((nb,)), dma((nb,)),
            dma((nd,)), dma((nd,)), dma((nd,)), dma((nd,)), dma((6,)), dma, dma,
            dma((nd,)), dma((nd,)), dma((nd, nc)), dma((nd, nc)),
            dma((nd,)), dma((nd,)), dma((nc,)), dma((nc,)), dma((nc,)), dma((nc,)),
        ],
        compiler_params=pltpu.CompilerParams(
            collective_id=2, has_side_effects=True, vmem_limit_bytes=FUSED_LIMIT),
        name="fused",
    )(records.reshape(records.shape[1:]), positions.reshape(nb, cap), weight.T,
      cotangent.reshape(cotangent.shape[1:]))
    return act.astype(bf16).reshape(cotangent.shape), grad


def body(nb, nd, records, positions, weight, cotangent):
    path = staged if records.shape[2] % 16 else fused
    return path(nb, nd, records, positions, weight, cotangent)


def solution(mesh):
    placed = (
        P(("dp", "brick"), None, None, None),
        P(("dp", "brick"), None, None),
        P("dp", None),
        P("dp", "brick", None, None),
    )
    return jax.shard_map(
        functools.partial(body, mesh.shape["brick"], mesh.shape["dp"]),
        mesh=mesh,
        in_specs=placed,
        out_specs=(P("dp", "brick", None, None), P("dp", None)),
        check_vma=False,
    )
```

```python
import functools

import jax
import jax.numpy as jnp
from jax import lax
from jax.experimental import pallas as pl
from jax.experimental.pallas import tpu as pltpu
from jax.sharding import PartitionSpec as P

C_IN = 96
C_OUT = 192
BS = 4
BX = 2
BY = 8
BZ = 8
TAPS = 27
PLANE = BS * BS * C_IN
ROW = BS * C_IN
KB = 512
SIDE = 64
NB = 256
MESH = pl.DeviceIdType.MESH
VMEM_LIMIT = 48 * 1024 * 1024
FUSED_LIMIT = 62 * 1024 * 1024


def up(n, k):
    return -(-n // k) * k


def copy_to(src, dst, send, recv, axis, peer):
    return pltpu.make_async_remote_copy(
        src_ref=src, dst_ref=dst, send_sem=send, recv_sem=recv,
        device_id={axis: peer}, device_id_type=MESH,
    )


def exchange_kernel(nb, nd, half, rec, pos, wt, rec_out, pos_out, wt_out,
                    rs, rr, ps, pr, ws, wr, xs, xr, loc):
    me = lax.axis_index("brick")
    dp = lax.axis_index("dp")
    core = lax.rem(me, 2)
    sib = me + 1 - 2 * core
    barrier = pltpu.get_barrier_semaphore()
    for k in range(1, nb):
        pl.semaphore_signal(barrier, inc=1, device_id={"brick": lax.rem(me + k, nb)}, device_id_type=MESH)
    for k in range(1, nd):
        pl.semaphore_signal(barrier, inc=1, device_id={"dp": lax.rem(dp + k, nd)}, device_id_type=MESH)
    own = [
        pltpu.make_async_copy(rec.at[me], rec_out.at[me], loc.at[0]),
        pltpu.make_async_copy(pos.at[me], pos_out.at[me], loc.at[1]),
        pltpu.make_async_copy(wt, wt_out.at[dp], loc.at[2]),
    ]
    for c in own:
        c.start()
    pl.semaphore_wait(barrier, nb + nd - 2)
    mine = pl.ds(pl.multiple_of(core * half, 16), half)
    sent = []
    for k in range(1, nd):
        o = lax.rem(dp + k, nd)
        c = copy_to(wt.at[mine], wt_out.at[dp, mine], ws.at[k], wr.at[k], "dp", o)
        c.start()
        sent.append(c)
    for k in range(1, nb):
        o = lax.rem(me + k, nb)
        c = copy_to(pos.at[o], pos_out.at[me], ps.at[k], pr.at[k], "brick", o)
        c.start()
        sent.append(c)
        c = copy_to(rec.at[o], rec_out.at[me], rs.at[k], rr.at[k], "brick", o)
        c.start()
        sent.append(c)
    theirs = pl.ds(pl.multiple_of((1 - core) * half, 16), half)
    for k in range(1, nd):
        s = lax.rem(dp + nd - k, nd)
        copy_to(wt.at[mine], wt_out.at[s, mine], ws.at[k], wr.at[k], "dp", s).wait_recv()
        c = copy_to(wt_out.at[s, mine], wt_out.at[s, mine], xs.at[k], xr.at[k], "brick", sib)
        c.start()
        sent.append(c)
    for k in range(1, nd):
        s = lax.rem(dp + nd - k, nd)
        copy_to(wt.at[theirs], wt_out.at[s, theirs], xs.at[k], xr.at[k], "brick", sib).wait_recv()
    for k in range(1, nb):
        s = lax.rem(me + nb - k, nb)
        copy_to(pos.at[s], pos_out.at[s], ps.at[k], pr.at[k], "brick", s).wait_recv()
        copy_to(rec.at[s], rec_out.at[s], rs.at[k], rr.at[k], "brick", s).wait_recv()
    for c in sent:
        c.wait_send()
    for c in own:
        c.wait()


def exchange(rec, pos, wt, nb, nd):
    half = wt.shape[0] // 2
    dma = pltpu.SemaphoreType.DMA
    return pl.pallas_call(
        functools.partial(exchange_kernel, nb, nd, half),
        out_shape=(
            jax.ShapeDtypeStruct(rec.shape, rec.dtype),
            jax.ShapeDtypeStruct(pos.shape, pos.dtype),
            jax.ShapeDtypeStruct((nd,) + wt.shape, wt.dtype),
        ),
        in_specs=[pl.BlockSpec(memory_space=pl.ANY)] * 3,
        out_specs=(pl.BlockSpec(memory_space=pl.ANY),) * 3,
        scratch_shapes=[dma((nb,)), dma((nb,)), dma((nb,)), dma((nb,)),
                        dma((nd,)), dma((nd,)), dma((nd,)), dma((nd,)), dma((3,))],
        compiler_params=pltpu.CompilerParams(collective_id=0, has_side_effects=True),
        name="exchange",
    )(rec, pos, wt)


def place_kernel(arrived, places, filled, rim):
    n = filled.shape[0]
    slots = arrived.shape[0]
    want = lax.broadcasted_iota(jnp.int32, (n, slots), 0)
    pick = jnp.where(places[...] == want, 1.0, 0.0).astype(jnp.bfloat16)
    for x in range(BS):
        lanes = slice(x * PLANE, (x + 1) * PLANE)
        part = jnp.dot(pick, arrived[:, lanes], preferred_element_type=jnp.float32).astype(jnp.bfloat16)
        filled[:, lanes] = part
        if x == BS - 1:
            rim[...] = part[n - n // BX:]


def place(arrived, places):
    n = BX * BY * BZ
    return pl.pallas_call(
        place_kernel,
        out_shape=(
            jax.ShapeDtypeStruct((n, arrived.shape[1]), arrived.dtype),
            jax.ShapeDtypeStruct((n // BX, PLANE), arrived.dtype),
        ),
        compiler_params=pltpu.CompilerParams(vmem_limit_bytes=VMEM_LIMIT),
        name="place",
    )(arrived, places)


def shift_matrix(n, dy, dz):
    r = lax.broadcasted_iota(jnp.int32, (n, n), 0)
    c = lax.broadcasted_iota(jnp.int32, (n, n), 1)
    hit = c == r - dy * BZ - dz
    if dy:
        hit = hit & (lax.rem(r // BZ, BY) > 0)
    if dz:
        hit = hit & (lax.rem(r, BZ) > 0)
    return jnp.where(hit, 1.0, 0.0).astype(jnp.bfloat16)


def row_parts(first, count, shard):
    done = 0
    while done < count:
        d, r = divmod(first + done, shard)
        take = min(count - done, shard - r)
        yield d, r, take, done
        done += take


def layer_kernel(nd, shard, cut, piece, filled, rim, wt, cot, act, terms, cols, band, slopes):
    n = filled.shape[0]
    rows = 4 * n
    f32, bf16 = jnp.float32, jnp.bfloat16
    band[...] = jnp.zeros_like(band)
    slopes[...] = jnp.zeros_like(slopes)
    terms[...] = jnp.zeros_like(terms)
    spots = {0: ((KB - C_IN, 0), (C_IN, NB)), 1: ((0, 0), (2 * C_IN, NB)), 2: ((C_IN, 0), (3 * C_IN, NB))}
    for t in range(TAPS):
        ab, e = divmod(t, 3)
        for d, r, take, off in row_parts(t * C_IN, C_IN, shard):
            w = wt[d, r:r + take, :]
            for row, col in spots[e]:
                at = ab * KB + row + off
                band[at:at + take, col:col + C_OUT] = w
    sy = shift_matrix(n, 1, 0)
    sz = shift_matrix(n, 0, 1)
    syz = shift_matrix(n, 1, 1)

    def move(s, v):
        return jnp.dot(s, v, preferred_element_type=f32).astype(bf16)

    for x in range(-1, BS):
        if x < 0:
            last = slice((BS - 1) * PLANE, BS * PLANE)
            plane = jnp.concatenate([rim[...], filled[:n - n // BX, last]], axis=0)
        else:
            plane = filled[:, x * PLANE:(x + 1) * PLANE]
        places_x = [(ox, x + 1 - 2 * ox) for ox in range(2) if 0 <= x + 1 - 2 * ox <= 2]
        for y in range(-1, BS):
            at = (y if y >= 0 else BS - 1) * ROW
            whole = plane[:, at:at + ROW]
            tail = plane[:, at + ROW - 128:at + ROW]
            if y < 0:
                whole, tail = move(sy, whole), move(syz, tail)
            else:
                tail = move(sz, tail)
            places_y = [(oy, y + 1 - 2 * oy) for oy in range(2) if 0 <= y + 1 - 2 * oy <= 2]
            for ox, a in places_x:
                for oy, b in places_y:
                    q = slice((ox * 2 + oy) * n, (ox * 2 + oy + 1) * n)
                    k = (a * 3 + b) * KB
                    cols[q, k:k + ROW] = whole
                    cols[q, k + ROW:k + KB] = tail
    for oz in range(2):
        v = jnp.dot(cols[...], band[:, oz * NB:(oz + 1) * NB], preferred_element_type=f32)[:, :C_OUT]
        s = 1.0 / (1.0 + jnp.exp(-v))
        act[oz] = (v * s).astype(bf16)
        slope = s * (1.0 + v * (1.0 - s))
        slopes[:, oz * NB:oz * NB + C_OUT] = (cot[oz].astype(f32) * slope).astype(bf16)
    for ab in range(9):
        g = lax.dot_general(cols[:, ab * KB:(ab + 1) * KB], slopes[...], (((0,), (0,)), ((), ())),
                            preferred_element_type=f32)
        for e in range(3):
            (r0, c0), (r1, c1) = spots[e]
            tap = g[r0:r0 + C_IN, c0:c0 + C_OUT] + g[r1:r1 + C_IN, c1:c1 + C_OUT]
            for d, r, take, off in row_parts((ab * 3 + e) * C_IN, C_IN, shard):
                left = max(0, min(take, cut - r))
                for start, length, base, lane in ((off, left, r, 0), (off + left, take - left, r + left - cut, C_OUT)):
                    if length:
                        for j, rr, tk, o2 in row_parts(base, length, piece):
                            terms[j, d, rr:rr + tk, lane:lane + C_OUT] = tap[start + o2:start + o2 + tk]


def layer(filled, rim, wt, cot, nb, nd, shard, cut, piece):
    rows = cot.shape[1]
    return pl.pallas_call(
        functools.partial(layer_kernel, nd, shard, cut, piece),
        out_shape=(
            jax.ShapeDtypeStruct(cot.shape, jnp.bfloat16),
            jax.ShapeDtypeStruct((nb, nd, piece, 2 * C_OUT), jnp.float32),
        ),
        scratch_shapes=[
            pltpu.VMEM((rows, 9 * KB), jnp.bfloat16),
            pltpu.VMEM((9 * KB, 2 * NB), jnp.bfloat16),
            pltpu.VMEM((rows, 2 * NB), jnp.bfloat16),
        ],
        compiler_params=pltpu.CompilerParams(vmem_limit_bytes=VMEM_LIMIT),
        name="layer",
    )(filled, rim, wt, cot)


def sum_kernel(nb, nd, shard, cut, piece, terms, out, got, pass_on, plane_in, down, down_in, final,
               s1, r1, s2, r2, s3, r3, s4, r4):
    f32, bf16 = jnp.float32, jnp.bfloat16
    nc = nb // 2
    me = lax.axis_index("brick")
    dp = lax.axis_index("dp")
    core = lax.rem(me, 2)
    chip = me // 2
    sib = me + 1 - 2 * core
    barrier = pltpu.get_barrier_semaphore()
    for k in range(1, nb):
        pl.semaphore_signal(barrier, inc=1, device_id={"brick": lax.rem(me + k, nb)}, device_id_type=MESH)
    for k in range(1, nd):
        pl.semaphore_signal(barrier, inc=1, device_id={"dp": lax.rem(dp + k, nd)}, device_id_type=MESH)
    pl.semaphore_wait(barrier, nb + nd - 2)
    sent = []
    for k in range(1, nc + 1):
        q = lax.rem(chip + k, nc)
        c = copy_to(terms.at[(1 - core) * nc + q], got.at[q], s1.at[k], r1.at[k], "brick", sib)
        c.start()
        sent.append(c)
    for k in range(1, nc):
        q = lax.rem(chip + k, nc)
        copy_to(terms.at[q], got.at[q], s1.at[k], r1.at[k], "brick", sib).wait_recv()
        pass_on[k] = (terms[core * nc + q] + got[q]).astype(bf16)
        c = copy_to(pass_on.at[k], plane_in.at[k], s2.at[k], r2.at[k], "brick", q * 2 + core)
        c.start()
        sent.append(c)
    copy_to(terms.at[chip], got.at[chip], s1.at[nc], r1.at[nc], "brick", sib).wait_recv()
    for k in range(1, nc):
        q = lax.rem(chip + nc - k, nc)
        copy_to(pass_on.at[k], plane_in.at[k], s2.at[k], r2.at[k], "brick", q * 2 + core).wait_recv()

    def plane_sum(d):
        total = terms[core * nc + chip, d] + got[chip, d]
        for k in range(1, nc):
            total = total + plane_in[k, d].astype(f32)
        return total

    for k in range(1, nd):
        o = lax.rem(dp + k, nd)
        down[k] = plane_sum(o).astype(bf16)
        c = copy_to(down.at[k], down_in.at[k], s3.at[k], r3.at[k], "dp", o)
        c.start()
        sent.append(c)
    total = plane_sum(dp)
    for k in range(1, nd):
        s = lax.rem(dp + nd - k, nd)
        copy_to(down.at[k], down_in.at[k], s3.at[k], r3.at[k], "dp", s).wait_recv()
        total = total + down_in[k].astype(f32)
    final[core * nc + chip] = total
    for k in range(1, nb):
        o = lax.rem(me + k, nb)
        slot = final.at[core * nc + chip]
        c = copy_to(slot, slot, s4.at[k], r4.at[k], "brick", o)
        c.start()
        sent.append(c)
    for k in range(1, nb):
        s = lax.rem(me + nb - k, nb)
        slot = final.at[lax.rem(s, 2) * nc + s // 2]
        copy_to(slot, slot, s4.at[k], r4.at[k], "brick", s).wait_recv()
    for j in range(nb):
        for rows, first, lane in ((cut, 0, 0), (shard - cut, cut, C_OUT)):
            take = min(piece, rows - j * piece)
            if take > 0:
                out[first + j * piece:first + j * piece + take, :] = (
                    final[j, :take, lane:lane + C_OUT])
    for c in sent:
        c.wait_send()


def sum_terms(terms, nb, nd, shard, cut, piece):
    bf16 = jnp.bfloat16
    dma = pltpu.SemaphoreType.DMA
    nc = nb // 2
    wide = 2 * C_OUT
    return pl.pallas_call(
        functools.partial(sum_kernel, nb, nd, shard, cut, piece),
        out_shape=jax.ShapeDtypeStruct((shard, C_OUT), jnp.float32),
        scratch_shapes=[
            pltpu.VMEM((nc, nd, piece, wide), jnp.float32),
            pltpu.VMEM((nc, nd, piece, wide), bf16),
            pltpu.VMEM((nc, nd, piece, wide), bf16),
            pltpu.VMEM((nd, piece, wide), bf16),
            pltpu.VMEM((nd, piece, wide), bf16),
            pltpu.VMEM((nb, piece, wide), jnp.float32),
            dma((nc + 1,)), dma((nc + 1,)), dma((nc,)), dma((nc,)),
            dma((nd,)), dma((nd,)), dma((nb,)), dma((nb,)),
        ],
        compiler_params=pltpu.CompilerParams(
            collective_id=1, has_side_effects=True, vmem_limit_bytes=VMEM_LIMIT),
        name="sum_terms",
    )(terms)


def staged(nb, nd, records, positions, weight, cotangent):
    cap = records.shape[2]
    shard = weight.shape[0]
    cut = up(-(-shard // 2), 8)
    piece = up(-(-cut // nb), 16)
    half = up(-(-shard // 2), 16)
    pos = jnp.pad(positions.reshape(nb, 1, cap), ((0, 0), (0, 7), (0, 128 - cap)))
    wt = jnp.pad(weight, ((0, 2 * half - shard), (0, 0)))
    arrived, places, full = exchange(records.reshape(records.shape[1:]), pos, wt, nb, nd)
    slots = nb * cap
    filled, edge = place(arrived.reshape(slots, -1), places[:, 0, :cap].reshape(1, slots))
    rim = lax.ppermute(edge, "brick", [(i, i + 1) for i in range(nb - 1)])
    shape7 = (BX, 2, BY, 2, BZ, 2, C_OUT)
    cot = cotangent.reshape(shape7).transpose(5, 1, 3, 0, 2, 4, 6).reshape(2, -1, C_OUT)
    act, terms = layer(filled, rim, full, cot, nb, nd, shard, cut, piece)
    act = act.reshape(2, 2, 2, BX, BY, BZ, C_OUT).transpose(3, 1, 4, 2, 5, 0, 6)
    return act.reshape(cotangent.shape), sum_terms(terms, nb, nd, shard, cut, piece)


def fused_kernel(nb, nd, cap, shard, main, piece, rec, pos_in, wt_in, cot_in, act_hbm, grad_out,
                 act_out, pos, wt, cot, linear, stage, spread, arrived, wts, turned_wts, filled, rim, cols, band, slopes, cots, acts,
                 terms, got, pass_on, plane_in, down, down_in, own, final,
                 rs, rr, ps, pr, ws, wr, xs, xr, loc, bs, br, s1, r1, s2, r2, s3, r3, s4, r4, s5, r5):
    f32, bf16 = jnp.float32, jnp.bfloat16
    n = BX * BY * BZ
    nc = nb // 2
    me = lax.axis_index("brick")
    dp = lax.axis_index("dp")
    core = lax.rem(me, 2)
    chip = me // 2
    sib = me + 1 - 2 * core
    barrier = pltpu.get_barrier_semaphore()
    for k in range(1, nb):
        pl.semaphore_signal(barrier, inc=1, device_id={"brick": lax.rem(me + k, nb)}, device_id_type=MESH)
    for k in range(1, nd):
        pl.semaphore_signal(barrier, inc=1, device_id={"dp": lax.rem(dp + k, nd)}, device_id_type=MESH)
    local = [
        pltpu.make_async_copy(rec.at[me], arrived.at[me], loc.at[0]),
        pltpu.make_async_copy(wt_in, wts.at[dp], loc.at[1]),
        pltpu.make_async_copy(cot_in, cot, loc.at[2]),
        pltpu.make_async_copy(wt_in, wt, loc.at[3]),
        pltpu.make_async_copy(pos_in, pos, loc.at[4]),
    ]
    for c in reversed(local):
        c.start()
    local[4].wait()
    lane = lax.broadcasted_iota(jnp.int32, (cap, nb * cap), 1)
    slot = lax.broadcasted_iota(jnp.int32, (cap, nb * cap), 0)
    to_lanes = jnp.where(lane == slot + me * cap, 1.0, 0.0).astype(bf16)
    lined = jnp.dot(pos[...].astype(f32).astype(bf16), to_lanes, preferred_element_type=f32)
    for o in range(nb):
        stage[o] = jnp.broadcast_to(lined[o:o + 1], stage.shape[1:])
    pl.semaphore_wait(barrier, nb + nd - 2)
    local[3].wait()
    half = wt.shape[0] // 2
    mine = pl.ds(pl.multiple_of(core * half, 16), half)
    theirs = pl.ds(pl.multiple_of((1 - core) * half, 16), half)
    sent = []

    def go(c):
        c.start()
        sent.append(c)

    for k in range(1, nd):
        o = lax.rem(dp + k, nd)
        go(copy_to(wt.at[mine], wts.at[dp, mine], ws.at[k], wr.at[k], "dp", o))
    for k in range(1, nb):
        o = lax.rem(me + k, nb)
        go(copy_to(stage.at[o], spread.at[me], ps.at[k], pr.at[k], "brick", o))
    order = (3, 1, 0, 2)

    def plane_of(x):
        return pl.ds(x * PLANE, PLANE)

    for x in order:
        for k in range(1, nb):
            o = lax.rem(me + k, nb)
            go(copy_to(rec.at[o, :, plane_of(x)], arrived.at[me, :, plane_of(x)],
                       rs.at[x, k], rr.at[x, k], "brick", o))
    band[...] = jnp.zeros_like(band)
    slopes[...] = jnp.zeros_like(slopes)
    terms[...] = jnp.zeros_like(terms)
    rows = 4 * n
    strip = 4 * BX * BY
    pair = 2 * C_OUT

    def home(r):
        bz, i, j = r // strip, lax.rem(r // (2 * BY), 2 * BX), lax.rem(r, 2 * BY)
        q = lax.rem(i, 2) * 2 + lax.rem(j, 2)
        return q * n + (i // 2) * (BY * BZ) + (j // 2) * BZ + bz

    r_id = lax.broadcasted_iota(jnp.int32, (rows, rows), 0)
    c_id = lax.broadcasted_iota(jnp.int32, (rows, rows), 1)
    turn = jnp.where(r_id == home(c_id), 1.0, 0.0).astype(bf16)
    local[2].wait()
    lined_cot = jnp.concatenate(
        [cot[:, :, z * pair:(z + 1) * pair].reshape(strip, pair) for z in range(BZ)], axis=0)
    turned = jnp.dot(turn, lined_cot, preferred_element_type=f32)
    cots[0] = turned[:, :C_OUT]
    cots[1] = turned[:, C_OUT:]
    sy = shift_matrix(n, 1, 0)
    sz = shift_matrix(n, 0, 1)
    syz = shift_matrix(n, 1, 1)
    for k in range(1, nb):
        s = lax.rem(me + nb - k, nb)
        copy_to(stage.at[s], spread.at[s], ps.at[k], pr.at[k], "brick", s).wait_recv()
    spread[me] = stage[me]
    local[0].wait()
    held = spread[0]
    for s in range(1, nb):
        held = held + spread[s]
    want = lax.broadcasted_iota(jnp.int32, (n, nb * cap), 0).astype(f32)
    pick = jnp.where(held[0:1] == want, 1.0, 0.0).astype(bf16)

    def place_plane(x):
        lanes = slice(x * PLANE, (x + 1) * PLANE)
        for k in range(1, nb):
            s = lax.rem(me + nb - k, nb)
            copy_to(rec.at[s, :, plane_of(x)], arrived.at[s, :, plane_of(x)],
                    rs.at[x, k], rr.at[x, k], "brick", s).wait_recv()
        records = arrived[:, :, lanes].reshape(nb * cap, PLANE)
        filled[:, lanes] = jnp.dot(pick, records, preferred_element_type=f32).astype(bf16)

    last = slice((BS - 1) * PLANE, BS * PLANE)
    edge = copy_to(filled.at[n - n // BX:n, last], rim, bs, br, "brick", lax.rem(me + 1, nb))

    def move(s, v):
        return jnp.dot(s, v, preferred_element_type=f32).astype(bf16)

    def fill_columns(x, plane):
        for y in range(-1, BS):
            at = (y if y >= 0 else BS - 1) * ROW
            whole = plane[:, at:at + ROW]
            tail = plane[:, at + ROW - 128:at + ROW]
            if y < 0:
                whole, tail = move(sy, whole), move(syz, tail)
            else:
                tail = move(sz, tail)
            for ox in range(2):
                a = x + 1 - 2 * ox
                for oy in range(2):
                    b = y + 1 - 2 * oy
                    if 0 <= a <= 2 and 0 <= b <= 2:
                        q = slice((ox * 2 + oy) * n, (ox * 2 + oy + 1) * n)
                        k = (a * 3 + b) * KB
                        cols[q, k:k + ROW] = whole
                        cols[q, k + ROW:k + KB] = tail

    def forward(ox, a, first=False):
        q = slice(ox * 2 * n, (ox + 1) * 2 * n)
        k = slice(a * 3 * KB, (a + 1) * 3 * KB)
        part = jnp.dot(cols[q, k], band[k, :], preferred_element_type=f32)
        linear[q, :] = part if first else linear[q, :] + part

    def activate(ox):
        q = slice(ox * 2 * n, (ox + 1) * 2 * n)
        for oz in range(2):
            v = linear[q, oz * NB:oz * NB + C_OUT]
            s = 1.0 / (1.0 + jnp.exp(-v))
            acts[q, oz * C_OUT:(oz + 1) * C_OUT] = v * s
            slope = s * (1.0 + v * (1.0 - s))
            slopes[q, oz * NB:oz * NB + C_OUT] = (cots[oz, q, :] * slope).astype(bf16)

    def take_plane(x):
        place_plane(x)
        if x == BS - 1:
            pl.when(me < nb - 1)(edge.start)
        fill_columns(x, filled[:, x * PLANE:(x + 1) * PLANE])

    def turn_weights(d):
        turned_wts[d] = wts[d].astype(f32).T.astype(bf16)

    for k in range(1, nd):
        s = lax.rem(dp + nd - k, nd)
        copy_to(wt.at[mine], wts.at[s, mine], ws.at[k], wr.at[k], "dp", s).wait_recv()
        go(copy_to(wts.at[s, mine], wts.at[s, mine], xs.at[k], xr.at[k], "brick", sib))
    take_plane(3)
    local[1].wait()
    turn_weights(dp)
    for k in range(1, nd):
        s = lax.rem(dp + nd - k, nd)
        copy_to(wt.at[theirs], wts.at[s, theirs], xs.at[k], xr.at[k], "brick", sib).wait_recv()
        turn_weights(s)
    spots = {0: ((KB - C_IN, 0), (C_IN, NB)), 1: ((0, 0), (2 * C_IN, NB)), 2: ((C_IN, 0), (3 * C_IN, NB))}
    for d in range(nd):
        w = turned_wts[d]
        for t in range(TAPS):
            ab, e = divmod(t, 3)
            for d2, r, take, off in row_parts(t * C_IN, C_IN, shard):
                if d2 == d:
                    for row, col in spots[e]:
                        at = ab * KB + row + off
                        band[at:at + take, col:col + C_OUT] = w[r:r + take]
    take_plane(1)
    forward(1, 2, True)
    forward(0, 2, True)
    forward(1, 0)
    take_plane(0)
    forward(0, 1)

    @pl.when(me > 0)
    def _():
        edge.wait_recv()

    @pl.when(me == 0)
    def _():
        rim[...] = jnp.zeros_like(rim)

    fill_columns(-1, jnp.concatenate([rim[...], filled[:n - n // BX, last]], axis=0))
    forward(0, 0)
    activate(0)
    def put(d, r, rows, first):
        count = rows.shape[0]
        head = max(0, min(count, main - r))
        spans = [(0, head, r, 0, 0, C_OUT)] if head else []
        if head < count:
            for m in range(C_OUT // SIDE):
                spans.append((head, count, r + head - main + m * (shard - main), C_OUT, m * SIDE, SIDE))
        for lo, hi, base, at, col, width in spans:
            for j, row, tk, off in row_parts(base, hi - lo, piece):
                part = rows[lo + off:lo + off + tk, col:col + width]
                if not first:
                    part = part + terms[d, j, row:row + tk, at:at + width]
                terms[d, j, row:row + tk, at:at + width] = part

    def tap_rows(ab, ox, first):
        q = slice(ox * 2 * n, (ox + 1) * 2 * n)
        g = lax.dot_general(cols[q, ab * KB:(ab + 1) * KB], slopes[q, :], (((0,), (0,)), ((), ())),
                            preferred_element_type=f32)
        for e in range(3):
            (r0, c0), (r1, c1) = spots[e]
            tap = g[r0:r0 + C_IN, c0:c0 + C_OUT] + g[r1:r1 + C_IN, c1:c1 + C_OUT]
            for d, r, take, off in row_parts((ab * 3 + e) * C_IN, C_IN, shard):
                put(d, r, tap[off:off + take], first)

    for ab in range(9):
        tap_rows(ab, 0, True)
    take_plane(2)
    forward(1, 1)
    activate(1)

    def to_sibling(d):
        return copy_to(terms.at[d, pl.ds((1 - core) * nc, nc)], got.at[d], s1.at[d], r1.at[d], "brick", sib)

    def to_chips(d):
        to_sibling(d).wait_recv()
        for k in range(1, nc):
            q = lax.rem(chip + k, nc)
            pass_on[d, k] = (terms[d, core * nc + q] + got[d, q]).astype(bf16)
            go(copy_to(pass_on.at[d, k], plane_in.at[d, k], s2.at[d, k], r2.at[d, k], "brick", q * 2 + core))

    half_rows = [pl.ds(h * (piece // 2), piece // 2) for h in range(2)]

    def to_dp(d, h, peer):
        return copy_to(down.at[d, half_rows[h]], down_in.at[dp, half_rows[h]], s3.at[d, h], r3.at[dp, h], "dp", peer)

    def from_dp(k, h):
        s = lax.rem(dp + nd - k, nd)
        copy_to(down.at[s, half_rows[h]], down_in.at[s, half_rows[h]], s3.at[s, h], r3.at[s, h], "dp", s).wait_recv()
        return down_in[s, half_rows[h], :].astype(f32)

    def to_rank(d):
        total = terms[d, core * nc + chip] + got[d, chip]
        for k in range(1, nc):
            q = lax.rem(chip + nc - k, nc)
            copy_to(pass_on.at[d, k], plane_in.at[d, k], s2.at[d, k], r2.at[d, k], "brick", q * 2 + core).wait_recv()
            total = total + plane_in[d, k].astype(f32)

        @pl.when(dp == d)
        def _():
            own[...] = total

        @pl.when(dp != d)
        def _():
            down[d] = total.astype(bf16)
            for h in range(2):
                to_dp(d, h, d).start()

    ready = 0
    for ab in range(9):
        tap_rows(ab, 1, False)
        while ready < nd and (ready + 1) * shard <= (ab + 1) * 3 * C_IN:
            go(to_sibling(ready))
            if ready:
                to_chips(ready - 1)
            ready += 1
    to_chips(nd - 1)
    shown = lax.dot_general(turn, acts[...].astype(bf16), (((0,), (0,)), ((), ())), preferred_element_type=f32)
    for z in range(BZ):
        act_out[:, :, z * pair:(z + 1) * pair] = (
            shown[z * strip:(z + 1) * strip].reshape(2 * BX, 2 * BY, pair))
    stored = pltpu.make_async_copy(act_out, act_hbm, loc.at[5])
    stored.start()
    for d in range(nd):
        to_rank(d)
    here = core * nc + chip
    for h in range(2):
        part = half_rows[h]
        total = own[part, :]
        for k in range(1, nd):
            total = total + from_dp(k, h)
        final[here, part, :] = total
        slot = final.at[here, part]
        for k in range(1, nc):
            q = lax.rem(chip + k, nc)
            go(copy_to(slot, slot, s4.at[h, k], r4.at[h, k], "brick", q * 2 + core))
        go(copy_to(slot, slot, s5.at[h, 0], r5.at[h, 0], "brick", sib))
    for h in range(2):
        for k in range(1, nc):
            q = lax.rem(chip + nc - k, nc)
            there = final.at[core * nc + q, half_rows[h]]
            copy_to(there, there, s4.at[h, k], r4.at[h, k], "brick", q * 2 + core).wait_recv()
            go(copy_to(there, there, s5.at[h, k], r5.at[h, k], "brick", sib))
    for h in range(2):
        for k in range(nc):
            q = lax.rem(chip + nc - k, nc)
            there = final.at[(1 - core) * nc + q, half_rows[h]]
            copy_to(there, there, s5.at[h, k], r5.at[h, k], "brick", sib).wait_recv()
    for j in range(nb):
        grad_out[j * piece:(j + 1) * piece, :] = final[j, :, :C_OUT]
    for m in range(C_OUT // SIDE):
        for j, row, tk, off in row_parts(m * (shard - main), shard - main, piece):
            grad_out[main + off:main + off + tk, m * SIDE:(m + 1) * SIDE] = final[j, row:row + tk, C_OUT:]
    stored.wait()
    for c in sent:
        c.wait_send()
    pl.when(me < nb - 1)(edge.wait_send)
    for d in range(nd):
        @pl.when(dp != d)
        def _():
            for h in range(2):
                to_dp(d, h, d).wait_send()


def fused(nb, nd, records, positions, weight, cotangent):
    cap = records.shape[2]
    shard = weight.shape[0]
    main = up(-(-shard * C_OUT // (C_OUT + SIDE)), nb * 16)
    piece = main // nb
    f32, bf16 = jnp.float32, jnp.bfloat16
    n = BX * BY * BZ
    nc = nb // 2
    wide = C_OUT + SIDE
    dma = pltpu.SemaphoreType.DMA
    vmem = pltpu.VMEM
    act, grad = pl.pallas_call(
        functools.partial(fused_kernel, nb, nd, cap, shard, main, piece),
        out_shape=(
            jax.ShapeDtypeStruct(cotangent.shape[1:], f32),
            jax.ShapeDtypeStruct((shard, C_OUT), f32),
        ),
        in_specs=[pl.BlockSpec(memory_space=pl.ANY)] * 4,
        out_specs=(pl.BlockSpec(memory_space=pl.ANY), pl.BlockSpec(memory_space=pltpu.VMEM)),
        scratch_shapes=[
            vmem(cotangent.shape[1:], f32),
            vmem((nb, cap), jnp.int32),
            vmem((C_OUT, shard), bf16),
            vmem(cotangent.shape[1:], bf16),
            vmem((4 * n, 2 * NB), f32),
            vmem((nb, 8, nb * cap), f32),
            vmem((nb, 8, nb * cap), f32),
            vmem(records.shape[1:], bf16),
            vmem((nd, C_OUT, shard), bf16),
            vmem((nd, shard, C_OUT), bf16),
            vmem((n, BS * PLANE), bf16),
            vmem((n // BX, PLANE), bf16),
            vmem((4 * n, 9 * KB), bf16),
            vmem((9 * KB, 2 * NB), bf16),
            vmem((4 * n, 2 * NB), bf16),
            vmem((2, 4 * n, C_OUT), f32),
            vmem((4 * n, 2 * C_OUT), f32),
            vmem((nd, nb, piece, wide), f32),
            vmem((nd, nc, piece, wide), f32),
            vmem((nd, nc, piece, wide), bf16),
            vmem((nd, nc, piece, wide), bf16),
            vmem((nd, piece, wide), bf16),
            vmem((nd, piece, wide), bf16),
            vmem((piece, wide), f32),
            vmem((nb, piece, wide), f32),
            dma((BS, nb)), dma((BS, nb)), dma((nb,)), dma((nb,)),
            dma((nd,)), dma((nd,)), dma((nd,)), dma((nd,)), dma((6,)), dma, dma,
            dma((nd,)), dma((nd,)), dma((nd, nc)), dma((nd, nc)),
            dma((nd, 2)), dma((nd, 2)), dma((2, nc)), dma((2, nc)), dma((2, nc)), dma((2, nc)),
        ],
        compiler_params=pltpu.CompilerParams(
            collective_id=2, has_side_effects=True, vmem_limit_bytes=FUSED_LIMIT),
        name="fused",
    )(records.reshape(records.shape[1:]), positions.reshape(nb, cap), weight.T,
      cotangent.reshape(cotangent.shape[1:]))
    return act.astype(bf16).reshape(cotangent.shape), grad


def body(nb, nd, records, positions, weight, cotangent):
    path = staged if records.shape[2] % 16 else fused
    return path(nb, nd, records, positions, weight, cotangent)


def solution(mesh):
    placed = (
        P(("dp", "brick"), None, None, None),
        P(("dp", "brick"), None, None),
        P("dp", None),
        P("dp", "brick", None, None),
    )
    return jax.shard_map(
        functools.partial(body, mesh.shape["brick"], mesh.shape["dp"]),
        mesh=mesh,
        in_specs=placed,
        out_specs=(P("dp", "brick", None, None), P("dp", None)),
        check_vma=False,
    )
```

```python
import functools

import jax
import jax.numpy as jnp
from jax import lax
from jax.experimental import pallas as pl
from jax.experimental.pallas import tpu as pltpu
from jax.sharding import PartitionSpec as P

C_IN = 96
C_OUT = 192
BS = 4
BX = 2
BY = 8
BZ = 8
TAPS = 27
PLANE = BS * BS * C_IN
ROW = BS * C_IN
KB = 512
SIDE = 64
NB = 256
MESH = pl.DeviceIdType.MESH
VMEM_LIMIT = 48 * 1024 * 1024
FUSED_LIMIT = 62 * 1024 * 1024


def up(n, k):
    return -(-n // k) * k


def copy_to(src, dst, send, recv, axis, peer):
    return pltpu.make_async_remote_copy(
        src_ref=src, dst_ref=dst, send_sem=send, recv_sem=recv,
        device_id={axis: peer}, device_id_type=MESH,
    )


def exchange_kernel(nb, nd, half, rec, pos, wt, rec_out, pos_out, wt_out,
                    rs, rr, ps, pr, ws, wr, xs, xr, loc):
    me = lax.axis_index("brick")
    dp = lax.axis_index("dp")
    core = lax.rem(me, 2)
    sib = me + 1 - 2 * core
    barrier = pltpu.get_barrier_semaphore()
    for k in range(1, nb):
        pl.semaphore_signal(barrier, inc=1, device_id={"brick": lax.rem(me + k, nb)}, device_id_type=MESH)
    for k in range(1, nd):
        pl.semaphore_signal(barrier, inc=1, device_id={"dp": lax.rem(dp + k, nd)}, device_id_type=MESH)
    own = [
        pltpu.make_async_copy(rec.at[me], rec_out.at[me], loc.at[0]),
        pltpu.make_async_copy(pos.at[me], pos_out.at[me], loc.at[1]),
        pltpu.make_async_copy(wt, wt_out.at[dp], loc.at[2]),
    ]
    for c in own:
        c.start()
    pl.semaphore_wait(barrier, nb + nd - 2)
    mine = pl.ds(pl.multiple_of(core * half, 16), half)
    sent = []
    for k in range(1, nd):
        o = lax.rem(dp + k, nd)
        c = copy_to(wt.at[mine], wt_out.at[dp, mine], ws.at[k], wr.at[k], "dp", o)
        c.start()
        sent.append(c)
    for k in range(1, nb):
        o = lax.rem(me + k, nb)
        c = copy_to(pos.at[o], pos_out.at[me], ps.at[k], pr.at[k], "brick", o)
        c.start()
        sent.append(c)
        c = copy_to(rec.at[o], rec_out.at[me], rs.at[k], rr.at[k], "brick", o)
        c.start()
        sent.append(c)
    theirs = pl.ds(pl.multiple_of((1 - core) * half, 16), half)
    for k in range(1, nd):
        s = lax.rem(dp + nd - k, nd)
        copy_to(wt.at[mine], wt_out.at[s, mine], ws.at[k], wr.at[k], "dp", s).wait_recv()
        c = copy_to(wt_out.at[s, mine], wt_out.at[s, mine], xs.at[k], xr.at[k], "brick", sib)
        c.start()
        sent.append(c)
    for k in range(1, nd):
        s = lax.rem(dp + nd - k, nd)
        copy_to(wt.at[theirs], wt_out.at[s, theirs], xs.at[k], xr.at[k], "brick", sib).wait_recv()
    for k in range(1, nb):
        s = lax.rem(me + nb - k, nb)
        copy_to(pos.at[s], pos_out.at[s], ps.at[k], pr.at[k], "brick", s).wait_recv()
        copy_to(rec.at[s], rec_out.at[s], rs.at[k], rr.at[k], "brick", s).wait_recv()
    for c in sent:
        c.wait_send()
    for c in own:
        c.wait()


def exchange(rec, pos, wt, nb, nd):
    half = wt.shape[0] // 2
    dma = pltpu.SemaphoreType.DMA
    return pl.pallas_call(
        functools.partial(exchange_kernel, nb, nd, half),
        out_shape=(
            jax.ShapeDtypeStruct(rec.shape, rec.dtype),
            jax.ShapeDtypeStruct(pos.shape, pos.dtype),
            jax.ShapeDtypeStruct((nd,) + wt.shape, wt.dtype),
        ),
        in_specs=[pl.BlockSpec(memory_space=pl.ANY)] * 3,
        out_specs=(pl.BlockSpec(memory_space=pl.ANY),) * 3,
        scratch_shapes=[dma((nb,)), dma((nb,)), dma((nb,)), dma((nb,)),
                        dma((nd,)), dma((nd,)), dma((nd,)), dma((nd,)), dma((3,))],
        compiler_params=pltpu.CompilerParams(collective_id=0, has_side_effects=True),
        name="exchange",
    )(rec, pos, wt)


def place_kernel(arrived, places, filled, rim):
    n = filled.shape[0]
    slots = arrived.shape[0]
    want = lax.broadcasted_iota(jnp.int32, (n, slots), 0)
    pick = jnp.where(places[...] == want, 1.0, 0.0).astype(jnp.bfloat16)
    for x in range(BS):
        lanes = slice(x * PLANE, (x + 1) * PLANE)
        part = jnp.dot(pick, arrived[:, lanes], preferred_element_type=jnp.float32).astype(jnp.bfloat16)
        filled[:, lanes] = part
        if x == BS - 1:
            rim[...] = part[n - n // BX:]


def place(arrived, places):
    n = BX * BY * BZ
    return pl.pallas_call(
        place_kernel,
        out_shape=(
            jax.ShapeDtypeStruct((n, arrived.shape[1]), arrived.dtype),
            jax.ShapeDtypeStruct((n // BX, PLANE), arrived.dtype),
        ),
        compiler_params=pltpu.CompilerParams(vmem_limit_bytes=VMEM_LIMIT),
        name="place",
    )(arrived, places)


def shift_matrix(n, dy, dz):
    r = lax.broadcasted_iota(jnp.int32, (n, n), 0)
    c = lax.broadcasted_iota(jnp.int32, (n, n), 1)
    hit = c == r - dy * BZ - dz
    if dy:
        hit = hit & (lax.rem(r // BZ, BY) > 0)
    if dz:
        hit = hit & (lax.rem(r, BZ) > 0)
    return jnp.where(hit, 1.0, 0.0).astype(jnp.bfloat16)


def row_parts(first, count, shard):
    done = 0
    while done < count:
        d, r = divmod(first + done, shard)
        take = min(count - done, shard - r)
        yield d, r, take, done
        done += take


def layer_kernel(nd, shard, cut, piece, filled, rim, wt, cot, act, terms, cols, band, slopes):
    n = filled.shape[0]
    rows = 4 * n
    f32, bf16 = jnp.float32, jnp.bfloat16
    band[...] = jnp.zeros_like(band)
    slopes[...] = jnp.zeros_like(slopes)
    terms[...] = jnp.zeros_like(terms)
    spots = {0: ((KB - C_IN, 0), (C_IN, NB)), 1: ((0, 0), (2 * C_IN, NB)), 2: ((C_IN, 0), (3 * C_IN, NB))}
    for t in range(TAPS):
        ab, e = divmod(t, 3)
        for d, r, take, off in row_parts(t * C_IN, C_IN, shard):
            w = wt[d, r:r + take, :]
            for row, col in spots[e]:
                at = ab * KB + row + off
                band[at:at + take, col:col + C_OUT] = w
    sy = shift_matrix(n, 1, 0)
    sz = shift_matrix(n, 0, 1)
    syz = shift_matrix(n, 1, 1)

    def move(s, v):
        return jnp.dot(s, v, preferred_element_type=f32).astype(bf16)

    for x in range(-1, BS):
        if x < 0:
            last = slice((BS - 1) * PLANE, BS * PLANE)
            plane = jnp.concatenate([rim[...], filled[:n - n // BX, last]], axis=0)
        else:
            plane = filled[:, x * PLANE:(x + 1) * PLANE]
        places_x = [(ox, x + 1 - 2 * ox) for ox in range(2) if 0 <= x + 1 - 2 * ox <= 2]
        for y in range(-1, BS):
            at = (y if y >= 0 else BS - 1) * ROW
            whole = plane[:, at:at + ROW]
            tail = plane[:, at + ROW - 128:at + ROW]
            if y < 0:
                whole, tail = move(sy, whole), move(syz, tail)
            else:
                tail = move(sz, tail)
            places_y = [(oy, y + 1 - 2 * oy) for oy in range(2) if 0 <= y + 1 - 2 * oy <= 2]
            for ox, a in places_x:
                for oy, b in places_y:
                    q = slice((ox * 2 + oy) * n, (ox * 2 + oy + 1) * n)
                    k = (a * 3 + b) * KB
                    cols[q, k:k + ROW] = whole
                    cols[q, k + ROW:k + KB] = tail
    for oz in range(2):
        v = jnp.dot(cols[...], band[:, oz * NB:(oz + 1) * NB], preferred_element_type=f32)[:, :C_OUT]
        s = 1.0 / (1.0 + jnp.exp(-v))
        act[oz] = (v * s).astype(bf16)
        slope = s * (1.0 + v * (1.0 - s))
        slopes[:, oz * NB:oz * NB + C_OUT] = (cot[oz].astype(f32) * slope).astype(bf16)
    for ab in range(9):
        g = lax.dot_general(cols[:, ab * KB:(ab + 1) * KB], slopes[...], (((0,), (0,)), ((), ())),
                            preferred_element_type=f32)
        for e in range(3):
            (r0, c0), (r1, c1) = spots[e]
            tap = g[r0:r0 + C_IN, c0:c0 + C_OUT] + g[r1:r1 + C_IN, c1:c1 + C_OUT]
            for d, r, take, off in row_parts((ab * 3 + e) * C_IN, C_IN, shard):
                left = max(0, min(take, cut - r))
                for start, length, base, lane in ((off, left, r, 0), (off + left, take - left, r + left - cut, C_OUT)):
                    if length:
                        for j, rr, tk, o2 in row_parts(base, length, piece):
                            terms[j, d, rr:rr + tk, lane:lane + C_OUT] = tap[start + o2:start + o2 + tk]


def layer(filled, rim, wt, cot, nb, nd, shard, cut, piece):
    rows = cot.shape[1]
    return pl.pallas_call(
        functools.partial(layer_kernel, nd, shard, cut, piece),
        out_shape=(
            jax.ShapeDtypeStruct(cot.shape, jnp.bfloat16),
            jax.ShapeDtypeStruct((nb, nd, piece, 2 * C_OUT), jnp.float32),
        ),
        scratch_shapes=[
            pltpu.VMEM((rows, 9 * KB), jnp.bfloat16),
            pltpu.VMEM((9 * KB, 2 * NB), jnp.bfloat16),
            pltpu.VMEM((rows, 2 * NB), jnp.bfloat16),
        ],
        compiler_params=pltpu.CompilerParams(vmem_limit_bytes=VMEM_LIMIT),
        name="layer",
    )(filled, rim, wt, cot)


def sum_kernel(nb, nd, shard, cut, piece, terms, out, got, pass_on, plane_in, down, down_in, final,
               s1, r1, s2, r2, s3, r3, s4, r4):
    f32, bf16 = jnp.float32, jnp.bfloat16
    nc = nb // 2
    me = lax.axis_index("brick")
    dp = lax.axis_index("dp")
    core = lax.rem(me, 2)
    chip = me // 2
    sib = me + 1 - 2 * core
    barrier = pltpu.get_barrier_semaphore()
    for k in range(1, nb):
        pl.semaphore_signal(barrier, inc=1, device_id={"brick": lax.rem(me + k, nb)}, device_id_type=MESH)
    for k in range(1, nd):
        pl.semaphore_signal(barrier, inc=1, device_id={"dp": lax.rem(dp + k, nd)}, device_id_type=MESH)
    pl.semaphore_wait(barrier, nb + nd - 2)
    sent = []
    for k in range(1, nc + 1):
        q = lax.rem(chip + k, nc)
        c = copy_to(terms.at[(1 - core) * nc + q], got.at[q], s1.at[k], r1.at[k], "brick", sib)
        c.start()
        sent.append(c)
    for k in range(1, nc):
        q = lax.rem(chip + k, nc)
        copy_to(terms.at[q], got.at[q], s1.at[k], r1.at[k], "brick", sib).wait_recv()
        pass_on[k] = (terms[core * nc + q] + got[q]).astype(bf16)
        c = copy_to(pass_on.at[k], plane_in.at[k], s2.at[k], r2.at[k], "brick", q * 2 + core)
        c.start()
        sent.append(c)
    copy_to(terms.at[chip], got.at[chip], s1.at[nc], r1.at[nc], "brick", sib).wait_recv()
    for k in range(1, nc):
        q = lax.rem(chip + nc - k, nc)
        copy_to(pass_on.at[k], plane_in.at[k], s2.at[k], r2.at[k], "brick", q * 2 + core).wait_recv()

    def plane_sum(d):
        total = terms[core * nc + chip, d] + got[chip, d]
        for k in range(1, nc):
            total = total + plane_in[k, d].astype(f32)
        return total

    for k in range(1, nd):
        o = lax.rem(dp + k, nd)
        down[k] = plane_sum(o).astype(bf16)
        c = copy_to(down.at[k], down_in.at[k], s3.at[k], r3.at[k], "dp", o)
        c.start()
        sent.append(c)
    total = plane_sum(dp)
    for k in range(1, nd):
        s = lax.rem(dp + nd - k, nd)
        copy_to(down.at[k], down_in.at[k], s3.at[k], r3.at[k], "dp", s).wait_recv()
        total = total + down_in[k].astype(f32)
    final[core * nc + chip] = total
    for k in range(1, nb):
        o = lax.rem(me + k, nb)
        slot = final.at[core * nc + chip]
        c = copy_to(slot, slot, s4.at[k], r4.at[k], "brick", o)
        c.start()
        sent.append(c)
    for k in range(1, nb):
        s = lax.rem(me + nb - k, nb)
        slot = final.at[lax.rem(s, 2) * nc + s // 2]
        copy_to(slot, slot, s4.at[k], r4.at[k], "brick", s).wait_recv()
    for j in range(nb):
        for rows, first, lane in ((cut, 0, 0), (shard - cut, cut, C_OUT)):
            take = min(piece, rows - j * piece)
            if take > 0:
                out[first + j * piece:first + j * piece + take, :] = (
                    final[j, :take, lane:lane + C_OUT])
    for c in sent:
        c.wait_send()


def sum_terms(terms, nb, nd, shard, cut, piece):
    bf16 = jnp.bfloat16
    dma = pltpu.SemaphoreType.DMA
    nc = nb // 2
    wide = 2 * C_OUT
    return pl.pallas_call(
        functools.partial(sum_kernel, nb, nd, shard, cut, piece),
        out_shape=jax.ShapeDtypeStruct((shard, C_OUT), jnp.float32),
        scratch_shapes=[
            pltpu.VMEM((nc, nd, piece, wide), jnp.float32),
            pltpu.VMEM((nc, nd, piece, wide), bf16),
            pltpu.VMEM((nc, nd, piece, wide), bf16),
            pltpu.VMEM((nd, piece, wide), bf16),
            pltpu.VMEM((nd, piece, wide), bf16),
            pltpu.VMEM((nb, piece, wide), jnp.float32),
            dma((nc + 1,)), dma((nc + 1,)), dma((nc,)), dma((nc,)),
            dma((nd,)), dma((nd,)), dma((nb,)), dma((nb,)),
        ],
        compiler_params=pltpu.CompilerParams(
            collective_id=1, has_side_effects=True, vmem_limit_bytes=VMEM_LIMIT),
        name="sum_terms",
    )(terms)


def staged(nb, nd, records, positions, weight, cotangent):
    cap = records.shape[2]
    shard = weight.shape[0]
    cut = up(-(-shard // 2), 8)
    piece = up(-(-cut // nb), 16)
    half = up(-(-shard // 2), 16)
    pos = jnp.pad(positions.reshape(nb, 1, cap), ((0, 0), (0, 7), (0, 128 - cap)))
    wt = jnp.pad(weight, ((0, 2 * half - shard), (0, 0)))
    arrived, places, full = exchange(records.reshape(records.shape[1:]), pos, wt, nb, nd)
    slots = nb * cap
    filled, edge = place(arrived.reshape(slots, -1), places[:, 0, :cap].reshape(1, slots))
    rim = lax.ppermute(edge, "brick", [(i, i + 1) for i in range(nb - 1)])
    shape7 = (BX, 2, BY, 2, BZ, 2, C_OUT)
    cot = cotangent.reshape(shape7).transpose(5, 1, 3, 0, 2, 4, 6).reshape(2, -1, C_OUT)
    act, terms = layer(filled, rim, full, cot, nb, nd, shard, cut, piece)
    act = act.reshape(2, 2, 2, BX, BY, BZ, C_OUT).transpose(3, 1, 4, 2, 5, 0, 6)
    return act.reshape(cotangent.shape), sum_terms(terms, nb, nd, shard, cut, piece)


def fused_kernel(nb, nd, cap, shard, main, piece, rec, pos_in, wt_in, cot_in, act_hbm, grad_out,
                 act_out, pos, wt, cot, linear, stage, spread, arrived, wts, tails, turned_wts, filled, rim, cols, band, slopes, cots, acts,
                 terms, got, pass_on, plane_in, down, down_in, own, final,
                 rs, rr, ps, pr, ws, wr, ts, tr, xs, xr, loc, bs, br, s1, r1, s2, r2, s3, r3, s4, r4, s5, r5):
    f32, bf16 = jnp.float32, jnp.bfloat16
    n = BX * BY * BZ
    nc = nb // 2
    me = lax.axis_index("brick")
    dp = lax.axis_index("dp")
    core = lax.rem(me, 2)
    chip = me // 2
    sib = me + 1 - 2 * core
    barrier = pltpu.get_barrier_semaphore()
    for k in range(1, nb):
        pl.semaphore_signal(barrier, inc=1, device_id={"brick": lax.rem(me + k, nb)}, device_id_type=MESH)
    for k in range(1, nd):
        pl.semaphore_signal(barrier, inc=1, device_id={"dp": lax.rem(dp + k, nd)}, device_id_type=MESH)
    local = [
        pltpu.make_async_copy(rec.at[me], arrived.at[me], loc.at[0]),
        pltpu.make_async_copy(wt_in, wts.at[dp], loc.at[1]),
        pltpu.make_async_copy(cot_in, cot, loc.at[2]),
        pltpu.make_async_copy(wt_in, wt, loc.at[3]),
        pltpu.make_async_copy(pos_in, pos, loc.at[4]),
    ]
    for c in reversed(local):
        c.start()
    local[4].wait()
    lane = lax.broadcasted_iota(jnp.int32, (cap, nb * cap), 1)
    slot = lax.broadcasted_iota(jnp.int32, (cap, nb * cap), 0)
    to_lanes = jnp.where(lane == slot + me * cap, 1.0, 0.0).astype(bf16)
    lined = jnp.dot(pos[...].astype(f32).astype(bf16), to_lanes, preferred_element_type=f32)
    for o in range(nb):
        stage[o] = jnp.broadcast_to(lined[o:o + 1], stage.shape[1:])
    pl.semaphore_wait(barrier, nb + nd - 2)
    local[3].wait()
    half = wt.shape[0] // 2
    body_lanes = shard - shard % 128
    mine = (pl.ds(pl.multiple_of(core * half, 16), half), pl.ds(0, body_lanes))
    theirs = (pl.ds(pl.multiple_of((1 - core) * half, 16), half), pl.ds(0, body_lanes))
    tail_rows = shard - body_lanes
    if tail_rows:
        tails[dp, :tail_rows, :] = wt[:, body_lanes:].astype(f32).T
    sent = []

    def go(c):
        c.start()
        sent.append(c)

    for k in range(1, nd):
        o = lax.rem(dp + k, nd)
        go(copy_to(wt.at[mine], wts.at[(dp,) + mine], ws.at[k], wr.at[k], "dp", o))
        if tail_rows:
            go(copy_to(tails.at[dp], tails.at[dp], ts.at[k], tr.at[k], "dp", o))
    for k in range(1, nb):
        o = lax.rem(me + k, nb)
        go(copy_to(stage.at[o], spread.at[me], ps.at[k], pr.at[k], "brick", o))
    order = (3, 1, 0, 2)

    def plane_of(x):
        return pl.ds(x * PLANE, PLANE)

    for x in order:
        for k in range(1, nb):
            o = lax.rem(me + k, nb)
            go(copy_to(rec.at[o, :, plane_of(x)], arrived.at[me, :, plane_of(x)],
                       rs.at[x, k], rr.at[x, k], "brick", o))
    band[...] = jnp.zeros_like(band)
    slopes[...] = jnp.zeros_like(slopes)
    terms[...] = jnp.zeros_like(terms)
    rows = 4 * n
    strip = 4 * BX * BY
    pair = 2 * C_OUT

    def home(r):
        bz, i, j = r // strip, lax.rem(r // (2 * BY), 2 * BX), lax.rem(r, 2 * BY)
        q = lax.rem(i, 2) * 2 + lax.rem(j, 2)
        return q * n + (i // 2) * (BY * BZ) + (j // 2) * BZ + bz

    r_id = lax.broadcasted_iota(jnp.int32, (rows, rows), 0)
    c_id = lax.broadcasted_iota(jnp.int32, (rows, rows), 1)
    turn = jnp.where(r_id == home(c_id), 1.0, 0.0).astype(bf16)
    local[2].wait()
    lined_cot = jnp.concatenate(
        [cot[:, :, z * pair:(z + 1) * pair].reshape(strip, pair) for z in range(BZ)], axis=0)
    turned = jnp.dot(turn, lined_cot, preferred_element_type=f32)
    cots[0] = turned[:, :C_OUT]
    cots[1] = turned[:, C_OUT:]
    sy = shift_matrix(n, 1, 0)
    sz = shift_matrix(n, 0, 1)
    syz = shift_matrix(n, 1, 1)
    for k in range(1, nb):
        s = lax.rem(me + nb - k, nb)
        copy_to(stage.at[s], spread.at[s], ps.at[k], pr.at[k], "brick", s).wait_recv()
    spread[me] = stage[me]
    local[0].wait()
    held = spread[0]
    for s in range(1, nb):
        held = held + spread[s]
    want = lax.broadcasted_iota(jnp.int32, (n, nb * cap), 0).astype(f32)
    pick = jnp.where(held[0:1] == want, 1.0, 0.0).astype(bf16)

    def place_plane(x):
        lanes = slice(x * PLANE, (x + 1) * PLANE)
        for k in range(1, nb):
            s = lax.rem(me + nb - k, nb)
            copy_to(rec.at[s, :, plane_of(x)], arrived.at[s, :, plane_of(x)],
                    rs.at[x, k], rr.at[x, k], "brick", s).wait_recv()
        records = arrived[:, :, lanes].reshape(nb * cap, PLANE)
        filled[:, lanes] = jnp.dot(pick, records, preferred_element_type=f32).astype(bf16)

    last = slice((BS - 1) * PLANE, BS * PLANE)
    edge = copy_to(filled.at[n - n // BX:n, last], rim, bs, br, "brick", lax.rem(me + 1, nb))

    def move(s, v):
        return jnp.dot(s, v, preferred_element_type=f32).astype(bf16)

    def fill_columns(x, plane):
        for y in range(-1, BS):
            at = (y if y >= 0 else BS - 1) * ROW
            whole = plane[:, at:at + ROW]
            tail = plane[:, at + ROW - 128:at + ROW]
            if y < 0:
                whole, tail = move(sy, whole), move(syz, tail)
            else:
                tail = move(sz, tail)
            for ox in range(2):
                a = x + 1 - 2 * ox
                for oy in range(2):
                    b = y + 1 - 2 * oy
                    if 0 <= a <= 2 and 0 <= b <= 2:
                        q = slice((ox * 2 + oy) * n, (ox * 2 + oy + 1) * n)
                        k = (a * 3 + b) * KB
                        cols[q, k:k + ROW] = whole
                        cols[q, k + ROW:k + KB] = tail

    def forward(ox, a, first=False):
        q = slice(ox * 2 * n, (ox + 1) * 2 * n)
        k = slice(a * 3 * KB, (a + 1) * 3 * KB)
        part = jnp.dot(cols[q, k], band[k, :], preferred_element_type=f32)
        linear[q, :] = part if first else linear[q, :] + part

    def activate(ox):
        q = slice(ox * 2 * n, (ox + 1) * 2 * n)
        for oz in range(2):
            v = linear[q, oz * NB:oz * NB + C_OUT]
            s = 1.0 / (1.0 + jnp.exp(-v))
            acts[q, oz * C_OUT:(oz + 1) * C_OUT] = v * s
            slope = s * (1.0 + v * (1.0 - s))
            slopes[q, oz * NB:oz * NB + C_OUT] = (cots[oz, q, :] * slope).astype(bf16)

    def take_plane(x):
        place_plane(x)
        if x == BS - 1:
            pl.when(me < nb - 1)(edge.start)
        fill_columns(x, filled[:, x * PLANE:(x + 1) * PLANE])

    def turn_weights(d):
        turned_wts[d, :body_lanes, :] = wts[d, :, :body_lanes].astype(f32).T.astype(bf16)
        if tail_rows:
            turned_wts[d, body_lanes:, :] = tails[d, :tail_rows, :].astype(bf16)

    take_plane(3)
    for k in range(1, nd):
        s = lax.rem(dp + nd - k, nd)
        copy_to(wt.at[mine], wts.at[(s,) + mine], ws.at[k], wr.at[k], "dp", s).wait_recv()
        go(copy_to(wts.at[(s,) + mine], wts.at[(s,) + mine], xs.at[k], xr.at[k], "brick", sib))
    local[1].wait()
    turn_weights(dp)
    for k in range(1, nd):
        s = lax.rem(dp + nd - k, nd)
        copy_to(wt.at[theirs], wts.at[(s,) + theirs], xs.at[k], xr.at[k], "brick", sib).wait_recv()
        if tail_rows:
            copy_to(tails.at[s], tails.at[s], ts.at[k], tr.at[k], "dp", s).wait_recv()
        turn_weights(s)
    spots = {0: ((KB - C_IN, 0), (C_IN, NB)), 1: ((0, 0), (2 * C_IN, NB)), 2: ((C_IN, 0), (3 * C_IN, NB))}
    for d in range(nd):
        w = turned_wts[d]
        for t in range(TAPS):
            ab, e = divmod(t, 3)
            for d2, r, take, off in row_parts(t * C_IN, C_IN, shard):
                if d2 == d:
                    for row, col in spots[e]:
                        at = ab * KB + row + off
                        band[at:at + take, col:col + C_OUT] = w[r:r + take]
    take_plane(1)
    forward(1, 2, True)
    forward(0, 2, True)
    forward(1, 0)
    take_plane(0)
    forward(0, 1)

    @pl.when(me > 0)
    def _():
        edge.wait_recv()

    @pl.when(me == 0)
    def _():
        rim[...] = jnp.zeros_like(rim)

    fill_columns(-1, jnp.concatenate([rim[...], filled[:n - n // BX, last]], axis=0))
    forward(0, 0)
    activate(0)
    def put(d, r, rows):
        count = rows.shape[0]
        head = max(0, min(count, main - r))
        spans = [(0, head, r, 0, 0, C_OUT)] if head else []
        if head < count:
            for m in range(C_OUT // SIDE):
                spans.append((head, count, r + head - main + m * (shard - main), C_OUT, m * SIDE, SIDE))
        for lo, hi, base, at, col, width in spans:
            for j, row, tk, off in row_parts(base, hi - lo, piece):
                part = rows[lo + off:lo + off + tk, col:col + width]
                terms[d, j, row:row + tk, at:at + width] = part

    def tap_rows(ab):
        g = lax.dot_general(cols[:, ab * KB:(ab + 1) * KB], slopes[...], (((0,), (0,)), ((), ())),
                            preferred_element_type=f32)
        for e in range(3):
            (r0, c0), (r1, c1) = spots[e]
            tap = g[r0:r0 + C_IN, c0:c0 + C_OUT] + g[r1:r1 + C_IN, c1:c1 + C_OUT]
            for d, r, take, off in row_parts((ab * 3 + e) * C_IN, C_IN, shard):
                put(d, r, tap[off:off + take])

    take_plane(2)
    forward(1, 1)
    activate(1)

    def to_sibling(d):
        return copy_to(terms.at[d, pl.ds((1 - core) * nc, nc)], got.at[d], s1.at[d], r1.at[d], "brick", sib)

    def to_chips(d):
        to_sibling(d).wait_recv()
        for k in range(1, nc):
            q = lax.rem(chip + k, nc)
            pass_on[d, k] = (terms[d, core * nc + q] + got[d, q]).astype(bf16)
            go(copy_to(pass_on.at[d, k], plane_in.at[d, k], s2.at[d, k], r2.at[d, k], "brick", q * 2 + core))

    half_rows = [pl.ds(h * (piece // 2), piece // 2) for h in range(2)]

    def to_dp(d, h, peer):
        return copy_to(down.at[d, half_rows[h]], down_in.at[dp, half_rows[h]], s3.at[d, h], r3.at[dp, h], "dp", peer)

    def from_dp(k, h):
        s = lax.rem(dp + nd - k, nd)
        copy_to(down.at[s, half_rows[h]], down_in.at[s, half_rows[h]], s3.at[s, h], r3.at[s, h], "dp", s).wait_recv()
        return down_in[s, half_rows[h], :].astype(f32)

    def to_rank(d):
        total = terms[d, core * nc + chip] + got[d, chip]
        for k in range(1, nc):
            q = lax.rem(chip + nc - k, nc)
            copy_to(pass_on.at[d, k], plane_in.at[d, k], s2.at[d, k], r2.at[d, k], "brick", q * 2 + core).wait_recv()
            total = total + plane_in[d, k].astype(f32)

        @pl.when(dp == d)
        def _():
            own[...] = total

        @pl.when(dp != d)
        def _():
            down[d] = total.astype(bf16)
            for h in range(2):
                to_dp(d, h, d).start()

    ready = 0
    for ab in range(9):
        tap_rows(ab)
        while ready < nd and (ready + 1) * shard <= (ab + 1) * 3 * C_IN:
            go(to_sibling(ready))
            if ready:
                to_chips(ready - 1)
            ready += 1
    to_chips(nd - 1)
    shown = lax.dot_general(turn, acts[...].astype(bf16), (((0,), (0,)), ((), ())), preferred_element_type=f32)
    for z in range(BZ):
        act_out[:, :, z * pair:(z + 1) * pair] = (
            shown[z * strip:(z + 1) * strip].reshape(2 * BX, 2 * BY, pair))
    stored = pltpu.make_async_copy(act_out, act_hbm, loc.at[5])
    stored.start()
    for d in range(nd):
        to_rank(d)
    here = core * nc + chip
    for h in range(2):
        part = half_rows[h]
        total = own[part, :]
        for k in range(1, nd):
            total = total + from_dp(k, h)
        final[here, part, :] = total
        slot = final.at[here, part]
        for k in range(1, nc):
            q = lax.rem(chip + k, nc)
            go(copy_to(slot, slot, s4.at[h, k], r4.at[h, k], "brick", q * 2 + core))
        go(copy_to(slot, slot, s5.at[h, 0], r5.at[h, 0], "brick", sib))
    for h in range(2):
        for k in range(1, nc):
            q = lax.rem(chip + nc - k, nc)
            there = final.at[core * nc + q, half_rows[h]]
            copy_to(there, there, s4.at[h, k], r4.at[h, k], "brick", q * 2 + core).wait_recv()
            go(copy_to(there, there, s5.at[h, k], r5.at[h, k], "brick", sib))
    for h in range(2):
        for k in range(nc):
            q = lax.rem(chip + nc - k, nc)
            there = final.at[(1 - core) * nc + q, half_rows[h]]
            copy_to(there, there, s5.at[h, k], r5.at[h, k], "brick", sib).wait_recv()
    for j in range(nb):
        grad_out[j * piece:(j + 1) * piece, :] = final[j, :, :C_OUT]
    for m in range(C_OUT // SIDE):
        for j, row, tk, off in row_parts(m * (shard - main), shard - main, piece):
            grad_out[main + off:main + off + tk, m * SIDE:(m + 1) * SIDE] = final[j, row:row + tk, C_OUT:]
    stored.wait()
    for c in sent:
        c.wait_send()
    pl.when(me < nb - 1)(edge.wait_send)
    for d in range(nd):
        @pl.when(dp != d)
        def _():
            for h in range(2):
                to_dp(d, h, d).wait_send()


def fused(nb, nd, records, positions, weight, cotangent):
    cap = records.shape[2]
    shard = weight.shape[0]
    main = up(-(-shard * C_OUT // (C_OUT + SIDE)), nb * 16)
    piece = main // nb
    f32, bf16 = jnp.float32, jnp.bfloat16
    n = BX * BY * BZ
    nc = nb // 2
    wide = C_OUT + SIDE
    dma = pltpu.SemaphoreType.DMA
    vmem = pltpu.VMEM
    act, grad = pl.pallas_call(
        functools.partial(fused_kernel, nb, nd, cap, shard, main, piece),
        out_shape=(
            jax.ShapeDtypeStruct(cotangent.shape[1:], f32),
            jax.ShapeDtypeStruct((shard, C_OUT), f32),
        ),
        in_specs=[pl.BlockSpec(memory_space=pl.ANY)] * 4,
        out_specs=(pl.BlockSpec(memory_space=pl.ANY), pl.BlockSpec(memory_space=pltpu.VMEM)),
        scratch_shapes=[
            vmem(cotangent.shape[1:], f32),
            vmem((nb, cap), jnp.int32),
            vmem((C_OUT, shard), bf16),
            vmem(cotangent.shape[1:], bf16),
            vmem((4 * n, 2 * NB), f32),
            vmem((nb, 8, nb * cap), f32),
            vmem((nb, 8, nb * cap), f32),
            vmem(records.shape[1:], bf16),
            vmem((nd, C_OUT, shard), bf16),
            vmem((nd, up(max(shard % 128, 1), 8), C_OUT), f32),
            vmem((nd, shard, C_OUT), bf16),
            vmem((n, BS * PLANE), bf16),
            vmem((n // BX, PLANE), bf16),
            vmem((4 * n, 9 * KB), bf16),
            vmem((9 * KB, 2 * NB), bf16),
            vmem((4 * n, 2 * NB), bf16),
            vmem((2, 4 * n, C_OUT), f32),
            vmem((4 * n, 2 * C_OUT), f32),
            vmem((nd, nb, piece, wide), f32),
            vmem((nd, nc, piece, wide), f32),
            vmem((nd, nc, piece, wide), bf16),
            vmem((nd, nc, piece, wide), bf16),
            vmem((nd, piece, wide), bf16),
            vmem((nd, piece, wide), bf16),
            vmem((piece, wide), f32),
            vmem((nb, piece, wide), f32),
            dma((BS, nb)), dma((BS, nb)), dma((nb,)), dma((nb,)),
            dma((nd,)), dma((nd,)), dma((nd,)), dma((nd,)), dma((nd,)), dma((nd,)), dma((6,)), dma, dma,
            dma((nd,)), dma((nd,)), dma((nd, nc)), dma((nd, nc)),
            dma((nd, 2)), dma((nd, 2)), dma((2, nc)), dma((2, nc)), dma((2, nc)), dma((2, nc)),
        ],
        compiler_params=pltpu.CompilerParams(
            collective_id=2, has_side_effects=True, vmem_limit_bytes=FUSED_LIMIT),
        name="fused",
    )(records.reshape(records.shape[1:]), positions.reshape(nb, cap), weight.T,
      cotangent.reshape(cotangent.shape[1:]))
    return act.astype(bf16).reshape(cotangent.shape), grad


def body(nb, nd, records, positions, weight, cotangent):
    path = staged if records.shape[2] % 16 else fused
    return path(nb, nd, records, positions, weight, cotangent)


def solution(mesh):
    placed = (
        P(("dp", "brick"), None, None, None),
        P(("dp", "brick"), None, None),
        P("dp", None),
        P("dp", "brick", None, None),
    )
    return jax.shard_map(
        functools.partial(body, mesh.shape["brick"], mesh.shape["dp"]),
        mesh=mesh,
        in_specs=placed,
        out_specs=(P("dp", "brick", None, None), P("dp", None)),
        check_vma=False,
    )
```

```python
import functools

import jax
import jax.numpy as jnp
from jax import lax
from jax.experimental import pallas as pl
from jax.experimental.pallas import tpu as pltpu
from jax.sharding import PartitionSpec as P

C_IN = 96
C_OUT = 192
BS = 4
BX = 2
BY = 8
BZ = 8
TAPS = 27
PLANE = BS * BS * C_IN
ROW = BS * C_IN
KB = 512
SIDE = 64
NB = 256
MESH = pl.DeviceIdType.MESH
VMEM_LIMIT = 48 * 1024 * 1024
FUSED_LIMIT = 62 * 1024 * 1024


def up(n, k):
    return -(-n // k) * k


def copy_to(src, dst, send, recv, axis, peer):
    return pltpu.make_async_remote_copy(
        src_ref=src, dst_ref=dst, send_sem=send, recv_sem=recv,
        device_id={axis: peer}, device_id_type=MESH,
    )


def exchange_kernel(nb, nd, half, rec, pos, wt, rec_out, pos_out, wt_out,
                    rs, rr, ps, pr, ws, wr, xs, xr, loc):
    me = lax.axis_index("brick")
    dp = lax.axis_index("dp")
    core = lax.rem(me, 2)
    sib = me + 1 - 2 * core
    barrier = pltpu.get_barrier_semaphore()
    for k in range(1, nb):
        pl.semaphore_signal(barrier, inc=1, device_id={"brick": lax.rem(me + k, nb)}, device_id_type=MESH)
    for k in range(1, nd):
        pl.semaphore_signal(barrier, inc=1, device_id={"dp": lax.rem(dp + k, nd)}, device_id_type=MESH)
    own = [
        pltpu.make_async_copy(rec.at[me], rec_out.at[me], loc.at[0]),
        pltpu.make_async_copy(pos.at[me], pos_out.at[me], loc.at[1]),
        pltpu.make_async_copy(wt, wt_out.at[dp], loc.at[2]),
    ]
    for c in own:
        c.start()
    pl.semaphore_wait(barrier, nb + nd - 2)
    mine = pl.ds(pl.multiple_of(core * half, 16), half)
    sent = []
    for k in range(1, nd):
        o = lax.rem(dp + k, nd)
        c = copy_to(wt.at[mine], wt_out.at[dp, mine], ws.at[k], wr.at[k], "dp", o)
        c.start()
        sent.append(c)
    for k in range(1, nb):
        o = lax.rem(me + k, nb)
        c = copy_to(pos.at[o], pos_out.at[me], ps.at[k], pr.at[k], "brick", o)
        c.start()
        sent.append(c)
        c = copy_to(rec.at[o], rec_out.at[me], rs.at[k], rr.at[k], "brick", o)
        c.start()
        sent.append(c)
    theirs = pl.ds(pl.multiple_of((1 - core) * half, 16), half)
    for k in range(1, nd):
        s = lax.rem(dp + nd - k, nd)
        copy_to(wt.at[mine], wt_out.at[s, mine], ws.at[k], wr.at[k], "dp", s).wait_recv()
        c = copy_to(wt_out.at[s, mine], wt_out.at[s, mine], xs.at[k], xr.at[k], "brick", sib)
        c.start()
        sent.append(c)
    for k in range(1, nd):
        s = lax.rem(dp + nd - k, nd)
        copy_to(wt.at[theirs], wt_out.at[s, theirs], xs.at[k], xr.at[k], "brick", sib).wait_recv()
    for k in range(1, nb):
        s = lax.rem(me + nb - k, nb)
        copy_to(pos.at[s], pos_out.at[s], ps.at[k], pr.at[k], "brick", s).wait_recv()
        copy_to(rec.at[s], rec_out.at[s], rs.at[k], rr.at[k], "brick", s).wait_recv()
    for c in sent:
        c.wait_send()
    for c in own:
        c.wait()


def exchange(rec, pos, wt, nb, nd):
    half = wt.shape[0] // 2
    dma = pltpu.SemaphoreType.DMA
    return pl.pallas_call(
        functools.partial(exchange_kernel, nb, nd, half),
        out_shape=(
            jax.ShapeDtypeStruct(rec.shape, rec.dtype),
            jax.ShapeDtypeStruct(pos.shape, pos.dtype),
            jax.ShapeDtypeStruct((nd,) + wt.shape, wt.dtype),
        ),
        in_specs=[pl.BlockSpec(memory_space=pl.ANY)] * 3,
        out_specs=(pl.BlockSpec(memory_space=pl.ANY),) * 3,
        scratch_shapes=[dma((nb,)), dma((nb,)), dma((nb,)), dma((nb,)),
                        dma((nd,)), dma((nd,)), dma((nd,)), dma((nd,)), dma((3,))],
        compiler_params=pltpu.CompilerParams(collective_id=0, has_side_effects=True),
        name="exchange",
    )(rec, pos, wt)


def place_kernel(arrived, places, filled, rim):
    n = filled.shape[0]
    slots = arrived.shape[0]
    want = lax.broadcasted_iota(jnp.int32, (n, slots), 0)
    pick = jnp.where(places[...] == want, 1.0, 0.0).astype(jnp.bfloat16)
    for x in range(BS):
        lanes = slice(x * PLANE, (x + 1) * PLANE)
        part = jnp.dot(pick, arrived[:, lanes], preferred_element_type=jnp.float32).astype(jnp.bfloat16)
        filled[:, lanes] = part
        if x == BS - 1:
            rim[...] = part[n - n // BX:]


def place(arrived, places):
    n = BX * BY * BZ
    return pl.pallas_call(
        place_kernel,
        out_shape=(
            jax.ShapeDtypeStruct((n, arrived.shape[1]), arrived.dtype),
            jax.ShapeDtypeStruct((n // BX, PLANE), arrived.dtype),
        ),
        compiler_params=pltpu.CompilerParams(vmem_limit_bytes=VMEM_LIMIT),
        name="place",
    )(arrived, places)


def shift_matrix(n, dy, dz):
    r = lax.broadcasted_iota(jnp.int32, (n, n), 0)
    c = lax.broadcasted_iota(jnp.int32, (n, n), 1)
    hit = c == r - dy * BZ - dz
    if dy:
        hit = hit & (lax.rem(r // BZ, BY) > 0)
    if dz:
        hit = hit & (lax.rem(r, BZ) > 0)
    return jnp.where(hit, 1.0, 0.0).astype(jnp.bfloat16)


def row_parts(first, count, shard):
    done = 0
    while done < count:
        d, r = divmod(first + done, shard)
        take = min(count - done, shard - r)
        yield d, r, take, done
        done += take


def layer_kernel(nd, shard, cut, piece, filled, rim, wt, cot, act, terms, cols, band, slopes):
    n = filled.shape[0]
    rows = 4 * n
    f32, bf16 = jnp.float32, jnp.bfloat16
    band[...] = jnp.zeros_like(band)
    slopes[...] = jnp.zeros_like(slopes)
    terms[...] = jnp.zeros_like(terms)
    spots = {0: ((KB - C_IN, 0), (C_IN, NB)), 1: ((0, 0), (2 * C_IN, NB)), 2: ((C_IN, 0), (3 * C_IN, NB))}
    for t in range(TAPS):
        ab, e = divmod(t, 3)
        for d, r, take, off in row_parts(t * C_IN, C_IN, shard):
            w = wt[d, r:r + take, :]
            for row, col in spots[e]:
                at = ab * KB + row + off
                band[at:at + take, col:col + C_OUT] = w
    sy = shift_matrix(n, 1, 0)
    sz = shift_matrix(n, 0, 1)
    syz = shift_matrix(n, 1, 1)

    def move(s, v):
        return jnp.dot(s, v, preferred_element_type=f32).astype(bf16)

    for x in range(-1, BS):
        if x < 0:
            last = slice((BS - 1) * PLANE, BS * PLANE)
            plane = jnp.concatenate([rim[...], filled[:n - n // BX, last]], axis=0)
        else:
            plane = filled[:, x * PLANE:(x + 1) * PLANE]
        places_x = [(ox, x + 1 - 2 * ox) for ox in range(2) if 0 <= x + 1 - 2 * ox <= 2]
        for y in range(-1, BS):
            at = (y if y >= 0 else BS - 1) * ROW
            whole = plane[:, at:at + ROW]
            tail = plane[:, at + ROW - 128:at + ROW]
            if y < 0:
                whole, tail = move(sy, whole), move(syz, tail)
            else:
                tail = move(sz, tail)
            places_y = [(oy, y + 1 - 2 * oy) for oy in range(2) if 0 <= y + 1 - 2 * oy <= 2]
            for ox, a in places_x:
                for oy, b in places_y:
                    q = slice((ox * 2 + oy) * n, (ox * 2 + oy + 1) * n)
                    k = (a * 3 + b) * KB
                    cols[q, k:k + ROW] = whole
                    cols[q, k + ROW:k + KB] = tail
    for oz in range(2):
        v = jnp.dot(cols[...], band[:, oz * NB:(oz + 1) * NB], preferred_element_type=f32)[:, :C_OUT]
        s = 1.0 / (1.0 + jnp.exp(-v))
        act[oz] = (v * s).astype(bf16)
        slope = s * (1.0 + v * (1.0 - s))
        slopes[:, oz * NB:oz * NB + C_OUT] = (cot[oz].astype(f32) * slope).astype(bf16)
    for ab in range(9):
        g = lax.dot_general(cols[:, ab * KB:(ab + 1) * KB], slopes[...], (((0,), (0,)), ((), ())),
                            preferred_element_type=f32)
        for e in range(3):
            (r0, c0), (r1, c1) = spots[e]
            tap = g[r0:r0 + C_IN, c0:c0 + C_OUT] + g[r1:r1 + C_IN, c1:c1 + C_OUT]
            for d, r, take, off in row_parts((ab * 3 + e) * C_IN, C_IN, shard):
                left = max(0, min(take, cut - r))
                for start, length, base, lane in ((off, left, r, 0), (off + left, take - left, r + left - cut, C_OUT)):
                    if length:
                        for j, rr, tk, o2 in row_parts(base, length, piece):
                            terms[j, d, rr:rr + tk, lane:lane + C_OUT] = tap[start + o2:start + o2 + tk]


def layer(filled, rim, wt, cot, nb, nd, shard, cut, piece):
    rows = cot.shape[1]
    return pl.pallas_call(
        functools.partial(layer_kernel, nd, shard, cut, piece),
        out_shape=(
            jax.ShapeDtypeStruct(cot.shape, jnp.bfloat16),
            jax.ShapeDtypeStruct((nb, nd, piece, 2 * C_OUT), jnp.float32),
        ),
        scratch_shapes=[
            pltpu.VMEM((rows, 9 * KB), jnp.bfloat16),
            pltpu.VMEM((9 * KB, 2 * NB), jnp.bfloat16),
            pltpu.VMEM((rows, 2 * NB), jnp.bfloat16),
        ],
        compiler_params=pltpu.CompilerParams(vmem_limit_bytes=VMEM_LIMIT),
        name="layer",
    )(filled, rim, wt, cot)


def sum_kernel(nb, nd, shard, cut, piece, terms, out, got, pass_on, plane_in, down, down_in, final,
               s1, r1, s2, r2, s3, r3, s4, r4):
    f32, bf16 = jnp.float32, jnp.bfloat16
    nc = nb // 2
    me = lax.axis_index("brick")
    dp = lax.axis_index("dp")
    core = lax.rem(me, 2)
    chip = me // 2
    sib = me + 1 - 2 * core
    barrier = pltpu.get_barrier_semaphore()
    for k in range(1, nb):
        pl.semaphore_signal(barrier, inc=1, device_id={"brick": lax.rem(me + k, nb)}, device_id_type=MESH)
    for k in range(1, nd):
        pl.semaphore_signal(barrier, inc=1, device_id={"dp": lax.rem(dp + k, nd)}, device_id_type=MESH)
    pl.semaphore_wait(barrier, nb + nd - 2)
    sent = []
    for k in range(1, nc + 1):
        q = lax.rem(chip + k, nc)
        c = copy_to(terms.at[(1 - core) * nc + q], got.at[q], s1.at[k], r1.at[k], "brick", sib)
        c.start()
        sent.append(c)
    for k in range(1, nc):
        q = lax.rem(chip + k, nc)
        copy_to(terms.at[q], got.at[q], s1.at[k], r1.at[k], "brick", sib).wait_recv()
        pass_on[k] = (terms[core * nc + q] + got[q]).astype(bf16)
        c = copy_to(pass_on.at[k], plane_in.at[k], s2.at[k], r2.at[k], "brick", q * 2 + core)
        c.start()
        sent.append(c)
    copy_to(terms.at[chip], got.at[chip], s1.at[nc], r1.at[nc], "brick", sib).wait_recv()
    for k in range(1, nc):
        q = lax.rem(chip + nc - k, nc)
        copy_to(pass_on.at[k], plane_in.at[k], s2.at[k], r2.at[k], "brick", q * 2 + core).wait_recv()

    def plane_sum(d):
        total = terms[core * nc + chip, d] + got[chip, d]
        for k in range(1, nc):
            total = total + plane_in[k, d].astype(f32)
        return total

    for k in range(1, nd):
        o = lax.rem(dp + k, nd)
        down[k] = plane_sum(o).astype(bf16)
        c = copy_to(down.at[k], down_in.at[k], s3.at[k], r3.at[k], "dp", o)
        c.start()
        sent.append(c)
    total = plane_sum(dp)
    for k in range(1, nd):
        s = lax.rem(dp + nd - k, nd)
        copy_to(down.at[k], down_in.at[k], s3.at[k], r3.at[k], "dp", s).wait_recv()
        total = total + down_in[k].astype(f32)
    final[core * nc + chip] = total
    for k in range(1, nb):
        o = lax.rem(me + k, nb)
        slot = final.at[core * nc + chip]
        c = copy_to(slot, slot, s4.at[k], r4.at[k], "brick", o)
        c.start()
        sent.append(c)
    for k in range(1, nb):
        s = lax.rem(me + nb - k, nb)
        slot = final.at[lax.rem(s, 2) * nc + s // 2]
        copy_to(slot, slot, s4.at[k], r4.at[k], "brick", s).wait_recv()
    for j in range(nb):
        for rows, first, lane in ((cut, 0, 0), (shard - cut, cut, C_OUT)):
            take = min(piece, rows - j * piece)
            if take > 0:
                out[first + j * piece:first + j * piece + take, :] = (
                    final[j, :take, lane:lane + C_OUT])
    for c in sent:
        c.wait_send()


def sum_terms(terms, nb, nd, shard, cut, piece):
    bf16 = jnp.bfloat16
    dma = pltpu.SemaphoreType.DMA
    nc = nb // 2
    wide = 2 * C_OUT
    return pl.pallas_call(
        functools.partial(sum_kernel, nb, nd, shard, cut, piece),
        out_shape=jax.ShapeDtypeStruct((shard, C_OUT), jnp.float32),
        scratch_shapes=[
            pltpu.VMEM((nc, nd, piece, wide), jnp.float32),
            pltpu.VMEM((nc, nd, piece, wide), bf16),
            pltpu.VMEM((nc, nd, piece, wide), bf16),
            pltpu.VMEM((nd, piece, wide), bf16),
            pltpu.VMEM((nd, piece, wide), bf16),
            pltpu.VMEM((nb, piece, wide), jnp.float32),
            dma((nc + 1,)), dma((nc + 1,)), dma((nc,)), dma((nc,)),
            dma((nd,)), dma((nd,)), dma((nb,)), dma((nb,)),
        ],
        compiler_params=pltpu.CompilerParams(
            collective_id=1, has_side_effects=True, vmem_limit_bytes=VMEM_LIMIT),
        name="sum_terms",
    )(terms)


def staged(nb, nd, records, positions, weight, cotangent):
    cap = records.shape[2]
    shard = weight.shape[0]
    cut = up(-(-shard // 2), 8)
    piece = up(-(-cut // nb), 16)
    half = up(-(-shard // 2), 16)
    pos = jnp.pad(positions.reshape(nb, 1, cap), ((0, 0), (0, 7), (0, 128 - cap)))
    wt = jnp.pad(weight, ((0, 2 * half - shard), (0, 0)))
    arrived, places, full = exchange(records.reshape(records.shape[1:]), pos, wt, nb, nd)
    slots = nb * cap
    filled, edge = place(arrived.reshape(slots, -1), places[:, 0, :cap].reshape(1, slots))
    rim = lax.ppermute(edge, "brick", [(i, i + 1) for i in range(nb - 1)])
    shape7 = (BX, 2, BY, 2, BZ, 2, C_OUT)
    cot = cotangent.reshape(shape7).transpose(5, 1, 3, 0, 2, 4, 6).reshape(2, -1, C_OUT)
    act, terms = layer(filled, rim, full, cot, nb, nd, shard, cut, piece)
    act = act.reshape(2, 2, 2, BX, BY, BZ, C_OUT).transpose(3, 1, 4, 2, 5, 0, 6)
    return act.reshape(cotangent.shape), sum_terms(terms, nb, nd, shard, cut, piece)


def fused_kernel(nb, nd, cap, shard, main, piece, rec, pos_in, wt_in, cot_in, act_hbm, grad_out,
                 act_out, pos, wt, cot, linear, stage, spread, arrived, wts, tails, turned_wts, filled, rim, cols, band, slopes, cots, acts,
                 terms, got, pass_on, plane_in, down, down_in, own, final,
                 rs, rr, ps, pr, ws, wr, ts, tr, xs, xr, loc, bs, br, s1, r1, s2, r2, s3, r3, s4, r4, s5, r5):
    f32, bf16 = jnp.float32, jnp.bfloat16
    n = BX * BY * BZ
    nc = nb // 2
    me = lax.axis_index("brick")
    dp = lax.axis_index("dp")
    core = lax.rem(me, 2)
    chip = me // 2
    sib = me + 1 - 2 * core
    barrier = pltpu.get_barrier_semaphore()
    for k in range(1, nb):
        pl.semaphore_signal(barrier, inc=1, device_id={"brick": lax.rem(me + k, nb)}, device_id_type=MESH)
    for k in range(1, nd):
        pl.semaphore_signal(barrier, inc=1, device_id={"dp": lax.rem(dp + k, nd)}, device_id_type=MESH)
    local = [
        pltpu.make_async_copy(rec.at[me], arrived.at[me], loc.at[0]),
        pltpu.make_async_copy(wt_in, wts.at[dp], loc.at[1]),
        pltpu.make_async_copy(cot_in, cot, loc.at[2]),
        pltpu.make_async_copy(wt_in, wt, loc.at[3]),
        pltpu.make_async_copy(pos_in, pos, loc.at[4]),
    ]
    for c in reversed(local):
        c.start()
    pl.semaphore_wait(barrier, nb + nd - 2)
    half = wt.shape[0] // 2
    body_lanes = shard - shard % 128
    mine = (pl.ds(pl.multiple_of(core * half, 16), half), pl.ds(0, body_lanes))
    theirs = (pl.ds(pl.multiple_of((1 - core) * half, 16), half), pl.ds(0, body_lanes))
    tail_rows = shard - body_lanes
    sent = []

    def go(c):
        c.start()
        sent.append(c)

    for k in range(1, nd):
        o = lax.rem(dp + k, nd)
        go(copy_to(wt_in.at[mine], wts.at[(dp,) + mine], ws.at[k], wr.at[k], "dp", o))
    order = (3, 1, 0, 2)

    def plane_of(x):
        return pl.ds(x * PLANE, PLANE)

    def send_plane(x):
        for k in range(1, nb):
            o = lax.rem(me + k, nb)
            go(copy_to(rec.at[o, :, plane_of(x)], arrived.at[me, :, plane_of(x)],
                       rs.at[x, k], rr.at[x, k], "brick", o))

    send_plane(order[0])
    local[4].wait()
    lane = lax.broadcasted_iota(jnp.int32, (cap, nb * cap), 1)
    slot = lax.broadcasted_iota(jnp.int32, (cap, nb * cap), 0)
    to_lanes = jnp.where(lane == slot + me * cap, 1.0, 0.0).astype(bf16)
    lined = jnp.dot(pos[...].astype(f32).astype(bf16), to_lanes, preferred_element_type=f32)
    for o in range(nb):
        stage[o] = jnp.broadcast_to(lined[o:o + 1], stage.shape[1:])
    for k in range(1, nb):
        o = lax.rem(me + k, nb)
        go(copy_to(stage.at[o], spread.at[me], ps.at[k], pr.at[k], "brick", o))
    for x in order[1:]:
        send_plane(x)
    local[3].wait()
    if tail_rows:
        tails[dp, :tail_rows, :] = wt[:, body_lanes:].astype(f32).T
        for k in range(1, nd):
            go(copy_to(tails.at[dp], tails.at[dp], ts.at[k], tr.at[k], "dp", lax.rem(dp + k, nd)))
    band[...] = jnp.zeros_like(band)
    slopes[...] = jnp.zeros_like(slopes)
    terms[...] = jnp.zeros_like(terms)
    rows = 4 * n
    strip = 4 * BX * BY
    pair = 2 * C_OUT

    def home(r):
        bz, i, j = r // strip, lax.rem(r // (2 * BY), 2 * BX), lax.rem(r, 2 * BY)
        q = lax.rem(i, 2) * 2 + lax.rem(j, 2)
        return q * n + (i // 2) * (BY * BZ) + (j // 2) * BZ + bz

    r_id = lax.broadcasted_iota(jnp.int32, (rows, rows), 0)
    c_id = lax.broadcasted_iota(jnp.int32, (rows, rows), 1)
    turn = jnp.where(r_id == home(c_id), 1.0, 0.0).astype(bf16)
    local[2].wait()
    lined_cot = jnp.concatenate(
        [cot[:, :, z * pair:(z + 1) * pair].reshape(strip, pair) for z in range(BZ)], axis=0)
    turned = jnp.dot(turn, lined_cot, preferred_element_type=f32)
    cots[0] = turned[:, :C_OUT]
    cots[1] = turned[:, C_OUT:]
    sy = shift_matrix(n, 1, 0)
    sz = shift_matrix(n, 0, 1)
    syz = shift_matrix(n, 1, 1)
    for k in range(1, nb):
        s = lax.rem(me + nb - k, nb)
        copy_to(stage.at[s], spread.at[s], ps.at[k], pr.at[k], "brick", s).wait_recv()
    spread[me] = stage[me]
    local[0].wait()
    held = spread[0]
    for s in range(1, nb):
        held = held + spread[s]
    want = lax.broadcasted_iota(jnp.int32, (n, nb * cap), 0).astype(f32)
    pick = jnp.where(held[0:1] == want, 1.0, 0.0).astype(bf16)

    def place_plane(x):
        lanes = slice(x * PLANE, (x + 1) * PLANE)
        for k in range(1, nb):
            s = lax.rem(me + nb - k, nb)
            copy_to(rec.at[s, :, plane_of(x)], arrived.at[s, :, plane_of(x)],
                    rs.at[x, k], rr.at[x, k], "brick", s).wait_recv()
        records = arrived[:, :, lanes].reshape(nb * cap, PLANE)
        filled[:, lanes] = jnp.dot(pick, records, preferred_element_type=f32).astype(bf16)

    last = slice((BS - 1) * PLANE, BS * PLANE)
    edge = copy_to(filled.at[n - n // BX:n, last], rim, bs, br, "brick", lax.rem(me + 1, nb))

    def move(s, v):
        return jnp.dot(s, v, preferred_element_type=f32).astype(bf16)

    def fill_columns(x, plane):
        for y in range(-1, BS):
            at = (y if y >= 0 else BS - 1) * ROW
            whole = plane[:, at:at + ROW]
            tail = plane[:, at + ROW - 128:at + ROW]
            if y < 0:
                whole, tail = move(sy, whole), move(syz, tail)
            else:
                tail = move(sz, tail)
            for ox in range(2):
                a = x + 1 - 2 * ox
                for oy in range(2):
                    b = y + 1 - 2 * oy
                    if 0 <= a <= 2 and 0 <= b <= 2:
                        q = slice((ox * 2 + oy) * n, (ox * 2 + oy + 1) * n)
                        k = (a * 3 + b) * KB
                        cols[q, k:k + ROW] = whole
                        cols[q, k + ROW:k + KB] = tail

    def forward(ox, a, first=False):
        q = slice(ox * 2 * n, (ox + 1) * 2 * n)
        k = slice(a * 3 * KB, (a + 1) * 3 * KB)
        part = jnp.dot(cols[q, k], band[k, :], preferred_element_type=f32)
        linear[q, :] = part if first else linear[q, :] + part

    def activate(ox):
        q = slice(ox * 2 * n, (ox + 1) * 2 * n)
        for oz in range(2):
            v = linear[q, oz * NB:oz * NB + C_OUT]
            s = 1.0 / (1.0 + jnp.exp(-v))
            acts[q, oz * C_OUT:(oz + 1) * C_OUT] = v * s
            slope = s * (1.0 + v * (1.0 - s))
            slopes[q, oz * NB:oz * NB + C_OUT] = (cots[oz, q, :] * slope).astype(bf16)

    def take_plane(x):
        place_plane(x)
        if x == BS - 1:
            pl.when(me < nb - 1)(edge.start)
        fill_columns(x, filled[:, x * PLANE:(x + 1) * PLANE])

    def turn_weights(d):
        turned_wts[d, :body_lanes, :] = wts[d, :, :body_lanes].astype(f32).T.astype(bf16)
        if tail_rows:
            turned_wts[d, body_lanes:, :] = tails[d, :tail_rows, :].astype(bf16)

    take_plane(3)
    for k in range(1, nd):
        s = lax.rem(dp + nd - k, nd)
        copy_to(wt.at[mine], wts.at[(s,) + mine], ws.at[k], wr.at[k], "dp", s).wait_recv()
        go(copy_to(wts.at[(s,) + mine], wts.at[(s,) + mine], xs.at[k], xr.at[k], "brick", sib))
    local[1].wait()
    turn_weights(dp)
    for k in range(1, nd):
        s = lax.rem(dp + nd - k, nd)
        copy_to(wt.at[theirs], wts.at[(s,) + theirs], xs.at[k], xr.at[k], "brick", sib).wait_recv()
        if tail_rows:
            copy_to(tails.at[s], tails.at[s], ts.at[k], tr.at[k], "dp", s).wait_recv()
        turn_weights(s)
    spots = {0: ((KB - C_IN, 0), (C_IN, NB)), 1: ((0, 0), (2 * C_IN, NB)), 2: ((C_IN, 0), (3 * C_IN, NB))}
    for d in range(nd):
        w = turned_wts[d]
        for t in range(TAPS):
            ab, e = divmod(t, 3)
            for d2, r, take, off in row_parts(t * C_IN, C_IN, shard):
                if d2 == d:
                    for row, col in spots[e]:
                        at = ab * KB + row + off
                        band[at:at + take, col:col + C_OUT] = w[r:r + take]
    take_plane(1)
    forward(1, 2, True)
    forward(0, 2, True)
    forward(1, 0)
    take_plane(0)
    forward(0, 1)

    @pl.when(me > 0)
    def _():
        edge.wait_recv()

    @pl.when(me == 0)
    def _():
        rim[...] = jnp.zeros_like(rim)

    fill_columns(-1, jnp.concatenate([rim[...], filled[:n - n // BX, last]], axis=0))
    forward(0, 0)
    activate(0)
    def put(d, r, rows):
        count = rows.shape[0]
        head = max(0, min(count, main - r))
        spans = [(0, head, r, 0, 0, C_OUT)] if head else []
        if head < count:
            for m in range(C_OUT // SIDE):
                spans.append((head, count, r + head - main + m * (shard - main), C_OUT, m * SIDE, SIDE))
        for lo, hi, base, at, col, width in spans:
            for j, row, tk, off in row_parts(base, hi - lo, piece):
                part = rows[lo + off:lo + off + tk, col:col + width]
                terms[d, j, row:row + tk, at:at + width] = part

    def tap_rows(ab):
        g = lax.dot_general(cols[:, ab * KB:(ab + 1) * KB], slopes[...], (((0,), (0,)), ((), ())),
                            preferred_element_type=f32)
        for e in range(3):
            (r0, c0), (r1, c1) = spots[e]
            tap = g[r0:r0 + C_IN, c0:c0 + C_OUT] + g[r1:r1 + C_IN, c1:c1 + C_OUT]
            for d, r, take, off in row_parts((ab * 3 + e) * C_IN, C_IN, shard):
                put(d, r, tap[off:off + take])

    take_plane(2)
    forward(1, 1)
    activate(1)

    def to_sibling(d):
        return copy_to(terms.at[d, pl.ds((1 - core) * nc, nc)], got.at[d], s1.at[d], r1.at[d], "brick", sib)

    def to_chips(d):
        to_sibling(d).wait_recv()
        for k in range(1, nc):
            q = lax.rem(chip + k, nc)
            pass_on[d, k] = (terms[d, core * nc + q] + got[d, q]).astype(bf16)
            go(copy_to(pass_on.at[d, k], plane_in.at[d, k], s2.at[d, k], r2.at[d, k], "brick", q * 2 + core))

    half_rows = [pl.ds(h * (piece // 2), piece // 2) for h in range(2)]

    def to_dp(d, h, peer):
        return copy_to(down.at[d, half_rows[h]], down_in.at[dp, half_rows[h]], s3.at[d, h], r3.at[dp, h], "dp", peer)

    def from_dp(k, h):
        s = lax.rem(dp + nd - k, nd)
        copy_to(down.at[s, half_rows[h]], down_in.at[s, half_rows[h]], s3.at[s, h], r3.at[s, h], "dp", s).wait_recv()
        return down_in[s, half_rows[h], :].astype(f32)

    def to_rank(d):
        total = terms[d, core * nc + chip] + got[d, chip]
        for k in range(1, nc):
            q = lax.rem(chip + nc - k, nc)
            copy_to(pass_on.at[d, k], plane_in.at[d, k], s2.at[d, k], r2.at[d, k], "brick", q * 2 + core).wait_recv()
            total = total + plane_in[d, k].astype(f32)

        @pl.when(dp == d)
        def _():
            own[...] = total

        @pl.when(dp != d)
        def _():
            down[d] = total.astype(bf16)
            for h in range(2):
                to_dp(d, h, d).start()

    ready = 0
    for ab in range(9):
        tap_rows(ab)
        while ready < nd and (ready + 1) * shard <= (ab + 1) * 3 * C_IN:
            go(to_sibling(ready))
            if ready:
                to_chips(ready - 1)
            ready += 1
    to_chips(nd - 1)
    shown = lax.dot_general(turn, acts[...].astype(bf16), (((0,), (0,)), ((), ())), preferred_element_type=f32)
    for z in range(BZ):
        act_out[:, :, z * pair:(z + 1) * pair] = (
            shown[z * strip:(z + 1) * strip].reshape(2 * BX, 2 * BY, pair))
    stored = pltpu.make_async_copy(act_out, act_hbm, loc.at[5])
    stored.start()
    for d in range(nd):
        to_rank(d)
    here = core * nc + chip
    for h in range(2):
        part = half_rows[h]
        total = own[part, :]
        for k in range(1, nd):
            total = total + from_dp(k, h)
        final[here, part, :] = total
        slot = final.at[here, part]
        for k in range(1, nc):
            q = lax.rem(chip + k, nc)
            go(copy_to(slot, slot, s4.at[h, k], r4.at[h, k], "brick", q * 2 + core))
        go(copy_to(slot, slot, s5.at[h, 0], r5.at[h, 0], "brick", sib))
    for h in range(2):
        for k in range(1, nc):
            q = lax.rem(chip + nc - k, nc)
            there = final.at[core * nc + q, half_rows[h]]
            copy_to(there, there, s4.at[h, k], r4.at[h, k], "brick", q * 2 + core).wait_recv()
            go(copy_to(there, there, s5.at[h, k], r5.at[h, k], "brick", sib))
    for h in range(2):
        for k in range(nc):
            q = lax.rem(chip + nc - k, nc)
            there = final.at[(1 - core) * nc + q, half_rows[h]]
            copy_to(there, there, s5.at[h, k], r5.at[h, k], "brick", sib).wait_recv()
    for j in range(nb):
        grad_out[j * piece:(j + 1) * piece, :] = final[j, :, :C_OUT]
    for m in range(C_OUT // SIDE):
        for j, row, tk, off in row_parts(m * (shard - main), shard - main, piece):
            grad_out[main + off:main + off + tk, m * SIDE:(m + 1) * SIDE] = final[j, row:row + tk, C_OUT:]
    stored.wait()
    for c in sent:
        c.wait_send()
    pl.when(me < nb - 1)(edge.wait_send)
    for d in range(nd):
        @pl.when(dp != d)
        def _():
            for h in range(2):
                to_dp(d, h, d).wait_send()


def fused(nb, nd, records, positions, weight, cotangent):
    cap = records.shape[2]
    shard = weight.shape[0]
    main = up(-(-shard * C_OUT // (C_OUT + SIDE)), nb * 16)
    piece = main // nb
    f32, bf16 = jnp.float32, jnp.bfloat16
    n = BX * BY * BZ
    nc = nb // 2
    wide = C_OUT + SIDE
    dma = pltpu.SemaphoreType.DMA
    vmem = pltpu.VMEM
    act, grad = pl.pallas_call(
        functools.partial(fused_kernel, nb, nd, cap, shard, main, piece),
        out_shape=(
            jax.ShapeDtypeStruct(cotangent.shape[1:], f32),
            jax.ShapeDtypeStruct((shard, C_OUT), f32),
        ),
        in_specs=[pl.BlockSpec(memory_space=pl.ANY)] * 4,
        out_specs=(pl.BlockSpec(memory_space=pl.ANY), pl.BlockSpec(memory_space=pltpu.VMEM)),
        scratch_shapes=[
            vmem(cotangent.shape[1:], f32),
            vmem((nb, cap), jnp.int32),
            vmem((C_OUT, shard), bf16),
            vmem(cotangent.shape[1:], bf16),
            vmem((4 * n, 2 * NB), f32),
            vmem((nb, 8, nb * cap), f32),
            vmem((nb, 8, nb * cap), f32),
            vmem(records.shape[1:], bf16),
            vmem((nd, C_OUT, shard), bf16),
            vmem((nd, up(max(shard % 128, 1), 8), C_OUT), f32),
            vmem((nd, shard, C_OUT), bf16),
            vmem((n, BS * PLANE), bf16),
            vmem((n // BX, PLANE), bf16),
            vmem((4 * n, 9 * KB), bf16),
            vmem((9 * KB, 2 * NB), bf16),
            vmem((4 * n, 2 * NB), bf16),
            vmem((2, 4 * n, C_OUT), f32),
            vmem((4 * n, 2 * C_OUT), f32),
            vmem((nd, nb, piece, wide), f32),
            vmem((nd, nc, piece, wide), f32),
            vmem((nd, nc, piece, wide), bf16),
            vmem((nd, nc, piece, wide), bf16),
            vmem((nd, piece, wide), bf16),
            vmem((nd, piece, wide), bf16),
            vmem((piece, wide), f32),
            vmem((nb, piece, wide), f32),
            dma((BS, nb)), dma((BS, nb)), dma((nb,)), dma((nb,)),
            dma((nd,)), dma((nd,)), dma((nd,)), dma((nd,)), dma((nd,)), dma((nd,)), dma((6,)), dma, dma,
            dma((nd,)), dma((nd,)), dma((nd, nc)), dma((nd, nc)),
            dma((nd, 2)), dma((nd, 2)), dma((2, nc)), dma((2, nc)), dma((2, nc)), dma((2, nc)),
        ],
        compiler_params=pltpu.CompilerParams(
            collective_id=2, has_side_effects=True, vmem_limit_bytes=FUSED_LIMIT),
        name="fused",
    )(records.reshape(records.shape[1:]), positions.reshape(nb, cap), weight.T,
      cotangent.reshape(cotangent.shape[1:]))
    return act.astype(bf16).reshape(cotangent.shape), grad


def body(nb, nd, records, positions, weight, cotangent):
    path = staged if records.shape[2] % 16 else fused
    return path(nb, nd, records, positions, weight, cotangent)


def solution(mesh):
    placed = (
        P(("dp", "brick"), None, None, None),
        P(("dp", "brick"), None, None),
        P("dp", None),
        P("dp", "brick", None, None),
    )
    return jax.shard_map(
        functools.partial(body, mesh.shape["brick"], mesh.shape["dp"]),
        mesh=mesh,
        in_specs=placed,
        out_specs=(P("dp", "brick", None, None), P("dp", None)),
        check_vma=False,
    )
```
